512 devices in a mesh: sector: 128 (over z, x, y_lo), slab: 4 (over y_hi, core).
Axes of the slice: x: 4, y: 4 (y_hi: 2, y_lo: 2; y = y_hi * 2 + y_lo), z: 16, core: 2. Of those that a mesh axis runs over, the one named last changes fastest.
Arguments:
- state: float32 [5, 64, 1024, 128], P(None, 'slab', 'sector'), may hold values from -6 to 6
- mean_velocity: float32 [64, 1024, 128], P('slab', 'sector'), may hold values from 0.2 to 1.2
- sound_speed: float32 [64, 1024, 128], P('slab', 'sector'), may hold values from 0.5 to 2
- flux_axial: float32 [5, 5], replicated, may hold values from -2 to 2
- flux_radial: float32 [5, 5], replicated, may hold values from -2 to 2
- flux_azimuthal: float32 [5, 5], replicated, may hold values from -2 to 2
- axis_pair: int32 [128, 8], P('sector'), may hold values from 0 to 7, each once within a row
- panel_weight: float32 [4, 49152], P('slab', 'sector'), may hold values from 0.25 to 1.75
- panel_cell: int32 [4, 49152], P('slab', 'sector'), may hold values from 0 to 127
- panel_owner: int32 [4, 49152, 1], P('slab', 'sector'), may hold values from 0 to 127; in each aligned block of 384 rows (0 to 383, 384 to 767, ..., all dimensions but the last counted through in order) at most 4 rows name the same one
- panel_count: int32 [4, 128], P('slab', 'sector'), may hold values from 1 to 384, 16384 in all within a row
Outputs:
- sensitivity: float32 [5, 64, 1024, 128], P(None, 'slab', 'sector')
- harmonics: float32 [4, 128, 31, 128], P('slab', 'sector')
The draws below stay inside these ranges and needn't reach their ends.
Inputs may be any that keep to these rules, and one draw needn't show every extreme that they name: `panel_owner`: in each device's 384 slots no owner is named more than 4 times, and some device names one owner exactly 4 times. `panel_count`: live slots of the device; some device has all 384 live. `axis_pair`: each row is a permutation of the columns.
All inputs are finite; a program needn't handle non-finite values.
Results may differ from the reference program's by a relative error of at most 0.0003.
Values sent between devices are 32-bit elements; how exact they have to be, the bound alone decides.
A program may use at most 64 MiB of HBM per device.

```python
import math
import jax
import jax.numpy as jnp
import numpy as np
from jax import lax

PLANES = 16
COLS = 8
RADII = 128
PANELS = 384
ORDERS = 16
MODES = 31
CAP = 4
AXIAL = 64
AZIMUTH = 1024
N_SECTOR = 128
N_SLAB = 4


def set_ends(result, rng, least, top_value):
    longest = result.shape.index(max(result.shape))
    spots = []
    for shift in (0, 1):
        where = [jax.random.randint(jax.random.fold_in(rng, axis), (), 0, length) for axis, length in enumerate(result.shape)]
        where[longest] = (where[longest] + shift) % result.shape[longest]
        spots.append(tuple(where))
    return result.at[spots[0]].set(least).at[spots[1]].set(top_value)


def steps_of(stream_key, shape, cuts, least, largest):
    level, own = 1.0, jax.random.fold_in(stream_key, 6)
    for axis_at, parts in cuts:
        steps = jnp.exp(jax.random.uniform(jax.random.fold_in(own, axis_at), (parts,), jnp.float32, least / len(cuts), largest / len(cuts)))
        level = level * jnp.repeat(steps, shape[axis_at] // parts).reshape([-1 if axis == axis_at else 1 for axis in range(len(shape))])
    return level


def length_profile(number_of, total, reach, slope):
    portions = [(1 << 20) // math.isqrt(rank ** slope) + 1 for rank in range(2, number_of + 1)]
    surplus, counts = total - reach - (number_of - 1), [1] * (number_of - 1)
    while surplus > 0:
        candidates = [i for i in range(number_of - 1) if counts[i] < reach]
        pool, budget = sum([portions[i] for i in candidates]), surplus
        for i in candidates:
            addition = min(reach - counts[i], max(1, budget * portions[i] // pool), surplus)
            counts[i] = counts[i] + addition
            surplus = surplus - addition
    return np.array([reach] + counts)


def ragged_sizes(key, count, total, most, lean):
    if count == 2:
        one = jax.random.randint(key, (), max(1, total - most), min(most, total - 1) + 1)
        return jnp.stack([one, total - one])
    sizes = jnp.asarray(length_profile(count, total, most, lean), jnp.int32)
    twos = (count - 1) // 2
    source_of, sink = sizes[1:1 + 2 * twos:2], sizes[2:2 + 2 * twos:2]
    slack = jnp.minimum(source_of - 1, most - sink)
    passed = jax.random.randint(jax.random.fold_in(key, 1), (twos,), 0, 1 << 20) % (slack + 1)
    sizes = sizes.at[1:1 + 2 * twos:2].set(source_of - passed).at[2:2 + 2 * twos:2].set(sink + passed)
    return sizes[jax.random.permutation(jax.random.fold_in(key, 2), count)]


def assign_block(key, own, number, rows, number_of, top, limit, lean):
    ranking = jax.random.permutation(key, number_of)
    packed, ordinary = shares(number_of, rows * top, limit, lean, True), shares(number_of, rows * top, limit, lean, False)
    places = jnp.arange(number_of)

    def named(sizes, offset_by):
        used = int((sizes > 0).sum())
        fixed = max(1, used // 4)
        shifted = fixed + (places - fixed + offset_by * (used - fixed)) % max(1, number_of - fixed)
        return jnp.zeros((number_of,), jnp.int32).at[ranking[jnp.where(places < fixed, places, shifted)]].set(jnp.asarray(sizes, jnp.int32))

    sizes = jnp.where(number % 4 == 0, named(packed, number // 4), named(ordinary, number - number // 4 - 1))
    mixed = jax.random.permutation(jax.random.fold_in(own, 3), number_of)
    giver, taker = mixed[0:number_of // 2 * 2:2], mixed[1:number_of // 2 * 2:2]
    slack = jnp.minimum(sizes[giver] - 1, limit - sizes[taker]) // 2
    slack = jnp.where((giver == ranking[0]) | (taker == ranking[0]) | (sizes[taker] == 0), 0, jnp.maximum(slack, 0))
    shifted = jax.random.randint(jax.random.fold_in(own, 4), (number_of // 2,), 0, 1 << 20) % (slack + 1)
    sizes = sizes.at[giver].add(-shifted).at[taker].add(shifted)
    items = jnp.searchsorted(jnp.cumsum(sizes), jnp.arange(rows * top), side="right").astype(jnp.int32)
    listing = items.reshape(top, rows).T
    listing = listing[jax.random.permutation(jax.random.fold_in(own, 1), rows)]
    offset_by = jax.random.randint(jax.random.fold_in(own, 2), (rows, 1), 0, top)
    return jnp.take_along_axis(listing, (jnp.arange(top)[None, :] + offset_by) % top, axis=1)


def shares(count, total, limit, skew, full):
    loads = [(1 << 20) // math.isqrt(rank ** skew) + 1 for rank in range(1, count + 1)]
    largest = limit if full else min(limit, max(-(-total // count), total * loads[0] // sum(loads)))
    least = 1 if total - largest >= count - 1 else 0
    counts, spare = [largest] + [least] * (count - 1), total - largest - least * (count - 1)
    while spare > 0:
        movable = [i for i in range(1, count) if counts[i] < largest] or [i for i in range(1, count) if counts[i] < limit]
        mass, remaining = sum([loads[i] for i in movable]), spare
        for i in movable:
            extra = min(limit - counts[i], max(1, remaining * loads[i] // mass), spare)
            counts[i] = counts[i] + extra
            spare = spare - extra
    return np.array(counts)


def noise(own_key, shape, deviation, most, cuts=(), kind=jnp.bfloat16):
    entries = deviation * jax.random.normal(own_key, shape, jnp.float32)
    if cuts:
        entries = entries * steps_of(own_key, shape, cuts, -0.22, 0.18)
    return jnp.clip(entries, -most, most).astype(kind)


def setup_inputs(seed: int = 0) -> dict:
    keys = jax.random.split(jax.random.key(seed), 12)
    state = noise(keys[0], (5, AXIAL, AZIMUTH, RADII), 1.0, 6.0, ((1, 4), (2, 128)), jnp.float32)
    mean_velocity = jnp.clip(0.2 + 1 * jax.random.uniform(keys[1], (AXIAL, AZIMUTH, RADII), jnp.float32) ** steps_of(keys[1], (AXIAL, AZIMUTH, RADII), ((0, 4), (1, 128)), -0.2, 0.2), 0.2, 1.2)
    sound_speed = jnp.clip(jnp.exp(math.log(2.0) - 1.3862944 * jax.random.uniform(keys[2], (AXIAL, AZIMUTH, RADII), jnp.float32) ** steps_of(keys[2], (AXIAL, AZIMUTH, RADII), ((0, 4), (1, 128)), -0.2, 0.2)), 0.5, 2.0)
    flux_axial = noise(keys[3], (5, 5), 0.4, 2.0, (), jnp.float32)
    flux_radial = noise(keys[4], (5, 5), 0.4, 2.0, (), jnp.float32)
    flux_azimuthal = noise(keys[5], (5, 5), 0.4, 2.0, (), jnp.float32)
    axis_pair = jax.vmap(lambda own: jax.random.permutation(own, COLS))(jax.random.split(keys[6], N_SECTOR)).reshape((N_SECTOR, COLS)).astype(jnp.int32)
    panel_weight = jnp.clip(1.0 + 0.15 * jax.random.normal(keys[7], (N_SLAB, N_SECTOR * PANELS), jnp.float32), 0.25, 1.75)
    panel_cell = set_ends(jax.random.randint(keys[8], (N_SLAB, N_SECTOR * PANELS), 0, PLANES * COLS), jax.random.fold_in(keys[8], 1), 0, (PLANES * COLS) - 1).astype(jnp.int32)
    panel_owner_keys = jax.random.split(jax.random.fold_in(keys[9], 1), N_SLAB * (N_SECTOR * PANELS) // PANELS)
    panel_owner_turns = jax.random.permutation(jax.random.fold_in(keys[9], 3), N_SLAB * (N_SECTOR * PANELS) // PANELS)
    panel_owner = jax.vmap(lambda own, number: assign_block(jax.random.fold_in(keys[9], 2), own, number, PANELS, N_SECTOR, 1, CAP, 2))(panel_owner_keys, panel_owner_turns).reshape((N_SLAB, N_SECTOR * PANELS, 1))
    panel_count = jax.vmap(lambda own: ragged_sizes(own, N_SECTOR, N_SECTOR * PANELS // 3, PANELS, 2))(jax.random.split(keys[10], N_SLAB)).reshape((N_SLAB, N_SECTOR)).astype(jnp.int32)
    return dict(state=state, mean_velocity=mean_velocity, sound_speed=sound_speed, flux_axial=flux_axial, flux_radial=flux_radial, flux_azimuthal=flux_azimuthal, axis_pair=axis_pair, panel_weight=panel_weight, panel_cell=panel_cell, panel_owner=panel_owner, panel_count=panel_count)


PRECISE = lax.Precision.HIGHEST
PARITY_SIGNS = (1.0, 1.0, -1.0, -1.0, 1.0)
TIME_STEP = 0.25
VISCOSITY = 0.05


def neighbours(field, mirror):
    zero_plane = jnp.zeros_like(field[:, :1])
    x_minus = jnp.concatenate([zero_plane, field[:, :-1]], 1)
    x_plus = jnp.concatenate([field[:, 1:], zero_plane], 1)
    t_minus = jnp.roll(field, 1, 2)
    t_plus = jnp.roll(field, -1, 2)
    zero_cycle = jnp.zeros_like(field[..., :1])
    r_minus = jnp.concatenate([mirror[..., None], field[..., :-1]], 3)
    r_plus = jnp.concatenate([field[..., 1:], zero_cycle], 3)
    return x_minus, x_plus, t_minus, t_plus, r_minus, r_plus


def couple(matrix, field):
    return jnp.einsum('fg,g...->f...', matrix, field, precision=PRECISE)


def laplace(field, near):
    return near[0] + near[1] + near[2] + near[3] + near[4] + near[5] - 6.0 * field


def forward_rate(field, near, coefs, fluxes, inverse_radius):
    axial_diff = 0.5 * (near[1] - near[0])
    angle_diff = 0.5 * (near[3] - near[2])
    radial_diff = 0.5 * (near[5] - near[4])
    mixed = couple(fluxes[0], axial_diff) + couple(fluxes[1], radial_diff) + inverse_radius * couple(fluxes[2], angle_diff)
    return -coefs[0] * axial_diff - coefs[1] * mixed + VISCOSITY * laplace(field, near)


def adjoint_rate(field, near, coef_near, fluxes, inverse_radius):
    carried = 0.5 * (coef_near[1][0] * near[1] - coef_near[0][0] * near[0])
    axial_diff = 0.5 * (coef_near[1][1] * near[1] - coef_near[0][1] * near[0])
    angle_diff = 0.5 * (coef_near[3][1] * near[3] - coef_near[2][1] * near[2])
    radial_diff = 0.5 * (coef_near[5][1] * near[5] - coef_near[4][1] * near[4])
    mixed = couple(fluxes[0].T, axial_diff) + couple(fluxes[1].T, radial_diff) + inverse_radius * couple(fluxes[2].T, angle_diff)
    return carried + mixed + VISCOSITY * laplace(field, near)


def basis_rows(angle):
    orders = jnp.arange(ORDERS, dtype=jnp.float32)
    cosines = jnp.cos(angle[..., None] * orders)
    sines = jnp.sin(angle[..., None] * orders[1:])
    return jnp.concatenate([cosines, sines], -1)


def reference(state, mean_velocity, sound_speed, flux_axial, flux_radial, flux_azimuthal, axis_pair, panel_weight, panel_cell, panel_owner, panel_count):
    azimuth = COLS * N_SECTOR
    opposite = (jnp.arange(N_SECTOR, dtype=jnp.int32) + N_SECTOR // 2) % N_SECTOR
    partner = (opposite[:, None] * COLS + axis_pair.astype(jnp.int32)).reshape(-1)
    signs = jnp.array(PARITY_SIGNS, jnp.float32)
    coefs = jnp.stack([mean_velocity, sound_speed])
    coef_near = neighbours(coefs, coefs[..., 0][:, :, partner])
    inverse_radius = 1.0 / (jnp.arange(RADII, dtype=jnp.float32) + 0.5)
    fluxes = (flux_axial, flux_radial, flux_azimuthal)
    current = state
    for section in range(2):
        near = neighbours(current, current[..., 0][:, :, partner] * signs[:, None, None])
        current = current + TIME_STEP * forward_rate(current, near, coefs, fluxes, inverse_radius)
    forward = current
    encode_scale = PANELS ** -0.5
    band = forward[4].reshape(N_SLAB, PLANES, N_SECTOR, COLS, RADII).transpose(0, 2, 1, 3, 4)
    band = band.reshape(N_SLAB, N_SECTOR, PLANES * COLS, RADII)
    cells = panel_cell.reshape(N_SLAB, N_SECTOR, PANELS).astype(jnp.int32)
    owners = panel_owner.reshape(N_SLAB, N_SECTOR, PANELS).astype(jnp.int32)
    alive = (jnp.arange(PANELS, dtype=jnp.int32)[None, None, :] < panel_count[:, :, None]).astype(jnp.float32)
    factor = panel_weight.reshape(N_SLAB, N_SECTOR, PANELS) * alive
    lines = jnp.take_along_axis(band, cells[..., None], axis=2) * factor[..., None]
    column = jnp.arange(N_SECTOR, dtype=jnp.int32)[None, :, None] * COLS + cells % COLS
    angle = column.astype(jnp.float32) * (2.0 * math.pi / azimuth)
    phase = basis_rows(angle)

    def add_source(total, items):
        load, wave, owner = items
        pick = (owner[..., None] == jnp.arange(N_SECTOR, dtype=jnp.int32)).astype(jnp.float32)
        weighted = (pick[..., None] * wave[..., None, :]).reshape(N_SLAB, PANELS, N_SECTOR * MODES)
        return total + jnp.einsum('spq,spr->sqr', weighted, load, precision=PRECISE), None

    start_total = jnp.zeros((N_SLAB, N_SECTOR * MODES, RADII), jnp.float32)
    total, unused = lax.scan(add_source, start_total, (lines.transpose(1, 0, 2, 3), phase.transpose(1, 0, 2, 3), owners.transpose(1, 0, 2)))
    harmonics = (encode_scale * total).reshape(N_SLAB, N_SECTOR, MODES, RADII)
    flat_harm = harmonics.reshape(N_SLAB, N_SECTOR, MODES * RADII)

    def pull_back(items):
        wave, owner = items
        pick = (owner[..., None] == jnp.arange(N_SECTOR, dtype=jnp.int32)).astype(jnp.float32)
        chosen = jnp.einsum('spn,snq->spq', pick, flat_harm, precision=PRECISE).reshape(N_SLAB, PANELS, MODES, RADII)
        return encode_scale * jnp.einsum('spm,spmr->spr', wave, chosen, precision=PRECISE)

    gradient = lax.map(pull_back, (phase.transpose(1, 0, 2, 3), owners.transpose(1, 0, 2))).transpose(1, 0, 2, 3)
    weighted_grad = gradient * factor[..., None]

    def spread(items):
        cell_row, grad_row = items
        cell_pick = (cell_row[..., None] == jnp.arange(PLANES * COLS, dtype=jnp.int32)).astype(jnp.float32)
        return jnp.einsum('spc,spr->scr', cell_pick, grad_row, precision=PRECISE)

    impulse = lax.map(spread, (cells.transpose(1, 0, 2), weighted_grad.transpose(1, 0, 2, 3)))
    impulse = impulse.reshape(N_SECTOR, N_SLAB, PLANES, COLS, RADII).transpose(1, 2, 0, 3, 4).reshape(AXIAL, azimuth, RADII)
    current = forward.at[4].add(impulse)
    for section in range(2):
        near = neighbours(current, current[..., 0][:, :, partner] * signs[:, None, None])
        current = current + TIME_STEP * adjoint_rate(current, near, coef_near, fluxes, inverse_radius)
    return current, harmonics
```

```python
import functools
import math

import jax
import jax.numpy as jnp
from jax import lax
from jax.experimental import pallas as pl
from jax.experimental.pallas import tpu as pltpu
from jax.sharding import PartitionSpec as P

PLANES = 16
COLS = 8
RADII = 128
PANELS = 384
ORDERS = 16
MODES = 31
SECTORS = 128
SLABS = 4
GROUPS = 4
MEMBERS = SECTORS // GROUPS
CAP = 4
SLOTS = GROUPS * CAP
ROWS = MEMBERS * SLOTS
WAVES = 32
SCALE = PANELS**-0.5
TIME_STEP = 0.25
VISCOSITY = 0.05
KEEP = 1.0 - 6.0 * VISCOSITY * TIME_STEP
SPREAD = VISCOSITY * TIME_STEP
HALF = 0.5 * TIME_STEP
MESH = pl.DeviceIdType.MESH
F32, BF16, I32 = jnp.float32, jnp.bfloat16, jnp.int32


def split(x):
    high = x.astype(BF16)
    return high, (x - high.astype(F32)).astype(BF16)


def dot(a, b):
    return lax.dot_general(a, b, (((1,), (0,)), ((), ())), preferred_element_type=F32)


def dot_nt(a, b):
    return lax.dot_general(a, b, (((1,), (1,)), ((), ())), preferred_element_type=F32)


def iota(shape, dim):
    return lax.broadcasted_iota(I32, shape, dim)


def kernel(
    state,
    mean,
    sound,
    flux_a,
    flux_r,
    flux_t,
    pair,
    weight,
    cell,
    owner,
    count,
    out,
    harm,
    q0,
    q1,
    p0,
    p1,
    col_send,
    col_recv,
    mir_send,
    mir_recv,
    pick,
    pick_t,
    factor,
    wave_out,
    wave_in,
    enc,
    enc_t,
    lines_out,
    lines_in,
    part,
    part_in,
    whole,
    grad_out,
    grad_in,
    load_sem,
    halo_send,
    halo_recv,
    many_send,
    many_recv,
    few_send,
    few_recv,
):
    sector = lax.axis_index("sector")
    slab = lax.axis_index("slab")
    group = lax.div(sector, MEMBERS)
    member = lax.rem(sector, MEMBERS)
    right = lax.rem(sector + 1, SECTORS)
    left = lax.rem(sector + SECTORS - 1, SECTORS)
    behind = lax.rem(sector + SECTORS // 2, SECTORS)

    def mate(r):
        return group * MEMBERS + lax.rem(member + r, MEMBERS)

    def twin(k):
        return lax.rem(group + k, GROUPS) * MEMBERS + member

    loads = [
        pltpu.make_async_copy(state, q0.at[pl.ds(0, 5), pl.ds(1, PLANES)], load_sem.at[0]),
        pltpu.make_async_copy(mean, q0.at[5, pl.ds(1, PLANES)], load_sem.at[1]),
        pltpu.make_async_copy(sound, q0.at[6, pl.ds(1, PLANES)], load_sem.at[2]),
    ]
    for load in loads:
        load.start()

    barrier = pltpu.get_barrier_semaphore()

    def greet(to_sector, to_slab):
        pl.semaphore_signal(barrier, inc=1, device_id=(to_sector, to_slab), device_id_type=MESH)

    greet(right, slab)
    greet(left, slab)

    @pl.when(slab > 0)
    def _():
        greet(sector, slab - 1)

    @pl.when(slab < SLABS - 1)
    def _():
        greet(sector, slab + 1)

    for k in range(1, GROUPS):
        greet(twin(k), slab)

    def greet_mate(r, carry):
        greet(mate(r), slab)
        return carry

    lax.fori_loop(1, MEMBERS, greet_mate, 0)

    row = iota((128, 128), 0)
    lane = iota((128, 128), 1)
    owners = owner[...]
    cells = cell[...]
    weights = weight[...]
    live = count[0, 0]
    across, down = [], []
    for q in range(3):
        wide = jnp.broadcast_to(owners[:, q * 128 : (q + 1) * 128], (128, 128)).astype(F32)
        across.append(wide)
        down.append(wide.T)
    slot_pieces, cell_pieces, weight_pieces = [], [], []
    tall = iota((ROWS, 128), 0)
    for q in range(3):
        earlier = jnp.where((down[q] == across[q]) & (row < lane), 1.0, 0.0)
        for s in range(q):
            earlier = earlier + jnp.where(down[s] == across[q], 1.0, 0.0)
        rank = jnp.sum(earlier, axis=0, keepdims=True).astype(I32)
        at = slice(q * 128, (q + 1) * 128)
        name = owners[:, at]
        relative = (name + MEMBERS - member) % MEMBERS
        slot = relative * SLOTS + (name // MEMBERS) * CAP + rank
        place = iota((1, 128), 1) + q * 128
        slot = jnp.where(place < live, slot, -1)
        slot_pieces.append(jnp.where(tall == slot, 1.0, 0.0).astype(BF16))
        cell_pieces.append(jnp.where(row == cells[:, at], 1.0, 0.0).astype(BF16))
        weight_pieces.append(jnp.broadcast_to(weights[:, at], (128, 128)))
    slots = jnp.concatenate(slot_pieces, axis=1)
    spots = jnp.concatenate(cell_pieces, axis=1)
    heavy, light = split(jnp.concatenate(weight_pieces, axis=1))
    picked = dot_nt(slots, spots).astype(BF16)
    pick[...] = picked
    pick_t[...] = dot_nt(spots, slots).astype(BF16)
    factor[...] = dot_nt(slots, heavy) + dot_nt(slots, light)
    order = lane % WAVES
    turn = jnp.where(order < ORDERS, order, order - (ORDERS - 1))
    turn = turn * (sector * COLS + row % COLS) + jnp.where(order < ORDERS, 0, 768)
    turn = turn % 1024
    table = jnp.cos(turn.astype(F32) * (2.0 * math.pi / 1024.0)) * SCALE
    table = jnp.where(order < MODES, table, 0.0)
    table_high, table_low = split(table)
    waves = dot(picked, table_high) + dot(picked, table_low)
    tall_lane = iota((ROWS, 128), 1)
    waves = jnp.where((tall % SLOTS) // CAP == tall_lane // WAVES, waves, 0.0)
    waves = waves.reshape(MEMBERS, SLOTS, 128)
    waves = (waves[:, :8] + waves[:, 8:]).reshape(MEMBERS * 8, 128)
    waves = waves.reshape(MEMBERS, 8, 128)
    waves = waves + jnp.concatenate([waves[:, 4:], waves[:, :4]], axis=1)
    wave_out[...] = waves

    sub = iota((8, 128), 0)
    ray = iota((8, 128), 1)
    pairs = jnp.zeros((8, 128), I32)
    for c in range(COLS):
        pairs = jnp.where(sub == c, pair[0, c], pairs)
    parity = jnp.where((ray % 8 == 2) | (ray % 8 == 3), -1.0, 1.0)

    @pl.when(slab == 0)
    def _():
        for ref in (q0, q1, p0, p1):
            ref[:, 0] = jnp.zeros_like(ref[:, 0])

    @pl.when(slab == SLABS - 1)
    def _():
        for ref in (q0, q1, p0, p1):
            ref[:, PLANES + 1] = jnp.zeros_like(ref[:, PLANES + 1])

    def pack_columns(ref, level, fields):
        flat = ref.reshape(ref.shape[0] * (PLANES + 2) * COLS, RADII)
        for f in fields:
            for side, c in ((0, 0), (1, COLS - 1)):
                begin = (f * (PLANES + 2) + 1) * COLS + c
                col_send[level, side, f * PLANES : (f + 1) * PLANES] = flat[
                    pl.ds(begin, PLANES, stride=COLS), :
                ]

    def columns_of(ref, level, phase, first, number):
        rows = pl.ds(first * PLANES, number * PLANES)
        copies = []
        for side, to in ((0, left), (1, right)):
            copies.append(
                pltpu.make_async_remote_copy(
                    src_ref=col_send.at[level, side, rows],
                    dst_ref=col_recv.at[level, side, rows],
                    send_sem=halo_send.at[phase, side],
                    recv_sem=halo_recv.at[phase, side],
                    device_id=(to, slab),
                    device_id_type=MESH,
                )
            )
        return copies

    def planes_of(ref, phase, first, number):
        fields = pl.ds(first, number)
        up = pltpu.make_async_remote_copy(
            src_ref=ref.at[fields, PLANES],
            dst_ref=ref.at[fields, 0],
            send_sem=halo_send.at[phase, 2],
            recv_sem=halo_recv.at[phase, 2],
            device_id=(sector, lax.rem(slab + 1, SLABS)),
            device_id_type=MESH,
        )
        downward = pltpu.make_async_remote_copy(
            src_ref=ref.at[fields, 1],
            dst_ref=ref.at[fields, PLANES + 1],
            send_sem=halo_send.at[phase, 3],
            recv_sem=halo_recv.at[phase, 3],
            device_id=(sector, lax.rem(slab + SLABS - 1, SLABS)),
            device_id_type=MESH,
        )
        return up, downward

    def mirror_of(level, phase):
        return pltpu.make_async_remote_copy(
            src_ref=mir_send.at[level],
            dst_ref=mir_recv.at[level],
            send_sem=halo_send.at[phase, 4],
            recv_sem=halo_recv.at[phase, 4],
            device_id=(behind, slab),
            device_id_type=MESH,
        )

    def exchange(ref, level, phase, first, number, with_mirror, act):
        for copy in columns_of(ref, level, phase, first, number):
            act(copy, "both")
        up, downward = planes_of(ref, phase, first, number)

        @pl.when(slab < SLABS - 1)
        def _():
            act(up, "send")
            act(downward, "recv")

        @pl.when(slab > 0)
        def _():
            act(downward, "send")
            act(up, "recv")

        if with_mirror:
            act(mirror_of(level, phase), "both")

    def start(copy, part_of):
        if part_of != "recv":
            copy.start()

    def arrive(copy, part_of):
        if part_of != "send":
            copy.wait_recv()

    def leave(copy, part_of):
        if part_of != "recv":
            copy.wait_send()

    def pack_mirror(i, fields, total):
        here = jnp.zeros((8, 128), F32)
        for f, value in enumerate(fields):
            here = jnp.where(ray == f, value if f == 0 else pltpu.roll(value, f, 1), here)
        return jnp.where(ray // 8 == i, pltpu.roll(here, i * 8, 1), total)

    def facing(level):
        raw = mir_recv[level]
        total = jnp.zeros((8, 128), F32)
        for c in range(COLS):
            total = jnp.where(pairs == c, jnp.broadcast_to(raw[c : c + 1], (8, 128)), total)
        return total * parity

    def at_plane(mirror, i):
        return pltpu.roll(mirror, lax.rem(128 - i * 8, 128), 1)

    def beside(value, level, f, i, inner):
        before = jnp.broadcast_to(col_recv[level, 1, pl.ds(f * PLANES + i, 1), :], (8, 128))
        after = jnp.broadcast_to(col_recv[level, 0, pl.ds(f * PLANES + i, 1), :], (8, 128))
        t_minus = jnp.where(sub == 0, before, pltpu.roll(value, 1, 0))
        t_plus = jnp.where(sub == COLS - 1, after, pltpu.roll(value, COLS - 1, 0))
        core = inner if f == 0 else pltpu.roll(inner, 128 - f, 1)
        r_minus = jnp.where(ray == 0, core, pltpu.roll(value, 1, 1))
        r_plus = jnp.where(ray == RADII - 1, 0.0, pltpu.roll(value, RADII - 1, 1))
        return t_minus, t_plus, r_minus, r_plus

    inverse = 1.0 / (ray.astype(F32) + 0.5)

    def forward_plane(src, level, dst, mirror, i, total):
        u, c = q0[5, i + 1] * HALF, q0[6, i + 1] * HALF
        inner = at_plane(mirror, i)
        values, dx, dr, dt, around = [], [], [], [], []
        for f in range(5):
            value, x_minus, x_plus = src[f, i + 1], src[f, i], src[f, i + 2]
            t_minus, t_plus, r_minus, r_plus = beside(value, level, f, i, inner)
            values.append(value)
            dx.append(x_plus - x_minus)
            dr.append(r_plus - r_minus)
            dt.append((t_plus - t_minus) * inverse)
            around.append((x_plus + x_minus) + (t_plus + t_minus) + (r_plus + r_minus))
        results = []
        for f in range(5):
            mixed = flux_a[f, 0] * dx[0] + flux_r[f, 0] * dr[0] + flux_t[f, 0] * dt[0]
            for g in range(1, 5):
                mixed = mixed + flux_a[f, g] * dx[g] + flux_r[f, g] * dr[g] + flux_t[f, g] * dt[g]
            result = values[f] * KEEP + around[f] * SPREAD - u * dx[f] - c * mixed
            dst[f, i + 1] = result
            results.append(result)
        return pack_mirror(i, results, total)

    def adjoint_plane(src, level, store, mirror, coef_mirror, i, total):
        u_minus, u_plus = q0[5, i] * HALF, q0[5, i + 2] * HALF
        c = q0[6, i + 1] * HALF
        c_minus, c_plus = q0[6, i] * HALF, q0[6, i + 2] * HALF
        before = jnp.broadcast_to(col_recv[0, 1, pl.ds(6 * PLANES + i, 1), :], (8, 128)) * HALF
        after = jnp.broadcast_to(col_recv[0, 0, pl.ds(6 * PLANES + i, 1), :], (8, 128)) * HALF
        core = pltpu.roll(at_plane(coef_mirror, i), 128 - 6, 1) * HALF
        c_t_minus = jnp.where(sub == 0, before, pltpu.roll(c, 1, 0)) * inverse
        c_t_plus = jnp.where(sub == COLS - 1, after, pltpu.roll(c, COLS - 1, 0)) * inverse
        c_r_minus = jnp.where(ray == 0, core, pltpu.roll(c, 1, 1))
        c_r_plus = pltpu.roll(c, RADII - 1, 1)
        inner = at_plane(mirror, i)
        carried, dx, dr, dt = [], [], [], []
        for f in range(5):
            value, x_minus, x_plus = src[f, i + 1], src[f, i], src[f, i + 2]
            t_minus, t_plus, r_minus, r_plus = beside(value, level, f, i, inner)
            dx.append(c_plus * x_plus - c_minus * x_minus)
            dr.append(c_r_plus * r_plus - c_r_minus * r_minus)
            dt.append(c_t_plus * t_plus - c_t_minus * t_minus)
            around = (x_plus + x_minus) + (t_plus + t_minus) + (r_plus + r_minus)
            carried.append(
                value * KEEP + around * SPREAD + (u_plus * x_plus - u_minus * x_minus)
            )
        results = []
        for f in range(5):
            result = carried[f]
            for g in range(5):
                result = result + flux_a[g, f] * dx[g] + flux_r[g, f] * dr[g] + flux_t[g, f] * dt[g]
            store(f, i, result)
            results.append(result)
        return results if total is None else pack_mirror(i, results, total)

    blank = jnp.zeros((8, 128), F32)

    for load in loads:
        load.wait()
    pack_columns(q0, 0, range(7))
    mir_send[0] = lax.fori_loop(
        0, PLANES, lambda i, total: pack_mirror(i, [q0[f, i + 1] for f in range(7)], total), blank
    )
    pl.semaphore_wait(
        barrier,
        MEMBERS - 1 + GROUPS - 1 + 2 + jnp.where(slab > 0, 1, 0) + jnp.where(slab < SLABS - 1, 1, 0),
    )
    exchange(q0, 0, 0, 0, 7, True, start)

    def to_mate(source, target, which):
        def copy_of(r):
            return pltpu.make_async_remote_copy(
                src_ref=source.at[r],
                dst_ref=target.at[r],
                send_sem=many_send.at[which],
                recv_sem=many_recv.at[which],
                device_id=(mate(r), slab),
                device_id_type=MESH,
            )

        return copy_of

    def back_mate(source, target, which):
        def copy_of(r):
            return pltpu.make_async_remote_copy(
                src_ref=source.at[r],
                dst_ref=target.at[r],
                send_sem=many_send.at[which],
                recv_sem=many_recv.at[which],
                device_id=(mate(MEMBERS - r), slab),
                device_id_type=MESH,
            )

        return copy_of

    def start_all(copy_of):
        def step(r, carry):
            copy_of(r).start()
            return carry

        lax.fori_loop(1, MEMBERS, step, 0)

    def all_of(source, target, which):
        rest = pl.ds(1, MEMBERS - 1)
        return pltpu.make_async_remote_copy(
            src_ref=source.at[rest],
            dst_ref=target.at[rest],
            send_sem=many_send.at[which],
            recv_sem=many_recv.at[which],
            device_id=(right, slab),
            device_id_type=MESH,
        )

    start_all(to_mate(wave_out, wave_in, 0))
    wave_in[0] = wave_out[0]
    exchange(q0, 0, 0, 0, 7, True, arrive)
    coef_mirror = facing(0)
    mir_send[1] = lax.fori_loop(
        0, PLANES, functools.partial(forward_plane, q0, 0, q1, coef_mirror), blank
    )
    pack_columns(q1, 1, range(5))
    exchange(q1, 1, 1, 0, 5, True, start)
    exchange(q1, 1, 1, 0, 5, True, arrive)
    mir_send[2] = lax.fori_loop(
        0, PLANES, functools.partial(forward_plane, q1, 1, p0, facing(1)), blank
    )

    pressure = p0[4, 1 : PLANES + 1].reshape(PLANES * COLS, RADII)
    high, low = split(pressure)
    lines = (dot(pick[...], high) + dot(pick[...], low)) * factor[...]
    lines_out[...] = lines.reshape(MEMBERS, SLOTS, RADII)
    start_all(to_mate(lines_out, lines_in, 1))
    lines_in[0] = lines_out[0]
    pack_columns(p0, 2, range(4))
    exchange(p0, 2, 2, 0, 4, False, start)
    all_of(wave_out, wave_in, 0).wait_recv()
    given = wave_in[...]
    sub3, ray3 = iota((MEMBERS, 8, 128), 1), iota((MEMBERS, 8, 128), 2)
    first = jnp.where(sub3 // CAP == ray3 // WAVES, given, 0.0)
    second = jnp.where(sub3 // CAP + 2 == ray3 // WAVES, given, 0.0)
    encoder = jnp.concatenate([first, second], axis=1).reshape(ROWS, 128)
    enc[0], enc[1] = split(encoder)
    enc_t[0], enc_t[1] = split(encoder.T)

    all_of(lines_out, lines_in, 1).wait_recv()
    high, low = split(lines_in[...].reshape(ROWS, RADII))
    part[...] = dot(enc_t[0], high) + (dot(enc_t[0], low) + dot(enc_t[1], high))

    def to_twin(k):
        return pltpu.make_async_remote_copy(
            src_ref=part.at[pl.ds(pl.multiple_of(lax.rem(group + k, GROUPS) * WAVES, WAVES), WAVES)],
            dst_ref=part_in.at[k - 1],
            send_sem=few_send.at[0, k - 1],
            recv_sem=few_recv.at[0, k - 1],
            device_id=(twin(k), slab),
            device_id_type=MESH,
        )

    own_rows = pl.ds(pl.multiple_of(group * WAVES, WAVES), WAVES)

    def from_owner(k):
        return pltpu.make_async_remote_copy(
            src_ref=whole.at[own_rows],
            dst_ref=whole.at[own_rows],
            send_sem=few_send.at[1, k - 1],
            recv_sem=few_recv.at[1, k - 1],
            device_id=(twin(k), slab),
            device_id_type=MESH,
        )

    for k in range(1, GROUPS):
        to_twin(k).start()
    mine = part[own_rows, :]
    for k in range(1, GROUPS):
        to_twin(k).wait_recv()
        mine = mine + part_in[k - 1]
    whole[own_rows, :] = mine
    for k in range(1, GROUPS):
        from_owner(k).start()
    harm[0, 0] = mine[:MODES]
    for k in range(1, GROUPS):
        from_owner(k).wait_recv()

    high, low = split(whole[...])
    grad = dot(enc[0], high) + (dot(enc[0], low) + dot(enc[1], high))
    grad_out[...] = grad.reshape(MEMBERS, SLOTS, RADII)
    start_all(back_mate(grad_out, grad_in, 2))
    grad_in[0] = grad_out[0]
    exchange(p0, 2, 2, 0, 4, False, arrive)
    all_of(grad_out, grad_in, 2).wait_recv()
    high, low = split(grad_in[...].reshape(ROWS, RADII) * factor[...])
    impulse = dot(pick_t[...], high) + dot(pick_t[...], low)
    impulse = impulse.reshape(PLANES, COLS, RADII)
    p0[4, 1 : PLANES + 1] = p0[4, 1 : PLANES + 1] + impulse

    mir_send[2] = lax.fori_loop(
        0, PLANES, lambda i, total: pack_mirror(i, [p0[f, i + 1] for f in range(5)], total), blank
    )
    pack_columns(p0, 2, (4,))
    exchange(p0, 2, 3, 4, 1, True, start)
    exchange(p0, 2, 3, 4, 1, True, arrive)

    def store_p1(f, i, value):
        p1[f, i + 1] = value

    def store_out(f, i, value):
        out[f, i] = value

    mirror = facing(2)
    mir_send[3] = lax.fori_loop(
        0,
        PLANES,
        lambda i, total: adjoint_plane(p0, 2, store_p1, mirror, coef_mirror, i, total),
        blank,
    )
    pack_columns(p1, 3, range(5))
    exchange(p1, 3, 4, 0, 5, True, start)
    exchange(p1, 3, 4, 0, 5, True, arrive)
    last_mirror = facing(3)

    def finish(i, carry):
        adjoint_plane(p1, 3, store_out, last_mirror, coef_mirror, i, None)
        return carry

    lax.fori_loop(0, PLANES, finish, 0)

    exchange(q0, 0, 0, 0, 7, True, leave)
    exchange(q1, 1, 1, 0, 5, True, leave)
    exchange(p0, 2, 2, 0, 4, False, leave)
    exchange(p0, 2, 3, 4, 1, True, leave)
    exchange(p1, 3, 4, 0, 5, True, leave)
    all_of(wave_out, wave_in, 0).wait_send()
    all_of(lines_out, lines_in, 1).wait_send()
    all_of(grad_out, grad_in, 2).wait_send()
    for k in range(1, GROUPS):
        to_twin(k).wait_send()
        from_owner(k).wait_send()


def local(
    state,
    mean_velocity,
    sound_speed,
    flux_axial,
    flux_radial,
    flux_azimuthal,
    axis_pair,
    panel_weight,
    panel_cell,
    panel_owner,
    panel_count,
):
    anywhere = pl.BlockSpec(memory_space=pl.ANY)
    scalar = pl.BlockSpec(memory_space=pltpu.SMEM)
    vector = pl.BlockSpec(memory_space=pltpu.VMEM)

    def grid_of(fields):
        return pltpu.VMEM((fields, PLANES + 2, COLS, RADII), F32)

    return pl.pallas_call(
        kernel,
        out_shape=(
            jax.ShapeDtypeStruct((5, PLANES, COLS, RADII), F32),
            jax.ShapeDtypeStruct((1, 1, MODES, RADII), F32),
        ),
        in_specs=[anywhere] * 3 + [scalar] * 4 + [vector] * 3 + [scalar],
        out_specs=(vector, vector),
        scratch_shapes=[
            grid_of(7),
            grid_of(5),
            grid_of(5),
            grid_of(5),
            pltpu.VMEM((4, 2, 7 * PLANES, RADII), F32),
            pltpu.VMEM((4, 2, 7 * PLANES, RADII), F32),
            pltpu.VMEM((4, 8, 128), F32),
            pltpu.VMEM((4, 8, 128), F32),
            pltpu.VMEM((ROWS, 128), BF16),
            pltpu.VMEM((128, ROWS), BF16),
            pltpu.VMEM((ROWS, 128), F32),
            pltpu.VMEM((MEMBERS, 8, 128), F32),
            pltpu.VMEM((MEMBERS, 8, 128), F32),
            pltpu.VMEM((2, ROWS, 128), BF16),
            pltpu.VMEM((2, 128, ROWS), BF16),
            pltpu.VMEM((MEMBERS, SLOTS, RADII), F32),
            pltpu.VMEM((MEMBERS, SLOTS, RADII), F32),
            pltpu.VMEM((GROUPS * WAVES, RADII), F32),
            pltpu.VMEM((GROUPS - 1, WAVES, RADII), F32),
            pltpu.VMEM((GROUPS * WAVES, RADII), F32),
            pltpu.VMEM((MEMBERS, SLOTS, RADII), F32),
            pltpu.VMEM((MEMBERS, SLOTS, RADII), F32),
            pltpu.SemaphoreType.DMA((3,)),
            pltpu.SemaphoreType.DMA((5, 5)),
            pltpu.SemaphoreType.DMA((5, 5)),
            pltpu.SemaphoreType.DMA((3,)),
            pltpu.SemaphoreType.DMA((3,)),
            pltpu.SemaphoreType.DMA((2, GROUPS - 1)),
            pltpu.SemaphoreType.DMA((2, GROUPS - 1)),
        ],
        compiler_params=pltpu.CompilerParams(
            collective_id=0, has_side_effects=True, vmem_limit_bytes=32 << 20
        ),
    )(
        state,
        mean_velocity,
        sound_speed,
        flux_axial,
        flux_radial,
        flux_azimuthal,
        axis_pair,
        panel_weight,
        panel_cell,
        panel_owner.reshape(1, PANELS),
        panel_count,
    )


def solution(mesh):
    return jax.shard_map(
        local,
        mesh=mesh,
        in_specs=(
            P(None, "slab", "sector", None),
            P("slab", "sector", None),
            P("slab", "sector", None),
            P(),
            P(),
            P(),
            P("sector", None),
            P("slab", "sector"),
            P("slab", "sector"),
            P("slab", "sector", None),
            P("slab", "sector"),
        ),
        out_specs=(P(None, "slab", "sector", None), P("slab", "sector", None, None)),
        check_vma=False,
    )
```

```python
import functools
import math

import jax
import jax.numpy as jnp
from jax import lax
from jax.experimental import pallas as pl
from jax.experimental.pallas import tpu as pltpu
from jax.sharding import PartitionSpec as P

PLANES = 16
COLS = 8
RADII = 128
PANELS = 384
ORDERS = 16
MODES = 31
SECTORS = 128
SLABS = 4
GROUPS = 8
MEMBERS = SECTORS // GROUPS
CAP = 4
SLOTS = GROUPS * CAP
ROWS = MEMBERS * SLOTS
WAVES = 32
LANES = GROUPS * WAVES
SCALE = PANELS**-0.5
TIME_STEP = 0.25
VISCOSITY = 0.05
KEEP = 1.0 - 6.0 * VISCOSITY * TIME_STEP
SPREAD = VISCOSITY * TIME_STEP
HALF = 0.5 * TIME_STEP
UNROLL = 4
VMEM_GRANT = 60 << 20
MESH = pl.DeviceIdType.MESH
F32, BF16, I32 = jnp.float32, jnp.bfloat16, jnp.int32


def split(x):
    high = x.astype(BF16)
    return high, (x - high.astype(F32)).astype(BF16)


def dot(a, b):
    return lax.dot_general(a, b, (((1,), (0,)), ((), ())), preferred_element_type=F32)


def dot_nt(a, b):
    return lax.dot_general(a, b, (((1,), (1,)), ((), ())), preferred_element_type=F32)


def iota(shape, dim):
    return lax.broadcasted_iota(I32, shape, dim)


def kernel(
    state,
    mean,
    sound,
    flux_a,
    flux_r,
    flux_t,
    pair,
    weight_in,
    cell_in,
    owner_in,
    count,
    out,
    harm,
    q0,
    q1,
    p0,
    p1,
    weight,
    cell,
    owner,
    col_send,
    col_recv,
    mir_send,
    mir_recv,
    rows0,
    turned,
    pick,
    pick_t,
    factor,
    wave_out,
    wave_in,
    enc,
    enc_t,
    lines_out,
    lines_in,
    part,
    part_in,
    whole,
    grad_out,
    grad_in,
    load_sem,
    halo_send,
    halo_recv,
    mirror_sems,
    many_send,
    many_recv,
    few_send,
    few_recv,
):
    sector = lax.axis_index("sector")
    slab = lax.axis_index("slab")
    group = lax.div(sector, MEMBERS)
    member = lax.rem(sector, MEMBERS)
    right = lax.rem(sector + 1, SECTORS)
    left = lax.rem(sector + SECTORS - 1, SECTORS)
    behind = lax.rem(sector + SECTORS // 2, SECTORS)

    def mate(r):
        return group * MEMBERS + lax.rem(member + r, MEMBERS)

    def twin(k):
        return lax.rem(group + k, GROUPS) * MEMBERS + member

    loads = [
        pltpu.make_async_copy(state, q0.at[pl.ds(0, 5), pl.ds(1, PLANES)], load_sem.at[0]),
        pltpu.make_async_copy(mean, q0.at[5, pl.ds(1, PLANES)], load_sem.at[1]),
        pltpu.make_async_copy(sound, q0.at[6, pl.ds(1, PLANES)], load_sem.at[2]),
    ]
    lists = [
        pltpu.make_async_copy(weight_in, weight, load_sem.at[3]),
        pltpu.make_async_copy(cell_in, cell, load_sem.at[4]),
        pltpu.make_async_copy(owner_in, owner, load_sem.at[5]),
    ]
    for load in lists + loads:
        load.start()

    sent = []

    barrier = pltpu.get_barrier_semaphore()

    def greet(to_sector, to_slab):
        pl.semaphore_signal(barrier, inc=1, device_id=(to_sector, to_slab), device_id_type=MESH)

    greet(right, slab)
    greet(left, slab)

    @pl.when(slab > 0)
    def _():
        greet(sector, slab - 1)

    @pl.when(slab < SLABS - 1)
    def _():
        greet(sector, slab + 1)

    for k in range(1, GROUPS):
        greet(twin(k), slab)

    def greet_mate(r, carry):
        greet(mate(r), slab)
        return carry

    lax.fori_loop(1, MEMBERS, greet_mate, 0)

    row = iota((128, 128), 0)
    lane = iota((128, 128), 1)
    for load in lists:
        load.wait()
    owners = owner[...]
    cells = cell[...]
    weights = weight[...]
    live = count[0, 0]
    across, down = [], []
    for q in range(3):
        wide = jnp.broadcast_to(owners[:, q * 128 : (q + 1) * 128], (128, 128)).astype(F32)
        across.append(wide)
        down.append(wide.T)
    slot_pieces, cell_pieces, weight_pieces = [], [], []
    tall = iota((ROWS, 128), 0)
    for q in range(3):
        earlier = jnp.where((down[q] == across[q]) & (row < lane), 1.0, 0.0)
        for s in range(q):
            earlier = earlier + jnp.where(down[s] == across[q], 1.0, 0.0)
        rank = jnp.sum(earlier, axis=0, keepdims=True).astype(I32)
        at = slice(q * 128, (q + 1) * 128)
        name = owners[:, at]
        relative = (name + MEMBERS - member) % MEMBERS
        slot = relative * SLOTS + (name // MEMBERS) * CAP + rank
        place = iota((1, 128), 1) + q * 128
        slot = jnp.where(place < live, slot, -1)
        slot_pieces.append(jnp.where(tall == slot, 1.0, 0.0).astype(BF16))
        cell_pieces.append(jnp.where(row == cells[:, at], 1.0, 0.0).astype(BF16))
        weight_pieces.append(jnp.broadcast_to(weights[:, at], (128, 128)))
    slots = jnp.concatenate(slot_pieces, axis=1)
    spots = jnp.concatenate(cell_pieces, axis=1)
    heavy, light = split(jnp.concatenate(weight_pieces, axis=1))
    picked = dot_nt(slots, spots).astype(BF16)
    pick[...] = picked
    pick_t[...] = dot_nt(spots, slots).astype(BF16)
    factor[...] = dot_nt(slots, heavy) + dot_nt(slots, light)
    spread_row, spread_lane = iota((128, LANES), 0), iota((128, LANES), 1)
    order = spread_lane % WAVES
    turn = jnp.where(order < ORDERS, order, order - (ORDERS - 1))
    turn = turn * (sector * COLS + spread_row % COLS) + jnp.where(order < ORDERS, 0, 768)
    turn = turn % 1024
    table = jnp.cos(turn.astype(F32) * (2.0 * math.pi / 1024.0)) * SCALE
    table = jnp.where(order < MODES, table, 0.0)
    table_high, table_low = split(table)
    waves = dot(picked, table_high) + dot(picked, table_low)
    tall, tall_lane = iota((ROWS, LANES), 0), iota((ROWS, LANES), 1)
    waves = jnp.where((tall % SLOTS) // CAP == tall_lane // WAVES, waves, 0.0)
    waves = waves.reshape(MEMBERS, SLOTS, LANES)
    halves = waves[:, :8]
    for h in range(1, SLOTS // 8):
        halves = halves + waves[:, h * 8 : (h + 1) * 8]
    wave_out[...] = halves + jnp.concatenate([halves[:, 4:], halves[:, :4]], axis=1)

    sub = iota((8, 128), 0)
    ray = iota((8, 128), 1)
    pairs = jnp.zeros((1, 128), I32)
    for c in range(COLS):
        pairs = jnp.where(lane[:1] % COLS == c, pair[0, c], pairs)
    parity = jnp.where((sub == 2) | (sub == 3), -1.0, 1.0)

    def crossing(columns):
        meets = (row % COLS == columns) & (row // COLS == lane // COLS)
        return jnp.where(meets, 1.0, 0.0).astype(BF16)

    cross = crossing(pairs)

    def across_axis(fields, matrix):
        high, low = split(fields)
        return dot(high, matrix) + dot(low, matrix)

    def matrix_columns(entry):
        columns = []
        for g in range(5):
            column = jnp.zeros((8, 128), F32)
            for f in range(5):
                column = jnp.where(sub == f, entry(f, g), column)
            columns.append(column)
        return columns

    radial = matrix_columns(lambda f, g: flux_r[f, g] * HALF)
    radial_t = matrix_columns(lambda f, g: -flux_r[g, f] * HALF)

    def met(columns, mirrored, speed):
        total = columns[0] * mirrored[:1]
        for g in range(1, 5):
            total = total + columns[g] * mirrored[g : g + 1]
        return jnp.where(sub < 5, mirrored * SPREAD + total * speed, 0.0)

    @pl.when(slab == 0)
    def _():
        for ref in (q0, q1, p0, p1):
            ref[:, 0] = jnp.zeros_like(ref[:, 0])

    @pl.when(slab == SLABS - 1)
    def _():
        for ref in (q0, q1, p0, p1):
            ref[:, PLANES + 1] = jnp.zeros_like(ref[:, PLANES + 1])

    def pack_columns(ref, level, fields):
        flat = ref.reshape(ref.shape[0] * (PLANES + 2) * COLS, RADII)
        for f in fields:
            for side, c in ((0, 0), (1, COLS - 1)):
                begin = (f * (PLANES + 2) + 1) * COLS + c
                col_send[level, side, f * PLANES : (f + 1) * PLANES] = flat[
                    pl.ds(begin, PLANES, stride=COLS), :
                ]

    def columns_of(ref, level, phase, first, number):
        rows = pl.ds(first * PLANES, number * PLANES)
        copies = []
        for side, to in ((0, left), (1, right)):
            copies.append(
                pltpu.make_async_remote_copy(
                    src_ref=col_send.at[level, side, rows],
                    dst_ref=col_recv.at[level, side, rows],
                    send_sem=halo_send.at[phase, side],
                    recv_sem=halo_recv.at[phase, side],
                    device_id=(to, slab),
                    device_id_type=MESH,
                )
            )
        return copies

    def planes_of(ref, phase, first, number):
        fields = pl.ds(first, number)
        up = pltpu.make_async_remote_copy(
            src_ref=ref.at[fields, PLANES],
            dst_ref=ref.at[fields, 0],
            send_sem=halo_send.at[phase, 2],
            recv_sem=halo_recv.at[phase, 2],
            device_id=(sector, lax.rem(slab + 1, SLABS)),
            device_id_type=MESH,
        )
        downward = pltpu.make_async_remote_copy(
            src_ref=ref.at[fields, 1],
            dst_ref=ref.at[fields, PLANES + 1],
            send_sem=halo_send.at[phase, 3],
            recv_sem=halo_recv.at[phase, 3],
            device_id=(sector, lax.rem(slab + SLABS - 1, SLABS)),
            device_id_type=MESH,
        )
        return up, downward

    def mirror_of(level):
        return pltpu.make_async_remote_copy(
            src_ref=mir_send.at[level],
            dst_ref=mir_recv.at[level],
            send_sem=mirror_sems.at[0, level],
            recv_sem=mirror_sems.at[1, level],
            device_id=(behind, slab),
            device_id_type=MESH,
        )

    def send_mirror(level):
        mirror_of(level).start()
        sent.append(lambda: mirror_of(level).wait_send())

    def exchange(ref, level, phase, first, number, act):
        for copy in columns_of(ref, level, phase, first, number):
            act(copy, "both")
        up, downward = planes_of(ref, phase, first, number)

        @pl.when(slab < SLABS - 1)
        def _():
            act(up, "send")
            act(downward, "recv")

        @pl.when(slab > 0)
        def _():
            act(downward, "send")
            act(up, "recv")

    def start(copy, part_of):
        if part_of != "recv":
            copy.start()

    def arrive(copy, part_of):
        if part_of != "send":
            copy.wait_recv()

    def leave(copy, part_of):
        if part_of != "recv":
            copy.wait_send()

    def pack_inner(i, fields):
        here = jnp.zeros((8, 128), F32)
        for f, value in enumerate(fields):
            here = jnp.where(ray == f, value if f == 0 else pltpu.roll(value, f, 1), here)
        rows0[i] = here

    def packed():
        return rows0[...].reshape(128, 128).T[:8]

    def unpack(fields):
        wide = jnp.concatenate([fields, jnp.zeros((120, 128), F32)], axis=0)
        turned[...] = wide.T.reshape(PLANES, COLS, 128)

    def lane_zero(inner, f):
        return inner if f == 0 else pltpu.roll(inner, 128 - f, 1)

    def add_inner(ref):
        def step(i, carry):
            inner = turned[i]
            for f in range(5):
                ref[f, i + 1] += jnp.where(ray == 0, lane_zero(inner, f), 0.0)
            return carry

        lax.fori_loop(0, PLANES, step, 0, unroll=4)

    def beside(value, level, f, i, inner):
        before = jnp.broadcast_to(col_recv[level, 1, pl.ds(f * PLANES + i, 1), :], (8, 128))
        after = jnp.broadcast_to(col_recv[level, 0, pl.ds(f * PLANES + i, 1), :], (8, 128))
        t_minus = jnp.where(sub == 0, before, pltpu.roll(value, 1, 0))
        t_plus = jnp.where(sub == COLS - 1, after, pltpu.roll(value, COLS - 1, 0))
        core = 0.0 if inner is None else lane_zero(inner, f)
        r_minus = jnp.where(ray == 0, core, pltpu.roll(value, 1, 1))
        r_plus = jnp.where(ray == RADII - 1, 0.0, pltpu.roll(value, RADII - 1, 1))
        return t_minus, t_plus, r_minus, r_plus

    inverse = 1.0 / (ray.astype(F32) + 0.5)

    def forward_plane(src, level, dst, mirrored, i):
        u, c = q0[5, i + 1] * HALF, q0[6, i + 1] * HALF
        inner = turned[i] if mirrored else None
        values, dx, dr, dt, around = [], [], [], [], []
        for f in range(5):
            value, x_minus, x_plus = src[f, i + 1], src[f, i], src[f, i + 2]
            t_minus, t_plus, r_minus, r_plus = beside(value, level, f, i, inner)
            values.append(value)
            dx.append(x_plus - x_minus)
            dr.append(r_plus - r_minus)
            dt.append((t_plus - t_minus) * inverse)
            around.append((x_plus + x_minus) + (t_plus + t_minus) + (r_plus + r_minus))
        results = []
        for f in range(5):
            mixed = flux_a[f, 0] * dx[0] + flux_r[f, 0] * dr[0] + flux_t[f, 0] * dt[0]
            for g in range(1, 5):
                mixed = mixed + flux_a[f, g] * dx[g] + flux_r[f, g] * dr[g] + flux_t[f, g] * dt[g]
            result = values[f] * KEEP + around[f] * SPREAD - u * dx[f] - c * mixed
            dst[f, i + 1] = result
            results.append(result)
        pack_inner(i, results)

    def adjoint_plane(src, level, store, mirrored, i):
        u_minus, u_plus = q0[5, i] * HALF, q0[5, i + 2] * HALF
        c = q0[6, i + 1] * HALF
        c_minus, c_plus = q0[6, i] * HALF, q0[6, i + 2] * HALF
        before = jnp.broadcast_to(col_recv[0, 1, pl.ds(6 * PLANES + i, 1), :], (8, 128)) * HALF
        after = jnp.broadcast_to(col_recv[0, 0, pl.ds(6 * PLANES + i, 1), :], (8, 128)) * HALF
        inner = turned[i] if mirrored else None
        c_t_minus = jnp.where(sub == 0, before, pltpu.roll(c, 1, 0)) * inverse
        c_t_plus = jnp.where(sub == COLS - 1, after, pltpu.roll(c, COLS - 1, 0)) * inverse
        core = lane_zero(inner, 5) * HALF if mirrored else 0.0
        c_r_minus = jnp.where(ray == 0, core, pltpu.roll(c, 1, 1))
        c_r_plus = pltpu.roll(c, RADII - 1, 1)
        carried, dx, dr, dt = [], [], [], []
        for f in range(5):
            value, x_minus, x_plus = src[f, i + 1], src[f, i], src[f, i + 2]
            t_minus, t_plus, r_minus, r_plus = beside(value, level, f, i, inner)
            dx.append(c_plus * x_plus - c_minus * x_minus)
            dr.append(c_r_plus * r_plus - c_r_minus * r_minus)
            dt.append(c_t_plus * t_plus - c_t_minus * t_minus)
            around = (x_plus + x_minus) + (t_plus + t_minus) + (r_plus + r_minus)
            carried.append(
                value * KEEP + around * SPREAD + (u_plus * x_plus - u_minus * x_minus)
            )
        results = []
        for f in range(5):
            result = carried[f]
            for g in range(5):
                result = result + flux_a[g, f] * dx[g] + flux_r[g, f] * dr[g] + flux_t[g, f] * dt[g]
            store(f, i, result)
            results.append(result)
        if not mirrored:
            pack_inner(i, results)

    def planes(body):
        def step(i, carry):
            body(i)
            return carry

        lax.fori_loop(0, PLANES, step, 0, unroll=UNROLL)

    for load in loads:
        load.wait()
    pack_columns(q0, 0, range(7))
    planes(lambda i: pack_inner(i, [q0[f, i + 1] for f in (0, 1, 2, 3, 4, 6)]))
    first_rows = jnp.where(sub == 6, pairs.astype(F32), packed())
    mir_send[0] = first_rows
    pl.semaphore_wait(
        barrier,
        MEMBERS - 1 + GROUPS - 1 + 2 + jnp.where(slab > 0, 1, 0) + jnp.where(slab < SLABS - 1, 1, 0),
    )
    send_mirror(0)
    exchange(q0, 0, 0, 0, 7, start)
    sent.append(lambda: exchange(q0, 0, 0, 0, 7, leave))

    def to_mate(source, target, which):
        def copy_of(r):
            return pltpu.make_async_remote_copy(
                src_ref=source.at[r],
                dst_ref=target.at[r],
                send_sem=many_send.at[which],
                recv_sem=many_recv.at[which],
                device_id=(mate(r), slab),
                device_id_type=MESH,
            )

        return copy_of

    def back_mate(source, target, which):
        def copy_of(r):
            return pltpu.make_async_remote_copy(
                src_ref=source.at[r],
                dst_ref=target.at[r],
                send_sem=many_send.at[which],
                recv_sem=many_recv.at[which],
                device_id=(mate(MEMBERS - r), slab),
                device_id_type=MESH,
            )

        return copy_of

    def start_all(copy_of):
        def step(r, carry):
            copy_of(r).start()
            return carry

        lax.fori_loop(1, MEMBERS, step, 0)

    def all_of(source, target, which):
        rest = pl.ds(1, MEMBERS - 1)
        return pltpu.make_async_remote_copy(
            src_ref=source.at[rest],
            dst_ref=target.at[rest],
            send_sem=many_send.at[which],
            recv_sem=many_recv.at[which],
            device_id=(right, slab),
            device_id_type=MESH,
        )

    start_all(to_mate(wave_out, wave_in, 0))
    sent.append(lambda: all_of(wave_out, wave_in, 0).wait_send())
    wave_in[0] = wave_out[0]
    exchange(q0, 0, 0, 0, 7, arrive)
    planes(functools.partial(forward_plane, q0, 0, q1, False))
    mir_send[1] = packed()
    send_mirror(1)
    mirror_of(0).wait_recv()
    theirs = mir_recv[0]
    mirrored = across_axis(theirs, cross)
    core_speed = mirrored[5:6]
    unpack(met(radial, mirrored * parity, first_rows[5:6]))
    add_inner(q1)
    pack_columns(q1, 1, range(5))
    exchange(q1, 1, 1, 0, 5, start)
    sent.append(lambda: exchange(q1, 1, 1, 0, 5, leave))
    cross_back = crossing(theirs[6:7].astype(I32))
    there = across_axis(first_rows, cross_back)
    core_speed_there = there[5:6]
    addition = met(radial, there * parity, theirs[5:6])
    mirror_of(1).wait_recv()
    unpack(across_axis(mir_recv[1] + addition, cross) * parity)
    exchange(q1, 1, 1, 0, 5, arrive)
    planes(functools.partial(forward_plane, q1, 1, p0, True))

    pressure = p0[4, 1 : PLANES + 1].reshape(PLANES * COLS, RADII)
    high, low = split(pressure)
    lines = (dot(pick[...], high) + dot(pick[...], low)) * factor[...]
    lines_out[...] = lines.reshape(MEMBERS, SLOTS, RADII)
    start_all(to_mate(lines_out, lines_in, 1))
    sent.append(lambda: all_of(lines_out, lines_in, 1).wait_send())
    lines_in[0] = lines_out[0]
    forward_rows = packed()
    pack_columns(p0, 2, range(4))
    exchange(p0, 2, 2, 0, 4, start)
    sent.append(lambda: exchange(p0, 2, 2, 0, 4, leave))
    all_of(wave_out, wave_in, 0).wait_recv()
    given = wave_in[...]
    sub3, ray3 = iota((MEMBERS, 8, LANES), 1), iota((MEMBERS, 8, LANES), 2)
    quarters = []
    for h in range(SLOTS // 8):
        quarters.append(jnp.where(sub3 // CAP + 2 * h == ray3 // WAVES, given, 0.0))
    encoder = jnp.concatenate(quarters, axis=1).reshape(ROWS, LANES)
    enc[0], enc[1] = split(encoder)
    enc_t[0], enc_t[1] = split(encoder.T)

    all_of(lines_out, lines_in, 1).wait_recv()
    high, low = split(lines_in[...].reshape(ROWS, RADII))
    part[...] = dot(enc_t[0], high) + (dot(enc_t[0], low) + dot(enc_t[1], high))

    def to_twin(k):
        return pltpu.make_async_remote_copy(
            src_ref=part.at[pl.ds(pl.multiple_of(lax.rem(group + k, GROUPS) * WAVES, WAVES), WAVES)],
            dst_ref=part_in.at[k - 1],
            send_sem=few_send.at[0, k - 1],
            recv_sem=few_recv.at[0, k - 1],
            device_id=(twin(k), slab),
            device_id_type=MESH,
        )

    own_rows = pl.ds(pl.multiple_of(group * WAVES, WAVES), WAVES)

    def from_owner(k):
        return pltpu.make_async_remote_copy(
            src_ref=whole.at[own_rows],
            dst_ref=whole.at[own_rows],
            send_sem=few_send.at[1, k - 1],
            recv_sem=few_recv.at[1, k - 1],
            device_id=(twin(k), slab),
            device_id_type=MESH,
        )

    for k in range(1, GROUPS):
        to_twin(k).start()
        sent.append(lambda k=k: to_twin(k).wait_send())
    mine = part[own_rows, :]
    for k in range(1, GROUPS):
        to_twin(k).wait_recv()
        mine = mine + part_in[k - 1]
    whole[own_rows, :] = mine
    for k in range(1, GROUPS):
        from_owner(k).start()
        sent.append(lambda k=k: from_owner(k).wait_send())
    harm[0, 0] = mine[:MODES]
    for k in range(1, GROUPS):
        from_owner(k).wait_recv()

    high, low = split(whole[...])
    grad = dot(enc[0], high) + (dot(enc[0], low) + dot(enc[1], high))
    grad_out[...] = grad.reshape(MEMBERS, SLOTS, RADII)
    start_all(back_mate(grad_out, grad_in, 2))
    sent.append(lambda: all_of(grad_out, grad_in, 2).wait_send())
    grad_in[0] = grad_out[0]
    exchange(p0, 2, 2, 0, 4, arrive)
    all_of(grad_out, grad_in, 2).wait_recv()
    high, low = split(grad_in[...].reshape(ROWS, RADII) * factor[...])
    impulse = dot(pick_t[...], high) + dot(pick_t[...], low)
    impulse = impulse.reshape(PLANES, COLS, RADII)
    p0[4, 1 : PLANES + 1] = p0[4, 1 : PLANES + 1] + impulse

    pressure = p0[4, 1 : PLANES + 1].reshape(PLANES * COLS, RADII)
    start_rows = jnp.where(sub == 4, pressure.T[:1], forward_rows)
    mir_send[2] = start_rows
    send_mirror(2)
    pack_columns(p0, 2, (4,))
    exchange(p0, 2, 3, 4, 1, start)
    sent.append(lambda: exchange(p0, 2, 3, 4, 1, leave))
    exchange(p0, 2, 3, 4, 1, arrive)

    def store_p1(f, i, value):
        p1[f, i + 1] = value

    def store_out(f, i, value):
        out[f, i] = value

    planes(functools.partial(adjoint_plane, p0, 2, store_p1, False))
    mir_send[3] = packed()
    send_mirror(3)
    there = across_axis(start_rows, cross_back) * parity
    addition = met(radial_t, there, core_speed_there)
    mirror_of(2).wait_recv()
    mirrored = across_axis(mir_recv[2], cross) * parity
    unpack(met(radial_t, mirrored, core_speed))
    add_inner(p1)
    pack_columns(p1, 3, range(5))
    exchange(p1, 3, 4, 0, 5, start)
    sent.append(lambda: exchange(p1, 3, 4, 0, 5, leave))
    mirror_of(3).wait_recv()
    mirrored = across_axis(mir_recv[3] + addition, cross) * parity
    unpack(jnp.where(sub == 5, core_speed, mirrored))
    exchange(p1, 3, 4, 0, 5, arrive)
    planes(functools.partial(adjoint_plane, p1, 3, store_out, True))

    for wait in sent:
        wait()


def local(
    state,
    mean_velocity,
    sound_speed,
    flux_axial,
    flux_radial,
    flux_azimuthal,
    axis_pair,
    panel_weight,
    panel_cell,
    panel_owner,
    panel_count,
):
    anywhere = pl.BlockSpec(memory_space=pl.ANY)
    scalar = pl.BlockSpec(memory_space=pltpu.SMEM)
    vector = pl.BlockSpec(memory_space=pltpu.VMEM)

    def grid_of(fields):
        return pltpu.VMEM((fields, PLANES + 2, COLS, RADII), F32)

    return pl.pallas_call(
        kernel,
        out_shape=(
            jax.ShapeDtypeStruct((5, PLANES, COLS, RADII), F32),
            jax.ShapeDtypeStruct((1, 1, MODES, RADII), F32),
        ),
        in_specs=[anywhere] * 3 + [scalar] * 4 + [anywhere] * 3 + [scalar],
        out_specs=(vector, vector),
        scratch_shapes=[
            grid_of(7),
            grid_of(5),
            grid_of(5),
            grid_of(5),
            pltpu.VMEM((1, PANELS), F32),
            pltpu.VMEM((1, PANELS), I32),
            pltpu.VMEM((1, PANELS), I32),
            pltpu.VMEM((4, 2, 7 * PLANES, RADII), F32),
            pltpu.VMEM((4, 2, 7 * PLANES, RADII), F32),
            pltpu.VMEM((4, 8, 128), F32),
            pltpu.VMEM((4, 8, 128), F32),
            pltpu.VMEM((PLANES, COLS, 128), F32),
            pltpu.VMEM((PLANES, COLS, 128), F32),
            pltpu.VMEM((ROWS, 128), BF16),
            pltpu.VMEM((128, ROWS), BF16),
            pltpu.VMEM((ROWS, 128), F32),
            pltpu.VMEM((MEMBERS, 8, LANES), F32),
            pltpu.VMEM((MEMBERS, 8, LANES), F32),
            pltpu.VMEM((2, ROWS, LANES), BF16),
            pltpu.VMEM((2, LANES, ROWS), BF16),
            pltpu.VMEM((MEMBERS, SLOTS, RADII), F32),
            pltpu.VMEM((MEMBERS, SLOTS, RADII), F32),
            pltpu.VMEM((GROUPS * WAVES, RADII), F32),
            pltpu.VMEM((GROUPS - 1, WAVES, RADII), F32),
            pltpu.VMEM((GROUPS * WAVES, RADII), F32),
            pltpu.VMEM((MEMBERS, SLOTS, RADII), F32),
            pltpu.VMEM((MEMBERS, SLOTS, RADII), F32),
            pltpu.SemaphoreType.DMA((6,)),
            pltpu.SemaphoreType.DMA((5, 4)),
            pltpu.SemaphoreType.DMA((5, 4)),
            pltpu.SemaphoreType.DMA((2, 4)),
            pltpu.SemaphoreType.DMA((3,)),
            pltpu.SemaphoreType.DMA((3,)),
            pltpu.SemaphoreType.DMA((2, GROUPS - 1)),
            pltpu.SemaphoreType.DMA((2, GROUPS - 1)),
        ],
        compiler_params=pltpu.CompilerParams(
            collective_id=0, has_side_effects=True, vmem_limit_bytes=VMEM_GRANT
        ),
    )(
        state,
        mean_velocity,
        sound_speed,
        flux_axial,
        flux_radial,
        flux_azimuthal,
        axis_pair,
        panel_weight,
        panel_cell,
        panel_owner.reshape(1, PANELS),
        panel_count,
    )


def solution(mesh):
    return jax.shard_map(
        local,
        mesh=mesh,
        in_specs=(
            P(None, "slab", "sector", None),
            P("slab", "sector", None),
            P("slab", "sector", None),
            P(),
            P(),
            P(),
            P("sector", None),
            P("slab", "sector"),
            P("slab", "sector"),
            P("slab", "sector", None),
            P("slab", "sector"),
        ),
        out_specs=(P(None, "slab", "sector", None), P("slab", "sector", None, None)),
        check_vma=False,
    )
```

```python
import functools
import math

import jax
import jax.numpy as jnp
from jax import lax
from jax.experimental import pallas as pl
from jax.experimental.pallas import tpu as pltpu
from jax.sharding import PartitionSpec as P

PLANES = 16
COLS = 8
RADII = 128
PANELS = 384
ORDERS = 16
MODES = 31
SECTORS = 128
SLABS = 4
GROUPS = 8
MEMBERS = SECTORS // GROUPS
CAP = 4
SLOTS = GROUPS * CAP
ROWS = MEMBERS * SLOTS
WAVES = 32
LANES = GROUPS * WAVES
SCALE = PANELS**-0.5
TIME_STEP = 0.25
VISCOSITY = 0.05
KEEP = 1.0 - 6.0 * VISCOSITY * TIME_STEP
SPREAD = VISCOSITY * TIME_STEP
HALF = 0.5 * TIME_STEP
FAR_FIRST = sorted(range(1, GROUPS), key=lambda k: abs(k - GROUPS // 2))
UNROLL = 4
VMEM_GRANT = 60 << 20
MESH = pl.DeviceIdType.MESH
F32, BF16, I32 = jnp.float32, jnp.bfloat16, jnp.int32


def split(x):
    high = x.astype(BF16)
    return high, (x - high.astype(F32)).astype(BF16)


def dot(a, b):
    return lax.dot_general(a, b, (((1,), (0,)), ((), ())), preferred_element_type=F32)


def dot_nt(a, b):
    return lax.dot_general(a, b, (((1,), (1,)), ((), ())), preferred_element_type=F32)


def iota(shape, dim):
    return lax.broadcasted_iota(I32, shape, dim)


def kernel(
    state,
    mean,
    sound,
    flux_a_in,
    flux_r_in,
    flux_t_in,
    pair_in,
    weight_in,
    cell_in,
    owner_in,
    count_in,
    out,
    harm,
    q0,
    q1,
    p0,
    p1,
    weight,
    cell,
    owner,
    flux_a,
    flux_r,
    flux_t,
    pair,
    count,
    col_send,
    col_recv,
    tile,
    near,
    far,
    far_near,
    rows0,
    turned,
    pick,
    pick_t,
    factor,
    wave_out,
    wave_in,
    enc,
    enc_t,
    lines_out,
    lines_in,
    part,
    part_in,
    whole,
    grad_out,
    grad_in,
    load_sem,
    halo_send,
    halo_recv,
    tile_send,
    tile_recv,
    many_send,
    many_recv,
    few_send,
    few_recv,
):
    sector = lax.axis_index("sector")
    slab = lax.axis_index("slab")
    group = lax.div(sector, MEMBERS)
    member = lax.rem(sector, MEMBERS)
    right = lax.rem(sector + 1, SECTORS)
    left = lax.rem(sector + SECTORS - 1, SECTORS)
    behind = lax.rem(sector + SECTORS // 2, SECTORS)

    def mate(r):
        return group * MEMBERS + lax.rem(member + r, MEMBERS)

    def twin(k):
        return lax.rem(group + k, GROUPS) * MEMBERS + member

    loads = [
        pltpu.make_async_copy(state, q0.at[pl.ds(0, 5), pl.ds(1, PLANES)], load_sem.at[0]),
        pltpu.make_async_copy(mean, q0.at[5, pl.ds(1, PLANES)], load_sem.at[1]),
        pltpu.make_async_copy(sound, q0.at[6, pl.ds(1, PLANES)], load_sem.at[2]),
    ]
    lists = [
        pltpu.make_async_copy(weight_in, weight, load_sem.at[3]),
        pltpu.make_async_copy(cell_in, cell, load_sem.at[4]),
        pltpu.make_async_copy(owner_in, owner, load_sem.at[5]),
        pltpu.make_async_copy(flux_a_in, flux_a, load_sem.at[6]),
        pltpu.make_async_copy(flux_r_in, flux_r, load_sem.at[7]),
        pltpu.make_async_copy(flux_t_in, flux_t, load_sem.at[8]),
        pltpu.make_async_copy(pair_in, pair, load_sem.at[9]),
        pltpu.make_async_copy(count_in, count, load_sem.at[10]),
    ]
    for load in lists + loads:
        load.start()

    sent = []

    barrier = pltpu.get_barrier_semaphore()

    def greet(to_sector, to_slab):
        pl.semaphore_signal(barrier, inc=1, device_id=(to_sector, to_slab), device_id_type=MESH)

    behind_right = lax.rem(behind + 1, SECTORS)
    behind_left = lax.rem(behind + SECTORS - 1, SECTORS)
    greet(right, slab)
    greet(left, slab)
    greet(behind_right, slab)
    greet(behind_left, slab)

    @pl.when(slab > 0)
    def _():
        greet(sector, slab - 1)
        greet(behind, slab - 1)

    @pl.when(slab < SLABS - 1)
    def _():
        greet(sector, slab + 1)
        greet(behind, slab + 1)

    for k in range(1, GROUPS):
        greet(twin(k), slab)

    def greet_mate(r, carry):
        greet(mate(r), slab)
        return carry

    lax.fori_loop(1, MEMBERS, greet_mate, 0)

    row = iota((128, 128), 0)
    lane = iota((128, 128), 1)
    for load in lists:
        load.wait()
    owners = owner[...]
    cells = cell[...]
    weights = weight[...]
    live = count[0, 0]
    across, down = [], []
    for q in range(3):
        wide = jnp.broadcast_to(owners[:, q * 128 : (q + 1) * 128], (128, 128)).astype(F32)
        across.append(wide)
        down.append(wide.T)
    slot_pieces, cell_pieces, weight_pieces = [], [], []
    tall = iota((ROWS, 128), 0)
    for q in range(3):
        earlier = jnp.where((down[q] == across[q]) & (row < lane), 1.0, 0.0)
        for s in range(q):
            earlier = earlier + jnp.where(down[s] == across[q], 1.0, 0.0)
        rank = jnp.sum(earlier, axis=0, keepdims=True).astype(I32)
        at = slice(q * 128, (q + 1) * 128)
        name = owners[:, at]
        relative = (name + MEMBERS - member) % MEMBERS
        slot = relative * SLOTS + (name // MEMBERS) * CAP + rank
        place = iota((1, 128), 1) + q * 128
        slot = jnp.where(place < live, slot, -1)
        slot_pieces.append(jnp.where(tall == slot, 1.0, 0.0).astype(BF16))
        cell_pieces.append(jnp.where(row == cells[:, at], 1.0, 0.0).astype(BF16))
        weight_pieces.append(jnp.broadcast_to(weights[:, at], (128, 128)))
    slots = jnp.concatenate(slot_pieces, axis=1)
    spots = jnp.concatenate(cell_pieces, axis=1)
    heavy, light = split(jnp.concatenate(weight_pieces, axis=1))
    picked = dot_nt(slots, spots).astype(BF16)
    pick[...] = picked
    pick_t[...] = dot_nt(spots, slots).astype(BF16)
    factor[...] = dot_nt(slots, heavy) + dot_nt(slots, light)
    spread_row, spread_lane = iota((128, LANES), 0), iota((128, LANES), 1)
    order = spread_lane % WAVES
    turn = jnp.where(order < ORDERS, order, order - (ORDERS - 1))
    turn = turn * (sector * COLS + spread_row % COLS) + jnp.where(order < ORDERS, 0, 768)
    turn = turn % 1024
    table = jnp.cos(turn.astype(F32) * (2.0 * math.pi / 1024.0)) * SCALE
    table = jnp.where(order < MODES, table, 0.0)
    table_high, table_low = split(table)
    waves = dot(picked, table_high) + dot(picked, table_low)
    tall, tall_lane = iota((ROWS, LANES), 0), iota((ROWS, LANES), 1)
    waves = jnp.where((tall % SLOTS) // CAP == tall_lane // WAVES, waves, 0.0)
    waves = waves.reshape(MEMBERS, SLOTS, LANES)
    halves = waves[:, :8]
    for h in range(1, SLOTS // 8):
        halves = halves + waves[:, h * 8 : (h + 1) * 8]
    wave_out[...] = halves + jnp.concatenate([halves[:, 4:], halves[:, :4]], axis=1)

    sub = iota((8, 128), 0)
    ray = iota((8, 128), 1)
    pairs = jnp.zeros((1, 128), I32)
    for c in range(COLS):
        pairs = jnp.where(lane[:1] % COLS == c, pair[0, c], pairs)
    parity = jnp.where((sub == 2) | (sub == 3), -1.0, 1.0)

    def crossing(columns):
        meets = (row % COLS == columns) & (row // COLS == lane // COLS)
        return jnp.where(meets, 1.0, 0.0).astype(BF16)

    cross = crossing(pairs)

    def across_axis(fields, matrix):
        high, low = split(fields)
        return dot(high, matrix) + dot(low, matrix)

    def matrix_columns(entry):
        columns = []
        for g in range(5):
            column = jnp.zeros((8, 128), F32)
            for f in range(5):
                column = jnp.where(sub == f, entry(f, g), column)
            columns.append(column)
        return columns

    axial = matrix_columns(lambda f, g: flux_a[f, g] * HALF)
    radial = matrix_columns(lambda f, g: flux_r[f, g] * HALF)
    angular = matrix_columns(lambda f, g: flux_t[f, g] * (2.0 * HALF))
    axial_t = matrix_columns(lambda f, g: flux_a[g, f] * HALF)
    radial_t = matrix_columns(lambda f, g: flux_r[g, f] * HALF)
    angular_t = matrix_columns(lambda f, g: flux_t[g, f] * (2.0 * HALF))
    radial_back = [-column for column in radial_t]

    def met(columns, mirrored, speed):
        return jnp.where(sub < 5, mirrored * SPREAD + mix(columns, mirrored) * speed, 0.0)

    @pl.when(slab == 0)
    def _():
        for ref in (near, far_near):
            ref[:, 3] = jnp.zeros((2, 8, 128), F32)
        for ref in (q0, q1, p0, p1):
            ref[:, 0] = jnp.zeros_like(ref[:, 0])

    @pl.when(slab == SLABS - 1)
    def _():
        for ref in (near, far_near):
            ref[:, 2] = jnp.zeros((2, 8, 128), F32)
        for ref in (q0, q1, p0, p1):
            ref[:, PLANES + 1] = jnp.zeros_like(ref[:, PLANES + 1])

    def pack_columns(ref, level, fields):
        flat = ref.reshape(ref.shape[0] * (PLANES + 2) * COLS, RADII)
        for f in fields:
            for side, c in ((0, 0), (1, COLS - 1)):
                begin = (f * (PLANES + 2) + 1) * COLS + c
                col_send[level, side, f * PLANES : (f + 1) * PLANES] = flat[
                    pl.ds(begin, PLANES, stride=COLS), :
                ]

    def columns_of(ref, level, phase, first, number):
        rows = pl.ds(first * PLANES, number * PLANES)
        copies = []
        for side, to in ((0, left), (1, right)):
            copies.append(
                pltpu.make_async_remote_copy(
                    src_ref=col_send.at[level, side, rows],
                    dst_ref=col_recv.at[level, side, rows],
                    send_sem=halo_send.at[phase, side],
                    recv_sem=halo_recv.at[phase, side],
                    device_id=(to, slab),
                    device_id_type=MESH,
                )
            )
        return copies

    def planes_of(ref, phase, first, number):
        fields = pl.ds(first, number)
        up = pltpu.make_async_remote_copy(
            src_ref=ref.at[fields, PLANES],
            dst_ref=ref.at[fields, 0],
            send_sem=halo_send.at[phase, 2],
            recv_sem=halo_recv.at[phase, 2],
            device_id=(sector, lax.rem(slab + 1, SLABS)),
            device_id_type=MESH,
        )
        downward = pltpu.make_async_remote_copy(
            src_ref=ref.at[fields, 1],
            dst_ref=ref.at[fields, PLANES + 1],
            send_sem=halo_send.at[phase, 3],
            recv_sem=halo_recv.at[phase, 3],
            device_id=(sector, lax.rem(slab + SLABS - 1, SLABS)),
            device_id_type=MESH,
        )
        return up, downward

    def tile_copy(which, place, source, target, to):
        return pltpu.make_async_remote_copy(
            src_ref=source,
            dst_ref=target,
            send_sem=tile_send.at[which, place],
            recv_sem=tile_recv.at[which, place],
            device_id=to,
            device_id_type=MESH,
        )

    slab_down, slab_up = lax.rem(slab + SLABS - 1, SLABS), lax.rem(slab + 1, SLABS)

    def exchange_tiles(which, act):
        inner = tile.at[which, pl.ds(0, 8)]
        act(tile_copy(which, 8, tile.at[which], far.at[which], (behind, slab)), "both")
        act(tile_copy(which, 4, inner, far_near.at[which, 0], (behind_left, slab)), "both")
        act(tile_copy(which, 5, inner, far_near.at[which, 1], (behind_right, slab)), "both")
        act(tile_copy(which, 0, inner, near.at[which, 0], (left, slab)), "both")
        act(tile_copy(which, 1, inner, near.at[which, 1], (right, slab)), "both")
        downward = (
            tile_copy(which, 6, inner, far_near.at[which, 2], (behind, slab_down)),
            tile_copy(which, 2, inner, near.at[which, 2], (sector, slab_down)),
        )
        upward = (
            tile_copy(which, 7, inner, far_near.at[which, 3], (behind, slab_up)),
            tile_copy(which, 3, inner, near.at[which, 3], (sector, slab_up)),
        )

        @pl.when(slab > 0)
        def _():
            for copy in downward:
                act(copy, "send")
            for copy in upward:
                act(copy, "recv")

        @pl.when(slab < SLABS - 1)
        def _():
            for copy in upward:
                act(copy, "send")
            for copy in downward:
                act(copy, "recv")

    def shifted(rows, beside):
        from_right, from_left, from_up, from_down = beside
        t_minus = jnp.where(ray % COLS == 0, pltpu.roll(from_left, 121, 1), pltpu.roll(rows, 1, 1))
        t_plus = jnp.where(ray % COLS == 7, pltpu.roll(from_right, 7, 1), pltpu.roll(rows, 127, 1))
        x_minus = jnp.where(ray < COLS, pltpu.roll(from_down, 8, 1), pltpu.roll(rows, 8, 1))
        x_plus = jnp.where(ray >= 120, pltpu.roll(from_up, 120, 1), pltpu.roll(rows, 120, 1))
        return x_minus, x_plus, t_minus, t_plus

    def mix(columns, fields):
        total = columns[0] * fields[:1]
        for g in range(1, 5):
            total = total + columns[g] * fields[g : g + 1]
        return total

    def forward_inner(rows, following, beside, speed, flow):
        x_minus, x_plus, t_minus, t_plus = shifted(rows, beside)
        dx = x_plus - x_minus
        mixed = mix(axial, dx) + mix(angular, t_plus - t_minus)
        around = x_plus + x_minus + t_plus + t_minus
        if following is not None:
            mixed, around = mixed + mix(radial, following), around + following
        result = rows * KEEP + around * SPREAD - (flow * HALF) * dx - speed * mixed
        return jnp.where(sub < 5, result, 0.0)

    def adjoint_inner(rows, following, beside, coefs, speed_next):
        x_minus, x_plus, t_minus, t_plus = shifted(rows, beside)
        k_x_minus, k_x_plus, k_t_minus, k_t_plus = coefs
        result = mix(axial_t, x_plus * k_x_plus[5:6] - x_minus * k_x_minus[5:6])
        result = result + mix(angular_t, t_plus * k_t_plus[5:6] - t_minus * k_t_minus[5:6])
        result = result + (x_plus * k_x_plus[6:7] - x_minus * k_x_minus[6:7]) * HALF
        around = x_plus + x_minus + t_plus + t_minus
        if following is not None:
            result, around = result + mix(radial_t, following * speed_next), around + following
        result = result + rows * KEEP + around * SPREAD
        return jnp.where(sub < 5, result, 0.0)

    def stack(which):
        return jnp.concatenate([far[which][:8], far_near[which, 2], far_near[which, 3]], axis=0)

    def exchange(ref, level, phase, first, number, act, planes_first=None):
        for copy in columns_of(ref, level, phase, first, number):
            act(copy, "both")
        if planes_first is None:
            up, downward = planes_of(ref, phase, first, number)
        else:
            up, downward = planes_of(ref, phase, planes_first, first + number - planes_first)

        @pl.when(slab < SLABS - 1)
        def _():
            act(up, "send")
            act(downward, "recv")

        @pl.when(slab > 0)
        def _():
            act(downward, "send")
            act(up, "recv")

    def start(copy, part_of):
        if part_of != "recv":
            copy.start()

    def arrive(copy, part_of):
        if part_of != "send":
            copy.wait_recv()

    def leave(copy, part_of):
        if part_of != "recv":
            copy.wait_send()

    wanted = jnp.where(row[:16] < 8, 2 * row[:16], 2 * (row[:16] - 8) + 1)
    chosen = jnp.where(lane[:16] == wanted, 1.0, 0.0).astype(BF16)

    def pack_inner(i, fields):
        here = jnp.zeros((8, 128), F32)
        for f, value in enumerate(fields):
            here = jnp.where(ray // 2 == f, value if f == 0 else pltpu.roll(value, 2 * f, 1), here)
        rows0[i] = here

    def packed():
        high, low = split(rows0[...].reshape(128, 128))
        both = dot_nt(chosen, high) + dot_nt(chosen, low)
        return both[:8], both[8:]

    def patch(ref, skip, inner, following, fields):
        wide = jnp.concatenate([inner, following, jnp.zeros((112, 128), F32)], axis=0)
        turned[...] = wide.T.reshape(PLANES, COLS, 128)

        def step(i, carry):
            here = turned[i]
            for f in fields:
                zero = here if f == 0 else pltpu.roll(here, 128 - f, 1)
                one = pltpu.roll(here, 121 - f, 1)
                ref[f, i + skip] += jnp.where(ray == 0, zero, jnp.where(ray == 1, one, 0.0))
            return carry

        lax.fori_loop(0, PLANES, step, 0, unroll=4)

    def beside(value, level, f, i):
        before = jnp.broadcast_to(col_recv[level, 1, pl.ds(f * PLANES + i, 1), :], (8, 128))
        after = jnp.broadcast_to(col_recv[level, 0, pl.ds(f * PLANES + i, 1), :], (8, 128))
        t_minus = jnp.where(sub == 0, before, pltpu.roll(value, 1, 0))
        t_plus = jnp.where(sub == COLS - 1, after, pltpu.roll(value, COLS - 1, 0))
        r_minus = jnp.where(ray == 0, 0.0, pltpu.roll(value, 1, 1))
        r_plus = jnp.where(ray == RADII - 1, 0.0, pltpu.roll(value, RADII - 1, 1))
        return t_minus, t_plus, r_minus, r_plus

    inverse = 1.0 / (ray.astype(F32) + 0.5)

    def forward_plane(src, level, dst, i):
        u, c = q0[5, i + 1] * HALF, q0[6, i + 1] * HALF
        values, dx, dr, dt, around = [], [], [], [], []
        for f in range(5):
            value, x_minus, x_plus = src[f, i + 1], src[f, i], src[f, i + 2]
            t_minus, t_plus, r_minus, r_plus = beside(value, level, f, i)
            values.append(value)
            dx.append(x_plus - x_minus)
            dr.append(r_plus - r_minus)
            dt.append((t_plus - t_minus) * inverse)
            around.append((x_plus + x_minus) + (t_plus + t_minus) + (r_plus + r_minus))
        for f in range(5):
            mixed = flux_a[f, 0] * dx[0] + flux_r[f, 0] * dr[0] + flux_t[f, 0] * dt[0]
            for g in range(1, 5):
                mixed = mixed + flux_a[f, g] * dx[g] + flux_r[f, g] * dr[g] + flux_t[f, g] * dt[g]
            dst[f, i + 1] = values[f] * KEEP + around[f] * SPREAD - u * dx[f] - c * mixed

    def adjoint_plane(src, level, store, i):
        u_minus, u_plus = q0[5, i] * HALF, q0[5, i + 2] * HALF
        c = q0[6, i + 1] * HALF
        c_minus, c_plus = q0[6, i] * HALF, q0[6, i + 2] * HALF
        before = jnp.broadcast_to(col_recv[0, 1, pl.ds(6 * PLANES + i, 1), :], (8, 128)) * HALF
        after = jnp.broadcast_to(col_recv[0, 0, pl.ds(6 * PLANES + i, 1), :], (8, 128)) * HALF
        c_t_minus = jnp.where(sub == 0, before, pltpu.roll(c, 1, 0)) * inverse
        c_t_plus = jnp.where(sub == COLS - 1, after, pltpu.roll(c, COLS - 1, 0)) * inverse
        c_r_minus = pltpu.roll(c, 1, 1)
        c_r_plus = pltpu.roll(c, RADII - 1, 1)
        carried, dx, dr, dt = [], [], [], []
        for f in range(5):
            value, x_minus, x_plus = src[f, i + 1], src[f, i], src[f, i + 2]
            t_minus, t_plus, r_minus, r_plus = beside(value, level, f, i)
            dx.append(c_plus * x_plus - c_minus * x_minus)
            dr.append(c_r_plus * r_plus - c_r_minus * r_minus)
            dt.append(c_t_plus * t_plus - c_t_minus * t_minus)
            around = (x_plus + x_minus) + (t_plus + t_minus) + (r_plus + r_minus)
            carried.append(
                value * KEEP + around * SPREAD + (u_plus * x_plus - u_minus * x_minus)
            )
        for f in range(5):
            result = carried[f]
            for g in range(5):
                result = result + flux_a[g, f] * dx[g] + flux_r[g, f] * dr[g] + flux_t[g, f] * dt[g]
            store(f, i, result)

    def planes(body):
        def step(i, carry):
            body(i)
            return carry

        lax.fori_loop(0, PLANES, step, 0, unroll=UNROLL)

    for load in loads:
        load.wait()
    pack_columns(q0, 0, (0, 1, 2, 3, 4, 6))
    planes(lambda i: pack_inner(i, [q0[f, i + 1] for f in (0, 1, 2, 3, 4, 6, 5)]))
    first_rows, first_next = packed()
    first_rows = jnp.where(sub == 7, pairs.astype(F32), first_rows)
    tile[0, :8] = first_rows
    tile[0, 8:] = first_next
    pl.semaphore_wait(
        barrier,
        MEMBERS - 1 + GROUPS - 1 + 4 + jnp.where(slab > 0, 2, 0) + jnp.where(slab < SLABS - 1, 2, 0),
    )
    exchange_tiles(0, start)
    sent.append(lambda: exchange_tiles(0, leave))
    exchange(q0, 0, 0, 0, 5, start)
    sent.append(lambda: exchange(q0, 0, 0, 0, 5, leave))

    def to_mate(source, target, which):
        def copy_of(r):
            return pltpu.make_async_remote_copy(
                src_ref=source.at[r],
                dst_ref=target.at[r],
                send_sem=many_send.at[which],
                recv_sem=many_recv.at[which],
                device_id=(mate(r), slab),
                device_id_type=MESH,
            )

        return copy_of

    def back_mate(source, target, which):
        def copy_of(r):
            return pltpu.make_async_remote_copy(
                src_ref=source.at[r],
                dst_ref=target.at[r],
                send_sem=many_send.at[which],
                recv_sem=many_recv.at[which],
                device_id=(mate(MEMBERS - r), slab),
                device_id_type=MESH,
            )

        return copy_of

    def start_all(copy_of):
        def step(r, carry):
            copy_of(r).start()
            return carry

        lax.fori_loop(4, MEMBERS, step, 0)
        lax.fori_loop(1, 4, step, 0)

    def all_of(source, target, which):
        rest = pl.ds(1, MEMBERS - 1)
        return pltpu.make_async_remote_copy(
            src_ref=source.at[rest],
            dst_ref=target.at[rest],
            send_sem=many_send.at[which],
            recv_sem=many_recv.at[which],
            device_id=(right, slab),
            device_id_type=MESH,
        )

    wave_in[0] = wave_out[0]
    exchange(q0, 0, 0, 0, 5, arrive)
    planes(functools.partial(forward_plane, q0, 0, q1))
    pack_columns(q1, 1, range(5))
    exchange(q1, 1, 1, 0, 5, start)
    sent.append(lambda: exchange(q1, 1, 1, 0, 5, leave))
    start_all(to_mate(wave_out, wave_in, 0))
    sent.append(lambda: all_of(wave_out, wave_in, 0).wait_send())
    exchange(q1, 1, 1, 0, 5, arrive)
    planes(functools.partial(forward_plane, q1, 1, p0))
    exchange_tiles(0, arrive)
    theirs, theirs_next = far[0][:8], far[0][8:]
    by_us = [near[0, k] for k in range(4)]
    by_them = [far_near[0, k] for k in range(4)]
    cross_right = crossing(by_us[0][7:8].astype(I32))
    cross_left = crossing(by_us[1][7:8].astype(I32))
    cross_back = crossing(theirs[7:8].astype(I32))

    def opposite_values(which):
        three = across_axis(stack(which), cross)
        return [
            three[:8],
            across_axis(far_near[which, 0], cross_right),
            across_axis(far_near[which, 1], cross_left),
            three[8:16],
            three[16:],
        ]

    met_values = opposite_values(0)
    met_speeds = [values[5:6] for values in met_values]
    speed, speed_next, flow = first_rows[5:6], first_next[5:6], first_rows[6:7]
    speeds = [speed] + [values[5:6] for values in by_us]
    added = [met(radial, values * parity, at) for values, at in zip(met_values, speeds)]
    there = across_axis(first_rows, cross_back)
    met_speed_there = there[5:6]
    theirs_after = forward_inner(theirs, theirs_next, by_them, theirs[5:6], theirs[6:7])
    theirs_after = theirs_after + met(radial, there * parity, theirs[5:6])
    mirrored = across_axis(theirs_after, cross) * parity
    inner = forward_inner(added[0], None, added[1:], speed, flow) + met(radial, mirrored, speed)
    following = met(radial, added[0], speed_next)
    patch(p0, 1, inner, following, (4,))

    pressure = p0[4, 1 : PLANES + 1].reshape(PLANES * COLS, RADII)
    high, low = split(pressure)
    lines = (dot(pick[...], high) + dot(pick[...], low)) * factor[...]
    lines_out[...] = lines.reshape(MEMBERS, SLOTS, RADII)
    start_all(to_mate(lines_out, lines_in, 1))
    sent.append(lambda: all_of(lines_out, lines_in, 1).wait_send())
    lines_in[0] = lines_out[0]
    patch(p0, 1, inner, following, range(4))
    planes(lambda i: pack_inner(i, [p0[f, i + 1] for f in range(4)]))
    forward_rows, forward_next = packed()
    all_of(wave_out, wave_in, 0).wait_recv()
    given = wave_in[...]
    sub3, ray3 = iota((MEMBERS, 8, LANES), 1), iota((MEMBERS, 8, LANES), 2)
    quarters = []
    for h in range(SLOTS // 8):
        quarters.append(jnp.where(sub3 // CAP + 2 * h == ray3 // WAVES, given, 0.0))
    encoder = jnp.concatenate(quarters, axis=1).reshape(ROWS, LANES)
    enc[0], enc[1] = split(encoder)
    enc_t[0], enc_t[1] = split(encoder.T)

    all_of(lines_out, lines_in, 1).wait_recv()
    high, low = split(lines_in[...].reshape(ROWS, RADII))
    part[...] = dot(enc_t[0], high) + (dot(enc_t[0], low) + dot(enc_t[1], high))

    def to_twin(k):
        return pltpu.make_async_remote_copy(
            src_ref=part.at[pl.ds(pl.multiple_of(lax.rem(group + k, GROUPS) * WAVES, WAVES), WAVES)],
            dst_ref=part_in.at[k - 1],
            send_sem=few_send.at[0, k - 1],
            recv_sem=few_recv.at[0, k - 1],
            device_id=(twin(k), slab),
            device_id_type=MESH,
        )

    own_rows = pl.ds(pl.multiple_of(group * WAVES, WAVES), WAVES)

    def from_owner(k):
        return pltpu.make_async_remote_copy(
            src_ref=whole.at[own_rows],
            dst_ref=whole.at[own_rows],
            send_sem=few_send.at[1, k - 1],
            recv_sem=few_recv.at[1, k - 1],
            device_id=(twin(k), slab),
            device_id_type=MESH,
        )

    for k in FAR_FIRST:
        to_twin(k).start()
        sent.append(lambda k=k: to_twin(k).wait_send())
    pack_columns(p0, 2, range(4))
    exchange(p0, 2, 2, 0, 4, start)
    sent.append(lambda: exchange(p0, 2, 2, 0, 4, leave))
    exchange(q0, 0, 5, 6, 1, start, 5)
    sent.append(lambda: exchange(q0, 0, 5, 6, 1, leave, 5))
    mine = part[own_rows, :]
    for k in range(1, GROUPS):
        to_twin(k).wait_recv()
        mine = mine + part_in[k - 1]
    whole[own_rows, :] = mine
    for k in FAR_FIRST:
        from_owner(k).start()
        sent.append(lambda k=k: from_owner(k).wait_send())
    harm[:, 0] = mine[:MODES]
    for k in range(1, GROUPS):
        from_owner(k).wait_recv()

    high, low = split(whole[...])
    grad = dot(enc[0], high) + (dot(enc[0], low) + dot(enc[1], high))
    grad_out[...] = grad.reshape(MEMBERS, SLOTS, RADII)
    start_all(back_mate(grad_out, grad_in, 2))
    sent.append(lambda: all_of(grad_out, grad_in, 2).wait_send())
    grad_in[0] = grad_out[0]
    exchange(p0, 2, 2, 0, 4, arrive)
    all_of(grad_out, grad_in, 2).wait_recv()
    high, low = split(grad_in[...].reshape(ROWS, RADII) * factor[...])
    impulse = dot(pick_t[...], high) + dot(pick_t[...], low)
    impulse = impulse.reshape(PLANES, COLS, RADII)
    p0[4, 1 : PLANES + 1] = p0[4, 1 : PLANES + 1] + impulse

    pressure = p0[4, 1 : PLANES + 1].reshape(PLANES * COLS, RADII)
    pressure = pressure.T
    start_rows = jnp.where(sub == 4, pressure[:1], forward_rows)
    start_next = jnp.where(sub == 4, pressure[1:2], forward_next)
    tile[1, :8] = start_rows
    tile[1, 8:] = start_next
    exchange_tiles(1, start)
    sent.append(lambda: exchange_tiles(1, leave))
    pack_columns(p0, 2, (4,))
    exchange(p0, 2, 3, 4, 1, start)
    sent.append(lambda: exchange(p0, 2, 3, 4, 1, leave))
    exchange(q0, 0, 5, 6, 1, arrive, 5)
    exchange(p0, 2, 3, 4, 1, arrive)

    def store_p1(f, i, value):
        p1[f, i + 1] = value

    def store_out(f, i, value):
        out[f, i] = value

    planes(functools.partial(adjoint_plane, p0, 2, store_p1))
    pack_columns(p1, 3, range(5))
    exchange(p1, 3, 4, 0, 5, start)
    sent.append(lambda: exchange(p1, 3, 4, 0, 5, leave))
    exchange(p1, 3, 4, 0, 5, arrive)
    planes(functools.partial(adjoint_plane, p1, 3, store_out))
    exchange_tiles(1, arrive)
    coefs = shifted(first_rows, by_us)
    added = [
        met(radial_back, values * parity, at) for values, at in zip(opposite_values(1), met_speeds)
    ]
    theirs, theirs_follow = far[1][:8], far[1][8:]
    theirs_after = adjoint_inner(
        theirs,
        theirs_follow,
        [far_near[1, k] for k in range(4)],
        shifted(far[0][:8], by_them),
        theirs_next[5:6],
    )
    there = across_axis(start_rows, cross_back) * parity
    theirs_after = theirs_after + met(radial_back, there, met_speed_there)
    mirrored = across_axis(theirs_after, cross) * parity
    inner = adjoint_inner(added[0], None, added[1:], coefs, None)
    inner = inner + met(radial_back, mirrored, met_speeds[0])
    following = met(radial_back, added[0], speed)
    patch(out, 0, inner, following, range(5))

    for wait in sent:
        wait()


def local(
    state,
    mean_velocity,
    sound_speed,
    flux_axial,
    flux_radial,
    flux_azimuthal,
    axis_pair,
    panel_weight,
    panel_cell,
    panel_owner,
    panel_count,
):
    outside = pl.BlockSpec(memory_space=pltpu.HBM)
    vector = pl.BlockSpec(memory_space=pltpu.VMEM)

    def grid_of(fields):
        return pltpu.VMEM((fields, PLANES + 2, COLS, RADII), F32)

    fields, rows = pl.pallas_call(
        kernel,
        out_shape=(
            jax.ShapeDtypeStruct((5, PLANES, COLS, RADII), F32),
            jax.ShapeDtypeStruct((MODES, 1, RADII), F32),
        ),
        in_specs=[outside] * 11,
        out_specs=(vector, vector),
        scratch_shapes=[
            grid_of(7),
            grid_of(5),
            grid_of(5),
            grid_of(5),
            pltpu.VMEM((1, PANELS), F32),
            pltpu.VMEM((1, PANELS), I32),
            pltpu.VMEM((1, PANELS), I32),
            pltpu.SMEM((5, 5), F32),
            pltpu.SMEM((5, 5), F32),
            pltpu.SMEM((5, 5), F32),
            pltpu.SMEM((1, COLS), I32),
            pltpu.SMEM((1, 1), I32),
            pltpu.VMEM((4, 2, 7 * PLANES, RADII), F32),
            pltpu.VMEM((4, 2, 7 * PLANES, RADII), F32),
            pltpu.VMEM((2, 16, 128), F32),
            pltpu.VMEM((2, 4, 8, 128), F32),
            pltpu.VMEM((2, 16, 128), F32),
            pltpu.VMEM((2, 4, 8, 128), F32),
            pltpu.VMEM((PLANES, COLS, 128), F32),
            pltpu.VMEM((PLANES, COLS, 128), F32),
            pltpu.VMEM((ROWS, 128), BF16),
            pltpu.VMEM((128, ROWS), BF16),
            pltpu.VMEM((ROWS, 128), F32),
            pltpu.VMEM((MEMBERS, 8, LANES), F32),
            pltpu.VMEM((MEMBERS, 8, LANES), F32),
            pltpu.VMEM((2, ROWS, LANES), BF16),
            pltpu.VMEM((2, LANES, ROWS), BF16),
            pltpu.VMEM((MEMBERS, SLOTS, RADII), F32),
            pltpu.VMEM((MEMBERS, SLOTS, RADII), F32),
            pltpu.VMEM((GROUPS * WAVES, RADII), F32),
            pltpu.VMEM((GROUPS - 1, WAVES, RADII), F32),
            pltpu.VMEM((GROUPS * WAVES, RADII), F32),
            pltpu.VMEM((MEMBERS, SLOTS, RADII), F32),
            pltpu.VMEM((MEMBERS, SLOTS, RADII), F32),
            pltpu.SemaphoreType.DMA((11,)),
            pltpu.SemaphoreType.DMA((6, 4)),
            pltpu.SemaphoreType.DMA((6, 4)),
            pltpu.SemaphoreType.DMA((2, 9)),
            pltpu.SemaphoreType.DMA((2, 9)),
            pltpu.SemaphoreType.DMA((3,)),
            pltpu.SemaphoreType.DMA((3,)),
            pltpu.SemaphoreType.DMA((2, GROUPS - 1)),
            pltpu.SemaphoreType.DMA((2, GROUPS - 1)),
        ],
        compiler_params=pltpu.CompilerParams(
            collective_id=0, has_side_effects=True, vmem_limit_bytes=VMEM_GRANT
        ),
    )(
        state,
        mean_velocity,
        sound_speed,
        flux_axial,
        flux_radial,
        flux_azimuthal,
        axis_pair,
        panel_weight,
        panel_cell,
        panel_owner.reshape(1, PANELS),
        panel_count,
    )
    return fields, rows.reshape(1, 1, MODES, RADII)


def solution(mesh):
    return jax.shard_map(
        local,
        mesh=mesh,
        in_specs=(
            P(None, "slab", "sector", None),
            P("slab", "sector", None),
            P("slab", "sector", None),
            P(),
            P(),
            P(),
            P("sector", None),
            P("slab", "sector"),
            P("slab", "sector"),
            P("slab", "sector", None),
            P("slab", "sector"),
        ),
        out_specs=(P(None, "slab", "sector", None), P("slab", "sector", None, None)),
        check_vma=False,
    )
```

```python
import functools
import math

import jax
import jax.numpy as jnp
from jax import lax
from jax.experimental import pallas as pl
from jax.experimental.pallas import tpu as pltpu
from jax.sharding import PartitionSpec as P

PLANES = 16
COLS = 8
RADII = 128
PANELS = 384
ORDERS = 16
MODES = 31
SECTORS = 128
SLABS = 4
GROUPS = 8
MEMBERS = SECTORS // GROUPS
CAP = 4
SLOTS = GROUPS * CAP
ROWS = MEMBERS * SLOTS
WAVES = 32
LANES = GROUPS * WAVES
SCALE = PANELS**-0.5
TIME_STEP = 0.25
VISCOSITY = 0.05
KEEP = 1.0 - 6.0 * VISCOSITY * TIME_STEP
SPREAD = VISCOSITY * TIME_STEP
HALF = 0.5 * TIME_STEP
ORDER = (4, 3, 5, 2, 6, 1, 7, 0)
HALVES = (ORDER[: GROUPS // 2], ORDER[GROUPS // 2 :])
PART = SLOTS // 2
UNROLL = 4
VMEM_GRANT = 60 << 20
MESH = pl.DeviceIdType.MESH
F32, BF16, I32 = jnp.float32, jnp.bfloat16, jnp.int32


def split(x):
    high = x.astype(BF16)
    return high, (x - high.astype(F32)).astype(BF16)


def dot(a, b):
    return lax.dot_general(a, b, (((1,), (0,)), ((), ())), preferred_element_type=F32)


def dot_nt(a, b):
    return lax.dot_general(a, b, (((1,), (1,)), ((), ())), preferred_element_type=F32)


def iota(shape, dim):
    return lax.broadcasted_iota(I32, shape, dim)


def kernel(
    state,
    mean,
    sound,
    flux_a_in,
    flux_r_in,
    flux_t_in,
    pair_in,
    weight_in,
    cell_in,
    owner_in,
    count_in,
    out,
    harm,
    q0,
    q1,
    p0,
    p1,
    weight,
    cell,
    owner,
    flux_a,
    flux_r,
    flux_t,
    pair,
    count,
    col_send,
    col_recv,
    tile,
    near,
    far,
    far_near,
    rows0,
    turned,
    pick,
    pick_t,
    factor,
    wave_out,
    wave_in,
    enc,
    enc_t,
    lines_out,
    lines_in,
    part,
    part_in,
    whole,
    grad_out,
    grad_in,
    load_sem,
    halo_send,
    halo_recv,
    tile_send,
    tile_recv,
    many_send,
    many_recv,
    few_send,
    few_recv,
):
    sector = lax.axis_index("sector")
    slab = lax.axis_index("slab")
    group = lax.div(sector, MEMBERS)
    member = lax.rem(sector, MEMBERS)
    right = lax.rem(sector + 1, SECTORS)
    left = lax.rem(sector + SECTORS - 1, SECTORS)
    behind = lax.rem(sector + SECTORS // 2, SECTORS)

    def mate(r):
        return group * MEMBERS + lax.rem(member + r, MEMBERS)

    def twin(k):
        return lax.rem(group + k, GROUPS) * MEMBERS + member

    sent = []

    barrier = pltpu.get_barrier_semaphore()

    def greet(to_sector, to_slab):
        pl.semaphore_signal(barrier, inc=1, device_id=(to_sector, to_slab), device_id_type=MESH)

    behind_right = lax.rem(behind + 1, SECTORS)
    behind_left = lax.rem(behind + SECTORS - 1, SECTORS)
    greet(right, slab)
    greet(left, slab)
    greet(behind_right, slab)
    greet(behind_left, slab)

    @pl.when(slab > 0)
    def _():
        greet(sector, slab - 1)
        greet(behind, slab - 1)

    @pl.when(slab < SLABS - 1)
    def _():
        greet(sector, slab + 1)
        greet(behind, slab + 1)

    for k in range(1, GROUPS):
        greet(twin(k), slab)

    def greet_mate(r, carry):
        greet(mate(r), slab)
        return carry

    lax.fori_loop(1, MEMBERS, greet_mate, 0)

    loads = [
        pltpu.make_async_copy(state, q0.at[pl.ds(0, 5), pl.ds(1, PLANES)], load_sem.at[0]),
        pltpu.make_async_copy(mean, q0.at[5, pl.ds(1, PLANES)], load_sem.at[1]),
        pltpu.make_async_copy(sound, q0.at[6, pl.ds(1, PLANES)], load_sem.at[2]),
    ]
    lists = [
        pltpu.make_async_copy(weight_in, weight, load_sem.at[3]),
        pltpu.make_async_copy(cell_in, cell, load_sem.at[4]),
        pltpu.make_async_copy(owner_in, owner, load_sem.at[5]),
        pltpu.make_async_copy(flux_a_in, flux_a, load_sem.at[6]),
        pltpu.make_async_copy(flux_r_in, flux_r, load_sem.at[7]),
        pltpu.make_async_copy(flux_t_in, flux_t, load_sem.at[8]),
        pltpu.make_async_copy(pair_in, pair, load_sem.at[9]),
        pltpu.make_async_copy(count_in, count, load_sem.at[10]),
    ]
    for load in lists + loads:
        load.start()


    row = iota((128, 128), 0)
    lane = iota((128, 128), 1)
    for load in lists:
        load.wait()
    owners = owner[...]
    cells = cell[...]
    weights = weight[...]
    live = count[0, 0]
    across, down = [], []
    for q in range(3):
        wide = jnp.broadcast_to(owners[:, q * 128 : (q + 1) * 128], (128, 128)).astype(F32)
        across.append(wide)
        down.append(wide.T)
    slot_pieces, cell_pieces, weight_pieces = [], [], []
    tall = iota((ROWS, 128), 0)
    for q in range(3):
        earlier = jnp.where((down[q] == across[q]) & (row < lane), 1.0, 0.0)
        for s in range(q):
            earlier = earlier + jnp.where(down[s] == across[q], 1.0, 0.0)
        rank = jnp.sum(earlier, axis=0, keepdims=True).astype(I32)
        at = slice(q * 128, (q + 1) * 128)
        name = owners[:, at]
        relative = (name + MEMBERS - member) % MEMBERS
        ahead = (name // MEMBERS + GROUPS - group) % GROUPS
        position = jnp.zeros((1, 128), I32)
        for at_position, k in enumerate(ORDER):
            position = jnp.where(ahead == k, at_position, position)
        half = position // (GROUPS // 2)
        slot = (half * MEMBERS + relative) * PART + (position % (GROUPS // 2)) * CAP + rank
        place = iota((1, 128), 1) + q * 128
        slot = jnp.where(place < live, slot, -1)
        slot_pieces.append(jnp.where(tall == slot, 1.0, 0.0).astype(BF16))
        cell_pieces.append(jnp.where(row == cells[:, at], 1.0, 0.0).astype(BF16))
        weight_pieces.append(jnp.broadcast_to(weights[:, at], (128, 128)))
    slots = jnp.concatenate(slot_pieces, axis=1)
    spots = jnp.concatenate(cell_pieces, axis=1)
    heavy, light = split(jnp.concatenate(weight_pieces, axis=1))
    picked = dot_nt(slots, spots).astype(BF16)
    pick[...] = picked
    pick_t[...] = dot_nt(spots, slots).astype(BF16)
    factor[...] = dot_nt(slots, heavy) + dot_nt(slots, light)
    spread_row, spread_lane = iota((128, LANES), 0), iota((128, LANES), 1)
    order = spread_lane % WAVES
    turn = jnp.where(order < ORDERS, order, order - (ORDERS - 1))
    turn = turn * (sector * COLS + spread_row % COLS) + jnp.where(order < ORDERS, 0, 768)
    turn = turn % 1024
    table = jnp.cos(turn.astype(F32) * (2.0 * math.pi / 1024.0)) * SCALE
    table = jnp.where(order < MODES, table, 0.0)
    table_high, table_low = split(table)
    waves = dot(picked, table_high) + dot(picked, table_low)
    tall, tall_lane = iota((ROWS, LANES), 0), iota((ROWS, LANES), 1)
    position = (tall % PART) // CAP + (tall // (MEMBERS * PART)) * (GROUPS // 2)
    waves = jnp.where(position == tall_lane // WAVES, waves, 0.0)
    waves = waves.reshape(2, MEMBERS, PART, LANES)
    halves = (waves[0, :, :8] + waves[0, :, 8:]) + (waves[1, :, :8] + waves[1, :, 8:])
    wave_out[...] = halves + jnp.concatenate([halves[:, 4:], halves[:, :4]], axis=1)

    sub = iota((8, 128), 0)
    ray = iota((8, 128), 1)
    pairs = jnp.zeros((1, 128), I32)
    for c in range(COLS):
        pairs = jnp.where(lane[:1] % COLS == c, pair[0, c], pairs)
    parity = jnp.where((sub == 2) | (sub == 3), -1.0, 1.0)

    def crossing(columns):
        meets = (row % COLS == columns) & (row // COLS == lane // COLS)
        return jnp.where(meets, 1.0, 0.0).astype(BF16)

    cross = crossing(pairs)

    def across_axis(fields, matrix):
        high, low = split(fields)
        return dot(high, matrix) + dot(low, matrix)

    def matrix_columns(entry):
        columns = []
        for g in range(5):
            column = jnp.zeros((8, 128), F32)
            for f in range(5):
                column = jnp.where(sub == f, entry(f, g), column)
            columns.append(column)
        return columns

    axial = matrix_columns(lambda f, g: flux_a[f, g] * HALF)
    radial = matrix_columns(lambda f, g: flux_r[f, g] * HALF)
    angular = matrix_columns(lambda f, g: flux_t[f, g] * (2.0 * HALF))
    axial_t = matrix_columns(lambda f, g: flux_a[g, f] * HALF)
    radial_t = matrix_columns(lambda f, g: flux_r[g, f] * HALF)
    angular_t = matrix_columns(lambda f, g: flux_t[g, f] * (2.0 * HALF))
    radial_back = [-column for column in radial_t]

    def met(columns, mirrored, speed):
        return jnp.where(sub < 5, mirrored * SPREAD + mix(columns, mirrored) * speed, 0.0)

    @pl.when(slab == 0)
    def _():
        for ref in (near, far_near):
            ref[:, 3] = jnp.zeros((2, 8, 128), F32)
        for ref in (q0, q1, p0, p1):
            ref[:, 0] = jnp.zeros_like(ref[:, 0])

    @pl.when(slab == SLABS - 1)
    def _():
        for ref in (near, far_near):
            ref[:, 2] = jnp.zeros((2, 8, 128), F32)
        for ref in (q0, q1, p0, p1):
            ref[:, PLANES + 1] = jnp.zeros_like(ref[:, PLANES + 1])

    def pack_columns(ref, level, fields):
        flat = ref.reshape(ref.shape[0] * (PLANES + 2) * COLS, RADII)
        for f in fields:
            for side, c in ((0, 0), (1, COLS - 1)):
                begin = (f * (PLANES + 2) + 1) * COLS + c
                col_send[level, side, f * PLANES : (f + 1) * PLANES] = flat[
                    pl.ds(begin, PLANES, stride=COLS), :
                ]

    def columns_of(ref, level, phase, first, number):
        rows = pl.ds(first * PLANES, number * PLANES)
        copies = []
        for side, to in ((0, left), (1, right)):
            copies.append(
                pltpu.make_async_remote_copy(
                    src_ref=col_send.at[level, side, rows],
                    dst_ref=col_recv.at[level, side, rows],
                    send_sem=halo_send.at[phase, side],
                    recv_sem=halo_recv.at[phase, side],
                    device_id=(to, slab),
                    device_id_type=MESH,
                )
            )
        return copies

    def planes_of(ref, phase, first, number):
        fields = pl.ds(first, number)
        up = pltpu.make_async_remote_copy(
            src_ref=ref.at[fields, PLANES],
            dst_ref=ref.at[fields, 0],
            send_sem=halo_send.at[phase, 2],
            recv_sem=halo_recv.at[phase, 2],
            device_id=(sector, lax.rem(slab + 1, SLABS)),
            device_id_type=MESH,
        )
        downward = pltpu.make_async_remote_copy(
            src_ref=ref.at[fields, 1],
            dst_ref=ref.at[fields, PLANES + 1],
            send_sem=halo_send.at[phase, 3],
            recv_sem=halo_recv.at[phase, 3],
            device_id=(sector, lax.rem(slab + SLABS - 1, SLABS)),
            device_id_type=MESH,
        )
        return up, downward

    def tile_copy(which, place, source, target, to):
        return pltpu.make_async_remote_copy(
            src_ref=source,
            dst_ref=target,
            send_sem=tile_send.at[which, place],
            recv_sem=tile_recv.at[which, place],
            device_id=to,
            device_id_type=MESH,
        )

    slab_down, slab_up = lax.rem(slab + SLABS - 1, SLABS), lax.rem(slab + 1, SLABS)

    def exchange_tiles(which, act):
        inner = tile.at[which, pl.ds(0, 8)]
        act(tile_copy(which, 8, tile.at[which], far.at[which], (behind, slab)), "both")
        act(tile_copy(which, 4, inner, far_near.at[which, 0], (behind_left, slab)), "both")
        act(tile_copy(which, 5, inner, far_near.at[which, 1], (behind_right, slab)), "both")
        act(tile_copy(which, 0, inner, near.at[which, 0], (left, slab)), "both")
        act(tile_copy(which, 1, inner, near.at[which, 1], (right, slab)), "both")
        downward = (
            tile_copy(which, 6, inner, far_near.at[which, 2], (behind, slab_down)),
            tile_copy(which, 2, inner, near.at[which, 2], (sector, slab_down)),
        )
        upward = (
            tile_copy(which, 7, inner, far_near.at[which, 3], (behind, slab_up)),
            tile_copy(which, 3, inner, near.at[which, 3], (sector, slab_up)),
        )

        @pl.when(slab > 0)
        def _():
            for copy in downward:
                act(copy, "send")
            for copy in upward:
                act(copy, "recv")

        @pl.when(slab < SLABS - 1)
        def _():
            for copy in upward:
                act(copy, "send")
            for copy in downward:
                act(copy, "recv")

    def shifted(rows, beside):
        from_right, from_left, from_up, from_down = beside
        t_minus = jnp.where(ray % COLS == 0, pltpu.roll(from_left, 121, 1), pltpu.roll(rows, 1, 1))
        t_plus = jnp.where(ray % COLS == 7, pltpu.roll(from_right, 7, 1), pltpu.roll(rows, 127, 1))
        x_minus = jnp.where(ray < COLS, pltpu.roll(from_down, 8, 1), pltpu.roll(rows, 8, 1))
        x_plus = jnp.where(ray >= 120, pltpu.roll(from_up, 120, 1), pltpu.roll(rows, 120, 1))
        return x_minus, x_plus, t_minus, t_plus

    def mix(columns, fields):
        total = columns[0] * fields[:1]
        for g in range(1, 5):
            total = total + columns[g] * fields[g : g + 1]
        return total

    def forward_inner(rows, following, beside, speed, flow):
        x_minus, x_plus, t_minus, t_plus = shifted(rows, beside)
        dx = x_plus - x_minus
        mixed = mix(axial, dx) + mix(angular, t_plus - t_minus)
        around = x_plus + x_minus + t_plus + t_minus
        if following is not None:
            mixed, around = mixed + mix(radial, following), around + following
        result = rows * KEEP + around * SPREAD - (flow * HALF) * dx - speed * mixed
        return jnp.where(sub < 5, result, 0.0)

    def adjoint_inner(rows, following, beside, coefs, speed_next):
        x_minus, x_plus, t_minus, t_plus = shifted(rows, beside)
        k_x_minus, k_x_plus, k_t_minus, k_t_plus = coefs
        result = mix(axial_t, x_plus * k_x_plus[5:6] - x_minus * k_x_minus[5:6])
        result = result + mix(angular_t, t_plus * k_t_plus[5:6] - t_minus * k_t_minus[5:6])
        result = result + (x_plus * k_x_plus[6:7] - x_minus * k_x_minus[6:7]) * HALF
        around = x_plus + x_minus + t_plus + t_minus
        if following is not None:
            result, around = result + mix(radial_t, following * speed_next), around + following
        result = result + rows * KEEP + around * SPREAD
        return jnp.where(sub < 5, result, 0.0)

    def stack(which):
        return jnp.concatenate([far[which][:8], far_near[which, 2], far_near[which, 3]], axis=0)

    def exchange(ref, level, phase, first, number, act, planes_first=None):
        for copy in columns_of(ref, level, phase, first, number):
            act(copy, "both")
        if planes_first is None:
            up, downward = planes_of(ref, phase, first, number)
        else:
            up, downward = planes_of(ref, phase, planes_first, first + number - planes_first)

        @pl.when(slab < SLABS - 1)
        def _():
            act(up, "send")
            act(downward, "recv")

        @pl.when(slab > 0)
        def _():
            act(downward, "send")
            act(up, "recv")

    def start(copy, part_of):
        if part_of != "recv":
            copy.start()

    def arrive(copy, part_of):
        if part_of != "send":
            copy.wait_recv()

    def leave(copy, part_of):
        if part_of != "recv":
            copy.wait_send()

    wanted = jnp.where(row[:16] < 8, 2 * row[:16], 2 * (row[:16] - 8) + 1)
    chosen = jnp.where(lane[:16] == wanted, 1.0, 0.0).astype(BF16)

    def pack_inner(i, fields):
        here = jnp.zeros((8, 128), F32)
        for f, value in enumerate(fields):
            here = jnp.where(ray // 2 == f, value if f == 0 else pltpu.roll(value, 2 * f, 1), here)
        rows0[i] = here

    def packed():
        high, low = split(rows0[...].reshape(128, 128))
        both = dot_nt(chosen, high) + dot_nt(chosen, low)
        return both[:8], both[8:]

    def patch(ref, skip, inner, following, fields):
        wide = jnp.concatenate([inner, following, jnp.zeros((112, 128), F32)], axis=0)
        turned[...] = wide.T.reshape(PLANES, COLS, 128)

        def step(i, carry):
            here = turned[i]
            for f in fields:
                zero = here if f == 0 else pltpu.roll(here, 128 - f, 1)
                one = pltpu.roll(here, 121 - f, 1)
                ref[f, i + skip] += jnp.where(ray == 0, zero, jnp.where(ray == 1, one, 0.0))
            return carry

        lax.fori_loop(0, PLANES, step, 0, unroll=4)

    def beside(value, level, f, i):
        before = jnp.broadcast_to(col_recv[level, 1, pl.ds(f * PLANES + i, 1), :], (8, 128))
        after = jnp.broadcast_to(col_recv[level, 0, pl.ds(f * PLANES + i, 1), :], (8, 128))
        t_minus = jnp.where(sub == 0, before, pltpu.roll(value, 1, 0))
        t_plus = jnp.where(sub == COLS - 1, after, pltpu.roll(value, COLS - 1, 0))
        r_minus = jnp.where(ray == 0, 0.0, pltpu.roll(value, 1, 1))
        r_plus = jnp.where(ray == RADII - 1, 0.0, pltpu.roll(value, RADII - 1, 1))
        return t_minus, t_plus, r_minus, r_plus

    inverse = 1.0 / (ray.astype(F32) + 0.5)

    def forward_plane(src, level, dst, i):
        u, c = q0[5, i + 1] * HALF, q0[6, i + 1] * HALF
        values, dx, dr, dt, around = [], [], [], [], []
        for f in range(5):
            value, x_minus, x_plus = src[f, i + 1], src[f, i], src[f, i + 2]
            t_minus, t_plus, r_minus, r_plus = beside(value, level, f, i)
            values.append(value)
            dx.append(x_plus - x_minus)
            dr.append(r_plus - r_minus)
            dt.append((t_plus - t_minus) * inverse)
            around.append((x_plus + x_minus) + (t_plus + t_minus) + (r_plus + r_minus))
        for f in range(5):
            mixed = flux_a[f, 0] * dx[0] + flux_r[f, 0] * dr[0] + flux_t[f, 0] * dt[0]
            for g in range(1, 5):
                mixed = mixed + flux_a[f, g] * dx[g] + flux_r[f, g] * dr[g] + flux_t[f, g] * dt[g]
            dst[f, i + 1] = values[f] * KEEP + around[f] * SPREAD - u * dx[f] - c * mixed

    def adjoint_plane(src, level, store, i):
        u_minus, u_plus = q0[5, i] * HALF, q0[5, i + 2] * HALF
        c = q0[6, i + 1] * HALF
        c_minus, c_plus = q0[6, i] * HALF, q0[6, i + 2] * HALF
        before = jnp.broadcast_to(col_recv[0, 1, pl.ds(6 * PLANES + i, 1), :], (8, 128)) * HALF
        after = jnp.broadcast_to(col_recv[0, 0, pl.ds(6 * PLANES + i, 1), :], (8, 128)) * HALF
        c_t_minus = jnp.where(sub == 0, before, pltpu.roll(c, 1, 0)) * inverse
        c_t_plus = jnp.where(sub == COLS - 1, after, pltpu.roll(c, COLS - 1, 0)) * inverse
        c_r_minus = pltpu.roll(c, 1, 1)
        c_r_plus = pltpu.roll(c, RADII - 1, 1)
        carried, dx, dr, dt = [], [], [], []
        for f in range(5):
            value, x_minus, x_plus = src[f, i + 1], src[f, i], src[f, i + 2]
            t_minus, t_plus, r_minus, r_plus = beside(value, level, f, i)
            dx.append(c_plus * x_plus - c_minus * x_minus)
            dr.append(c_r_plus * r_plus - c_r_minus * r_minus)
            dt.append(c_t_plus * t_plus - c_t_minus * t_minus)
            around = (x_plus + x_minus) + (t_plus + t_minus) + (r_plus + r_minus)
            carried.append(
                value * KEEP + around * SPREAD + (u_plus * x_plus - u_minus * x_minus)
            )
        for f in range(5):
            result = carried[f]
            for g in range(5):
                result = result + flux_a[g, f] * dx[g] + flux_r[g, f] * dr[g] + flux_t[g, f] * dt[g]
            store(f, i, result)

    def planes(body):
        def step(i, carry):
            body(i)
            return carry

        lax.fori_loop(0, PLANES, step, 0, unroll=UNROLL)

    for load in loads:
        load.wait()
    pack_columns(q0, 0, (0, 1, 2, 3, 4, 6))
    planes(lambda i: pack_inner(i, [q0[f, i + 1] for f in (0, 1, 2, 3, 4, 6, 5)]))
    first_rows, first_next = packed()
    first_rows = jnp.where(sub == 7, pairs.astype(F32), first_rows)
    tile[0, :8] = first_rows
    tile[0, 8:] = first_next
    pl.semaphore_wait(
        barrier,
        MEMBERS - 1 + GROUPS - 1 + 4 + jnp.where(slab > 0, 2, 0) + jnp.where(slab < SLABS - 1, 2, 0),
    )
    exchange_tiles(0, start)
    sent.append(lambda: exchange_tiles(0, leave))
    exchange(q0, 0, 0, 0, 5, start)
    sent.append(lambda: exchange(q0, 0, 0, 0, 5, leave))

    def mate_copy(source, target, which, r, to):
        return pltpu.make_async_remote_copy(
            src_ref=source.at[r],
            dst_ref=target.at[r],
            send_sem=many_send.at[which],
            recv_sem=many_recv.at[which],
            device_id=(to, slab),
            device_id_type=MESH,
        )

    def to_mate(source, target, which):
        return lambda r: mate_copy(source, target, which, r, mate(r))

    def back_mate(source, target, which):
        return lambda r: mate_copy(source, target, which, r, mate(MEMBERS - r))

    def start_all(copy_of):
        def step(r, carry):
            copy_of(r).start()
            return carry

        lax.fori_loop(4, MEMBERS, step, 0)
        lax.fori_loop(1, 4, step, 0)

    def all_of(source, target, which):
        rest = pl.ds(1, MEMBERS - 1)
        return pltpu.make_async_remote_copy(
            src_ref=source.at[rest],
            dst_ref=target.at[rest],
            send_sem=many_send.at[which],
            recv_sem=many_recv.at[which],
            device_id=(right, slab),
            device_id_type=MESH,
        )

    wave_in[0] = wave_out[0]
    exchange(q0, 0, 0, 0, 5, arrive)
    planes(functools.partial(forward_plane, q0, 0, q1))
    pack_columns(q1, 1, range(5))
    exchange(q1, 1, 1, 0, 5, start)
    sent.append(lambda: exchange(q1, 1, 1, 0, 5, leave))
    start_all(to_mate(wave_out, wave_in, 0))
    sent.append(lambda: all_of(wave_out, wave_in, 0).wait_send())
    exchange(q1, 1, 1, 0, 5, arrive)
    planes(functools.partial(forward_plane, q1, 1, p0))
    exchange_tiles(0, arrive)
    theirs, theirs_next = far[0][:8], far[0][8:]
    by_us = [near[0, k] for k in range(4)]
    by_them = [far_near[0, k] for k in range(4)]
    cross_right = crossing(by_us[0][7:8].astype(I32))
    cross_left = crossing(by_us[1][7:8].astype(I32))
    cross_back = crossing(theirs[7:8].astype(I32))

    def opposite_values(which):
        three = across_axis(stack(which), cross)
        return [
            three[:8],
            across_axis(far_near[which, 0], cross_right),
            across_axis(far_near[which, 1], cross_left),
            three[8:16],
            three[16:],
        ]

    met_values = opposite_values(0)
    met_speeds = [values[5:6] for values in met_values]
    speed, speed_next, flow = first_rows[5:6], first_next[5:6], first_rows[6:7]
    speeds = [speed] + [values[5:6] for values in by_us]
    added = [met(radial, values * parity, at) for values, at in zip(met_values, speeds)]
    there = across_axis(first_rows, cross_back)
    met_speed_there = there[5:6]
    theirs_after = forward_inner(theirs, theirs_next, by_them, theirs[5:6], theirs[6:7])
    theirs_after = theirs_after + met(radial, there * parity, theirs[5:6])
    mirrored = across_axis(theirs_after, cross) * parity
    inner = forward_inner(added[0], None, added[1:], speed, flow) + met(radial, mirrored, speed)
    following = met(radial, added[0], speed_next)
    patch(p0, 1, inner, following, (4,))

    pressure = p0[4, 1 : PLANES + 1].reshape(PLANES * COLS, RADII)
    high, low = split(pressure)
    lines = (dot(pick[...], high) + dot(pick[...], low)) * factor[...]
    lines_out[...] = lines.reshape(2, MEMBERS, PART, RADII)
    for h in range(2):
        start_all(to_mate(lines_out.at[h], lines_in.at[h], 1 + h))
        sent.append(lambda h=h: all_of(lines_out.at[h], lines_in.at[h], 1 + h).wait_send())
        lines_in[h, 0] = lines_out[h, 0]
    patch(p0, 1, inner, following, range(4))
    planes(lambda i: pack_inner(i, [p0[f, i + 1] for f in range(4)]))
    forward_rows, forward_next = packed()
    pack_columns(p0, 2, range(4))
    all_of(wave_out, wave_in, 0).wait_recv()
    given = wave_in[...]
    sub3, ray3 = iota((MEMBERS, 8, 128), 1), iota((MEMBERS, 8, 128), 2)
    for h in range(2):
        some = given[:, :, h * 128 : (h + 1) * 128]
        first = jnp.where(sub3 // CAP == ray3 // WAVES, some, 0.0)
        second = jnp.where(sub3 // CAP + 2 == ray3 // WAVES, some, 0.0)
        encoder = jnp.concatenate([first, second], axis=1).reshape(MEMBERS * PART, 128)
        enc[h, 0], enc[h, 1] = split(encoder)
        enc_t[h, 0], enc_t[h, 1] = split(encoder.T)

    def rows_of(k):
        return pl.ds(ORDER.index(k % GROUPS) * WAVES, WAVES)

    def to_twin(k):
        return pltpu.make_async_remote_copy(
            src_ref=part.at[rows_of(k)],
            dst_ref=part_in.at[k - 1],
            send_sem=few_send.at[0, k - 1],
            recv_sem=few_recv.at[0, k - 1],
            device_id=(twin(k), slab),
            device_id_type=MESH,
        )

    def from_owner(k):
        return pltpu.make_async_remote_copy(
            src_ref=whole.at[rows_of(0)],
            dst_ref=whole.at[rows_of(GROUPS - k)],
            send_sem=few_send.at[1, k - 1],
            recv_sem=few_recv.at[1, k - 1],
            device_id=(twin(k), slab),
            device_id_type=MESH,
        )

    for h in range(2):
        all_of(lines_out.at[h], lines_in.at[h], 1 + h).wait_recv()
        high, low = split(lines_in[h].reshape(MEMBERS * PART, RADII))
        part[h * 128 : (h + 1) * 128] = dot(enc_t[h, 0], high) + (
            dot(enc_t[h, 0], low) + dot(enc_t[h, 1], high)
        )
        for k in HALVES[h]:
            if k > 0:
                to_twin(k).start()
                sent.append(lambda k=k: to_twin(k).wait_send())
    exchange(p0, 2, 2, 0, 4, start)
    sent.append(lambda: exchange(p0, 2, 2, 0, 4, leave))
    exchange(q0, 0, 5, 6, 1, start, 5)
    sent.append(lambda: exchange(q0, 0, 5, 6, 1, leave, 5))
    mine = part[rows_of(0), :]
    for k in ORDER[::-1][1:]:
        to_twin(k).wait_recv()
        mine = mine + part_in[k - 1]
    whole[rows_of(0), :] = mine
    for k in ORDER[:-1]:
        from_owner(k).start()
        sent.append(lambda k=k: from_owner(k).wait_send())
    harm[:, 0] = mine[:MODES]

    for h in (1, 0):
        for k in HALVES[h]:
            if k > 0:
                from_owner(GROUPS - k).wait_recv()
        high, low = split(whole[h * 128 : (h + 1) * 128])
        grad = dot(enc[h, 0], high) + (dot(enc[h, 0], low) + dot(enc[h, 1], high))
        grad_out[h] = grad.reshape(MEMBERS, PART, RADII)
        start_all(back_mate(grad_out.at[h], grad_in.at[h], 3 + h))
        sent.append(lambda h=h: all_of(grad_out.at[h], grad_in.at[h], 3 + h).wait_send())
        grad_in[h, 0] = grad_out[h, 0]
    exchange(p0, 2, 2, 0, 4, arrive)
    for h in (1, 0):
        all_of(grad_out.at[h], grad_in.at[h], 3 + h).wait_recv()
    high, low = split(grad_in[...].reshape(ROWS, RADII) * factor[...])
    impulse = dot(pick_t[...], high) + dot(pick_t[...], low)
    impulse = impulse.reshape(PLANES, COLS, RADII)
    p0[4, 1 : PLANES + 1] = p0[4, 1 : PLANES + 1] + impulse

    pressure = p0[4, 1 : PLANES + 1].reshape(PLANES * COLS, RADII)
    pressure = pressure.T
    start_rows = jnp.where(sub == 4, pressure[:1], forward_rows)
    start_next = jnp.where(sub == 4, pressure[1:2], forward_next)
    tile[1, :8] = start_rows
    tile[1, 8:] = start_next
    exchange_tiles(1, start)
    sent.append(lambda: exchange_tiles(1, leave))
    pack_columns(p0, 2, (4,))
    exchange(p0, 2, 3, 4, 1, start)
    sent.append(lambda: exchange(p0, 2, 3, 4, 1, leave))
    exchange(q0, 0, 5, 6, 1, arrive, 5)
    exchange(p0, 2, 3, 4, 1, arrive)

    def store_p1(f, i, value):
        p1[f, i + 1] = value

    def store_out(f, i, value):
        out[f, i] = value

    planes(functools.partial(adjoint_plane, p0, 2, store_p1))
    pack_columns(p1, 3, range(5))
    exchange(p1, 3, 4, 0, 5, start)
    sent.append(lambda: exchange(p1, 3, 4, 0, 5, leave))
    exchange(p1, 3, 4, 0, 5, arrive)
    planes(functools.partial(adjoint_plane, p1, 3, store_out))
    exchange_tiles(1, arrive)
    coefs = shifted(first_rows, by_us)
    added = [
        met(radial_back, values * parity, at) for values, at in zip(opposite_values(1), met_speeds)
    ]
    theirs, theirs_follow = far[1][:8], far[1][8:]
    theirs_after = adjoint_inner(
        theirs,
        theirs_follow,
        [far_near[1, k] for k in range(4)],
        shifted(far[0][:8], by_them),
        theirs_next[5:6],
    )
    there = across_axis(start_rows, cross_back) * parity
    theirs_after = theirs_after + met(radial_back, there, met_speed_there)
    mirrored = across_axis(theirs_after, cross) * parity
    inner = adjoint_inner(added[0], None, added[1:], coefs, None)
    inner = inner + met(radial_back, mirrored, met_speeds[0])
    following = met(radial_back, added[0], speed)
    patch(out, 0, inner, following, range(5))

    for wait in sent:
        wait()


def local(
    state,
    mean_velocity,
    sound_speed,
    flux_axial,
    flux_radial,
    flux_azimuthal,
    axis_pair,
    panel_weight,
    panel_cell,
    panel_owner,
    panel_count,
):
    outside = pl.BlockSpec(memory_space=pltpu.HBM)
    vector = pl.BlockSpec(memory_space=pltpu.VMEM)

    def grid_of(fields):
        return pltpu.VMEM((fields, PLANES + 2, COLS, RADII), F32)

    fields, rows = pl.pallas_call(
        kernel,
        out_shape=(
            jax.ShapeDtypeStruct((5, PLANES, COLS, RADII), F32),
            jax.ShapeDtypeStruct((MODES, 1, RADII), F32),
        ),
        in_specs=[outside] * 11,
        out_specs=(vector, vector),
        scratch_shapes=[
            grid_of(7),
            grid_of(5),
            grid_of(5),
            grid_of(5),
            pltpu.VMEM((1, PANELS), F32),
            pltpu.VMEM((1, PANELS), I32),
            pltpu.VMEM((1, PANELS), I32),
            pltpu.SMEM((5, 5), F32),
            pltpu.SMEM((5, 5), F32),
            pltpu.SMEM((5, 5), F32),
            pltpu.SMEM((1, COLS), I32),
            pltpu.SMEM((1, 1), I32),
            pltpu.VMEM((4, 2, 7 * PLANES, RADII), F32),
            pltpu.VMEM((4, 2, 7 * PLANES, RADII), F32),
            pltpu.VMEM((2, 16, 128), F32),
            pltpu.VMEM((2, 4, 8, 128), F32),
            pltpu.VMEM((2, 16, 128), F32),
            pltpu.VMEM((2, 4, 8, 128), F32),
            pltpu.VMEM((PLANES, COLS, 128), F32),
            pltpu.VMEM((PLANES, COLS, 128), F32),
            pltpu.VMEM((ROWS, 128), BF16),
            pltpu.VMEM((128, ROWS), BF16),
            pltpu.VMEM((ROWS, 128), F32),
            pltpu.VMEM((MEMBERS, 8, LANES), F32),
            pltpu.VMEM((MEMBERS, 8, LANES), F32),
            pltpu.VMEM((2, 2, MEMBERS * PART, 128), BF16),
            pltpu.VMEM((2, 2, 128, MEMBERS * PART), BF16),
            pltpu.VMEM((2, MEMBERS, PART, RADII), F32),
            pltpu.VMEM((2, MEMBERS, PART, RADII), F32),
            pltpu.VMEM((GROUPS * WAVES, RADII), F32),
            pltpu.VMEM((GROUPS - 1, WAVES, RADII), F32),
            pltpu.VMEM((GROUPS * WAVES, RADII), F32),
            pltpu.VMEM((2, MEMBERS, PART, RADII), F32),
            pltpu.VMEM((2, MEMBERS, PART, RADII), F32),
            pltpu.SemaphoreType.DMA((11,)),
            pltpu.SemaphoreType.DMA((6, 4)),
            pltpu.SemaphoreType.DMA((6, 4)),
            pltpu.SemaphoreType.DMA((2, 9)),
            pltpu.SemaphoreType.DMA((2, 9)),
            pltpu.SemaphoreType.DMA((5,)),
            pltpu.SemaphoreType.DMA((5,)),
            pltpu.SemaphoreType.DMA((2, GROUPS - 1)),
            pltpu.SemaphoreType.DMA((2, GROUPS - 1)),
        ],
        compiler_params=pltpu.CompilerParams(
            collective_id=0, has_side_effects=True, vmem_limit_bytes=VMEM_GRANT
        ),
    )(
        state,
        mean_velocity,
        sound_speed,
        flux_axial,
        flux_radial,
        flux_azimuthal,
        axis_pair,
        panel_weight,
        panel_cell,
        panel_owner.reshape(1, PANELS),
        panel_count,
    )
    return fields, rows.reshape(1, 1, MODES, RADII)


def solution(mesh):
    return jax.shard_map(
        local,
        mesh=mesh,
        in_specs=(
            P(None, "slab", "sector", None),
            P("slab", "sector", None),
            P("slab", "sector", None),
            P(),
            P(),
            P(),
            P("sector", None),
            P("slab", "sector"),
            P("slab", "sector"),
            P("slab", "sector", None),
            P("slab", "sector"),
        ),
        out_specs=(P(None, "slab", "sector", None), P("slab", "sector", None, None)),
        check_vma=False,
    )
```

```python
import functools
import math

import jax
import jax.numpy as jnp
from jax import lax
from jax.experimental import pallas as pl
from jax.experimental.pallas import tpu as pltpu
from jax.sharding import PartitionSpec as P

PLANES = 16
COLS = 8
RADII = 128
PANELS = 384
ORDERS = 16
MODES = 31
SECTORS = 128
SLABS = 4
GROUPS = 8
MEMBERS = SECTORS // GROUPS
CAP = 4
SLOTS = GROUPS * CAP
ROWS = MEMBERS * SLOTS
WAVES = 32
LANES = GROUPS * WAVES
SCALE = PANELS**-0.5
TIME_STEP = 0.25
VISCOSITY = 0.05
KEEP = 1.0 - 6.0 * VISCOSITY * TIME_STEP
SPREAD = VISCOSITY * TIME_STEP
HALF = 0.5 * TIME_STEP
ORDER = (4, 3, 5, 2, 6, 1, 7, 0)
HALVES = (ORDER[: GROUPS // 2], ORDER[GROUPS // 2 :])
PART = SLOTS // 2
UNROLL = 4
VMEM_GRANT = 32 << 20
MESH = pl.DeviceIdType.MESH
F32, BF16, I32 = jnp.float32, jnp.bfloat16, jnp.int32


def split(x):
    high = x.astype(BF16)
    return high, (x - high.astype(F32)).astype(BF16)


def dot(a, b):
    return lax.dot_general(a, b, (((1,), (0,)), ((), ())), preferred_element_type=F32)


def dot_nt(a, b):
    return lax.dot_general(a, b, (((1,), (1,)), ((), ())), preferred_element_type=F32)


def iota(shape, dim):
    return lax.broadcasted_iota(I32, shape, dim)


def kernel(
    state,
    mean,
    sound,
    flux_a_in,
    flux_r_in,
    flux_t_in,
    pair_in,
    weight_in,
    cell_in,
    owner_in,
    count_in,
    out,
    harm,
    q0,
    q1,
    p0,
    p1,
    weight,
    cell,
    owner,
    flux_a,
    flux_r,
    flux_t,
    pair,
    count,
    col_send,
    col_recv,
    tile,
    near,
    far,
    far_near,
    rows0,
    turned,
    pick,
    pick_t,
    factor,
    wave_out,
    wave_in,
    enc,
    enc_t,
    lines_out,
    lines_in,
    part,
    part_in,
    whole,
    grad_out,
    grad_in,
    load_sem,
    halo_send,
    halo_recv,
    tile_send,
    tile_recv,
    many_send,
    many_recv,
    few_send,
    few_recv,
):
    sector = lax.axis_index("sector")
    slab = lax.axis_index("slab")
    group = lax.div(sector, MEMBERS)
    member = lax.rem(sector, MEMBERS)
    right = lax.rem(sector + 1, SECTORS)
    left = lax.rem(sector + SECTORS - 1, SECTORS)
    behind = lax.rem(sector + SECTORS // 2, SECTORS)

    def mate(r):
        return group * MEMBERS + lax.rem(member + r, MEMBERS)

    def twin(k):
        return lax.rem(group + k, GROUPS) * MEMBERS + member

    sent = []

    barrier = pltpu.get_barrier_semaphore()

    def greet(to_sector, to_slab):
        pl.semaphore_signal(barrier, inc=1, device_id=(to_sector, to_slab), device_id_type=MESH)

    behind_right = lax.rem(behind + 1, SECTORS)
    behind_left = lax.rem(behind + SECTORS - 1, SECTORS)
    greet(right, slab)
    greet(left, slab)
    greet(behind_right, slab)
    greet(behind_left, slab)

    @pl.when(slab > 0)
    def _():
        greet(sector, slab - 1)
        greet(behind, slab - 1)

    @pl.when(slab < SLABS - 1)
    def _():
        greet(sector, slab + 1)
        greet(behind, slab + 1)

    for k in range(1, GROUPS):
        greet(twin(k), slab)

    def greet_mate(r, carry):
        greet(mate(r), slab)
        return carry

    lax.fori_loop(1, MEMBERS, greet_mate, 0)

    loads = [
        pltpu.make_async_copy(state, q0.at[pl.ds(0, 5), pl.ds(1, PLANES)], load_sem.at[0]),
        pltpu.make_async_copy(mean, q0.at[5, pl.ds(1, PLANES)], load_sem.at[1]),
        pltpu.make_async_copy(sound, q0.at[6, pl.ds(1, PLANES)], load_sem.at[2]),
    ]
    lists = [
        pltpu.make_async_copy(weight_in, weight, load_sem.at[3]),
        pltpu.make_async_copy(cell_in, cell, load_sem.at[4]),
        pltpu.make_async_copy(owner_in, owner, load_sem.at[5]),
        pltpu.make_async_copy(flux_a_in, flux_a, load_sem.at[6]),
        pltpu.make_async_copy(flux_r_in, flux_r, load_sem.at[7]),
        pltpu.make_async_copy(flux_t_in, flux_t, load_sem.at[8]),
        pltpu.make_async_copy(pair_in, pair, load_sem.at[9]),
        pltpu.make_async_copy(count_in, count, load_sem.at[10]),
    ]
    for load in lists + loads:
        load.start()


    row = iota((128, 128), 0)
    lane = iota((128, 128), 1)
    for load in lists:
        load.wait()
    owners = owner[...]
    cells = cell[...]
    weights = weight[...]
    live = count[0, 0]
    across, down = [], []
    for q in range(3):
        wide = jnp.broadcast_to(owners[:, q * 128 : (q + 1) * 128], (128, 128)).astype(F32)
        across.append(wide)
        down.append(wide.T)
    slot_pieces, cell_pieces, weight_pieces = [], [], []
    tall = iota((ROWS, 128), 0)
    for q in range(3):
        earlier = jnp.where((down[q] == across[q]) & (row < lane), 1.0, 0.0)
        for s in range(q):
            earlier = earlier + jnp.where(down[s] == across[q], 1.0, 0.0)
        rank = jnp.sum(earlier, axis=0, keepdims=True).astype(I32)
        at = slice(q * 128, (q + 1) * 128)
        name = owners[:, at]
        relative = (name + MEMBERS - member) % MEMBERS
        ahead = (name // MEMBERS + GROUPS - group) % GROUPS
        position = jnp.zeros((1, 128), I32)
        for at_position, k in enumerate(ORDER):
            position = jnp.where(ahead == k, at_position, position)
        half = position // (GROUPS // 2)
        slot = (half * MEMBERS + relative) * PART + (position % (GROUPS // 2)) * CAP + rank
        place = iota((1, 128), 1) + q * 128
        slot = jnp.where(place < live, slot, -1)
        slot_pieces.append(jnp.where(tall == slot, 1.0, 0.0).astype(BF16))
        cell_pieces.append(jnp.where(row == cells[:, at], 1.0, 0.0).astype(BF16))
        weight_pieces.append(jnp.broadcast_to(weights[:, at], (128, 128)))
    slots = jnp.concatenate(slot_pieces, axis=1)
    spots = jnp.concatenate(cell_pieces, axis=1)
    heavy, light = split(jnp.concatenate(weight_pieces, axis=1))
    picked = dot_nt(slots, spots).astype(BF16)
    pick[...] = picked
    pick_t[...] = dot_nt(spots, slots).astype(BF16)
    factor[...] = dot_nt(slots, heavy) + dot_nt(slots, light)
    spread_row, spread_lane = iota((128, LANES), 0), iota((128, LANES), 1)
    order = spread_lane % WAVES
    turn = jnp.where(order < ORDERS, order, order - (ORDERS - 1))
    turn = turn * (sector * COLS + spread_row % COLS) + jnp.where(order < ORDERS, 0, 768)
    turn = turn % 1024
    table = jnp.cos(turn.astype(F32) * (2.0 * math.pi / 1024.0)) * SCALE
    table = jnp.where(order < MODES, table, 0.0)
    table_high, table_low = split(table)
    waves = dot(picked, table_high) + dot(picked, table_low)
    tall, tall_lane = iota((ROWS, LANES), 0), iota((ROWS, LANES), 1)
    position = (tall % PART) // CAP + (tall // (MEMBERS * PART)) * (GROUPS // 2)
    waves = jnp.where(position == tall_lane // WAVES, waves, 0.0)
    waves = waves.reshape(2, MEMBERS, PART, LANES)
    halves = (waves[0, :, :8] + waves[0, :, 8:]) + (waves[1, :, :8] + waves[1, :, 8:])
    wave_out[...] = halves + jnp.concatenate([halves[:, 4:], halves[:, :4]], axis=1)

    sub = iota((8, 128), 0)
    ray = iota((8, 128), 1)
    pairs = jnp.zeros((1, 128), I32)
    for c in range(COLS):
        pairs = jnp.where(lane[:1] % COLS == c, pair[0, c], pairs)
    parity = jnp.where((sub == 2) | (sub == 3), -1.0, 1.0)

    def crossing(columns):
        meets = (row % COLS == columns) & (row // COLS == lane // COLS)
        return jnp.where(meets, 1.0, 0.0).astype(BF16)

    cross = crossing(pairs)

    def across_axis(fields, matrix):
        high, low = split(fields)
        return dot(high, matrix) + dot(low, matrix)

    def matrix_columns(entry):
        columns = []
        for g in range(5):
            column = jnp.zeros((8, 128), F32)
            for f in range(5):
                column = jnp.where(sub == f, entry(f, g), column)
            columns.append(column)
        return columns

    axial = matrix_columns(lambda f, g: flux_a[f, g] * HALF)
    radial = matrix_columns(lambda f, g: flux_r[f, g] * HALF)
    angular = matrix_columns(lambda f, g: flux_t[f, g] * (2.0 * HALF))
    axial_t = matrix_columns(lambda f, g: flux_a[g, f] * HALF)
    radial_t = matrix_columns(lambda f, g: flux_r[g, f] * HALF)
    angular_t = matrix_columns(lambda f, g: flux_t[g, f] * (2.0 * HALF))
    radial_back = [-column for column in radial_t]

    def met(columns, mirrored, speed):
        return jnp.where(sub < 5, mirrored * SPREAD + mix(columns, mirrored) * speed, 0.0)

    @pl.when(slab == 0)
    def _():
        for ref in (near, far_near):
            ref[:, 3] = jnp.zeros((2, 8, 128), F32)
        for ref in (q0, q1, p0, p1):
            ref[:, 0] = jnp.zeros_like(ref[:, 0])

    @pl.when(slab == SLABS - 1)
    def _():
        for ref in (near, far_near):
            ref[:, 2] = jnp.zeros((2, 8, 128), F32)
        for ref in (q0, q1, p0, p1):
            ref[:, PLANES + 1] = jnp.zeros_like(ref[:, PLANES + 1])

    def pack_columns(ref, level, fields):
        flat = ref.reshape(ref.shape[0] * (PLANES + 2) * COLS, RADII)
        for f in fields:
            for side, c in ((0, 0), (1, COLS - 1)):
                begin = (f * (PLANES + 2) + 1) * COLS + c
                col_send[level, side, f * PLANES : (f + 1) * PLANES] = flat[
                    pl.ds(begin, PLANES, stride=COLS), :
                ]

    def columns_of(ref, level, phase, first, number):
        rows = pl.ds(first * PLANES, number * PLANES)
        copies = []
        for side, to in ((0, left), (1, right)):
            copies.append(
                pltpu.make_async_remote_copy(
                    src_ref=col_send.at[level, side, rows],
                    dst_ref=col_recv.at[level, side, rows],
                    send_sem=halo_send.at[phase, side],
                    recv_sem=halo_recv.at[phase, side],
                    device_id=(to, slab),
                    device_id_type=MESH,
                )
            )
        return copies

    def planes_of(ref, phase, first, number):
        fields = pl.ds(first, number)
        up = pltpu.make_async_remote_copy(
            src_ref=ref.at[fields, PLANES],
            dst_ref=ref.at[fields, 0],
            send_sem=halo_send.at[phase, 2],
            recv_sem=halo_recv.at[phase, 2],
            device_id=(sector, lax.rem(slab + 1, SLABS)),
            device_id_type=MESH,
        )
        downward = pltpu.make_async_remote_copy(
            src_ref=ref.at[fields, 1],
            dst_ref=ref.at[fields, PLANES + 1],
            send_sem=halo_send.at[phase, 3],
            recv_sem=halo_recv.at[phase, 3],
            device_id=(sector, lax.rem(slab + SLABS - 1, SLABS)),
            device_id_type=MESH,
        )
        return up, downward

    def tile_copy(which, place, source, target, to):
        return pltpu.make_async_remote_copy(
            src_ref=source,
            dst_ref=target,
            send_sem=tile_send.at[which, place],
            recv_sem=tile_recv.at[which, place],
            device_id=to,
            device_id_type=MESH,
        )

    slab_down, slab_up = lax.rem(slab + SLABS - 1, SLABS), lax.rem(slab + 1, SLABS)

    def exchange_tiles(which, act):
        inner = tile.at[which, pl.ds(0, 8)]
        act(tile_copy(which, 8, tile.at[which], far.at[which], (behind, slab)), "both")
        act(tile_copy(which, 4, inner, far_near.at[which, 0], (behind_left, slab)), "both")
        act(tile_copy(which, 5, inner, far_near.at[which, 1], (behind_right, slab)), "both")
        act(tile_copy(which, 0, inner, near.at[which, 0], (left, slab)), "both")
        act(tile_copy(which, 1, inner, near.at[which, 1], (right, slab)), "both")
        downward = (
            tile_copy(which, 6, inner, far_near.at[which, 2], (behind, slab_down)),
            tile_copy(which, 2, inner, near.at[which, 2], (sector, slab_down)),
        )
        upward = (
            tile_copy(which, 7, inner, far_near.at[which, 3], (behind, slab_up)),
            tile_copy(which, 3, inner, near.at[which, 3], (sector, slab_up)),
        )

        @pl.when(slab > 0)
        def _():
            for copy in downward:
                act(copy, "send")
            for copy in upward:
                act(copy, "recv")

        @pl.when(slab < SLABS - 1)
        def _():
            for copy in upward:
                act(copy, "send")
            for copy in downward:
                act(copy, "recv")

    def shifted(rows, beside):
        from_right, from_left, from_up, from_down = beside
        t_minus = jnp.where(ray % COLS == 0, pltpu.roll(from_left, 121, 1), pltpu.roll(rows, 1, 1))
        t_plus = jnp.where(ray % COLS == 7, pltpu.roll(from_right, 7, 1), pltpu.roll(rows, 127, 1))
        x_minus = jnp.where(ray < COLS, pltpu.roll(from_down, 8, 1), pltpu.roll(rows, 8, 1))
        x_plus = jnp.where(ray >= 120, pltpu.roll(from_up, 120, 1), pltpu.roll(rows, 120, 1))
        return x_minus, x_plus, t_minus, t_plus

    def mix(columns, fields):
        total = columns[0] * fields[:1]
        for g in range(1, 5):
            total = total + columns[g] * fields[g : g + 1]
        return total

    def forward_inner(rows, following, beside, speed, flow):
        x_minus, x_plus, t_minus, t_plus = shifted(rows, beside)
        dx = x_plus - x_minus
        mixed = mix(axial, dx) + mix(angular, t_plus - t_minus)
        around = x_plus + x_minus + t_plus + t_minus
        if following is not None:
            mixed, around = mixed + mix(radial, following), around + following
        result = rows * KEEP + around * SPREAD - (flow * HALF) * dx - speed * mixed
        return jnp.where(sub < 5, result, 0.0)

    def adjoint_inner(rows, following, beside, coefs, speed_next):
        x_minus, x_plus, t_minus, t_plus = shifted(rows, beside)
        k_x_minus, k_x_plus, k_t_minus, k_t_plus = coefs
        result = mix(axial_t, x_plus * k_x_plus[5:6] - x_minus * k_x_minus[5:6])
        result = result + mix(angular_t, t_plus * k_t_plus[5:6] - t_minus * k_t_minus[5:6])
        result = result + (x_plus * k_x_plus[6:7] - x_minus * k_x_minus[6:7]) * HALF
        around = x_plus + x_minus + t_plus + t_minus
        if following is not None:
            result, around = result + mix(radial_t, following * speed_next), around + following
        result = result + rows * KEEP + around * SPREAD
        return jnp.where(sub < 5, result, 0.0)

    def stack(which):
        return jnp.concatenate([far[which][:8], far_near[which, 2], far_near[which, 3]], axis=0)

    def exchange(ref, level, phase, first, number, act, planes_first=None):
        for copy in columns_of(ref, level, phase, first, number):
            act(copy, "both")
        if planes_first is None:
            up, downward = planes_of(ref, phase, first, number)
        else:
            up, downward = planes_of(ref, phase, planes_first, first + number - planes_first)

        @pl.when(slab < SLABS - 1)
        def _():
            act(up, "send")
            act(downward, "recv")

        @pl.when(slab > 0)
        def _():
            act(downward, "send")
            act(up, "recv")

    def start(copy, part_of):
        if part_of != "recv":
            copy.start()

    def arrive(copy, part_of):
        if part_of != "send":
            copy.wait_recv()

    def leave(copy, part_of):
        if part_of != "recv":
            copy.wait_send()

    wanted = jnp.where(row[:16] < 8, 2 * row[:16], 2 * (row[:16] - 8) + 1)
    chosen = jnp.where(lane[:16] == wanted, 1.0, 0.0).astype(BF16)

    def pack_inner(i, fields):
        here = jnp.zeros((8, 128), F32)
        for f, value in enumerate(fields):
            here = jnp.where(ray // 2 == f, value if f == 0 else pltpu.roll(value, 2 * f, 1), here)
        rows0[i] = here

    def packed():
        high, low = split(rows0[...].reshape(128, 128))
        both = dot_nt(chosen, high) + dot_nt(chosen, low)
        return both[:8], both[8:]

    def patch(ref, skip, inner, following, fields):
        wide = jnp.concatenate([inner, following, jnp.zeros((112, 128), F32)], axis=0)
        turned[...] = wide.T.reshape(PLANES, COLS, 128)

        def step(i, carry):
            here = turned[i]
            for f in fields:
                zero = here if f == 0 else pltpu.roll(here, 128 - f, 1)
                one = pltpu.roll(here, 121 - f, 1)
                ref[f, i + skip] += jnp.where(ray == 0, zero, jnp.where(ray == 1, one, 0.0))
            return carry

        lax.fori_loop(0, PLANES, step, 0, unroll=4)

    def beside(value, level, f, i):
        before = jnp.broadcast_to(col_recv[level, 1, pl.ds(f * PLANES + i, 1), :], (8, 128))
        after = jnp.broadcast_to(col_recv[level, 0, pl.ds(f * PLANES + i, 1), :], (8, 128))
        t_minus = jnp.where(sub == 0, before, pltpu.roll(value, 1, 0))
        t_plus = jnp.where(sub == COLS - 1, after, pltpu.roll(value, COLS - 1, 0))
        r_minus = jnp.where(ray == 0, 0.0, pltpu.roll(value, 1, 1))
        r_plus = jnp.where(ray == RADII - 1, 0.0, pltpu.roll(value, RADII - 1, 1))
        return t_minus, t_plus, r_minus, r_plus

    inverse = 1.0 / (ray.astype(F32) + 0.5)

    def forward_plane(src, level, dst, i):
        u, c = q0[5, i + 1] * HALF, q0[6, i + 1] * HALF
        values, dx, dr, dt, around = [], [], [], [], []
        for f in range(5):
            value, x_minus, x_plus = src[f, i + 1], src[f, i], src[f, i + 2]
            t_minus, t_plus, r_minus, r_plus = beside(value, level, f, i)
            values.append(value)
            dx.append(x_plus - x_minus)
            dr.append(r_plus - r_minus)
            dt.append((t_plus - t_minus) * inverse)
            around.append((x_plus + x_minus) + (t_plus + t_minus) + (r_plus + r_minus))
        for f in range(5):
            mixed = flux_a[f, 0] * dx[0] + flux_r[f, 0] * dr[0] + flux_t[f, 0] * dt[0]
            for g in range(1, 5):
                mixed = mixed + flux_a[f, g] * dx[g] + flux_r[f, g] * dr[g] + flux_t[f, g] * dt[g]
            dst[f, i + 1] = values[f] * KEEP + around[f] * SPREAD - u * dx[f] - c * mixed

    def adjoint_plane(src, level, store, i):
        u_minus, u_plus = q0[5, i] * HALF, q0[5, i + 2] * HALF
        c = q0[6, i + 1] * HALF
        c_minus, c_plus = q0[6, i] * HALF, q0[6, i + 2] * HALF
        before = jnp.broadcast_to(col_recv[0, 1, pl.ds(6 * PLANES + i, 1), :], (8, 128)) * HALF
        after = jnp.broadcast_to(col_recv[0, 0, pl.ds(6 * PLANES + i, 1), :], (8, 128)) * HALF
        c_t_minus = jnp.where(sub == 0, before, pltpu.roll(c, 1, 0)) * inverse
        c_t_plus = jnp.where(sub == COLS - 1, after, pltpu.roll(c, COLS - 1, 0)) * inverse
        c_r_minus = pltpu.roll(c, 1, 1)
        c_r_plus = pltpu.roll(c, RADII - 1, 1)
        carried, dx, dr, dt = [], [], [], []
        for f in range(5):
            value, x_minus, x_plus = src[f, i + 1], src[f, i], src[f, i + 2]
            t_minus, t_plus, r_minus, r_plus = beside(value, level, f, i)
            dx.append(c_plus * x_plus - c_minus * x_minus)
            dr.append(c_r_plus * r_plus - c_r_minus * r_minus)
            dt.append(c_t_plus * t_plus - c_t_minus * t_minus)
            around = (x_plus + x_minus) + (t_plus + t_minus) + (r_plus + r_minus)
            carried.append(
                value * KEEP + around * SPREAD + (u_plus * x_plus - u_minus * x_minus)
            )
        for f in range(5):
            result = carried[f]
            for g in range(5):
                result = result + flux_a[g, f] * dx[g] + flux_r[g, f] * dr[g] + flux_t[g, f] * dt[g]
            store(f, i, result)

    def planes(body):
        def step(i, carry):
            body(i)
            return carry

        lax.fori_loop(0, PLANES, step, 0, unroll=UNROLL)

    for load in loads:
        load.wait()
    pack_columns(q0, 0, (0, 1, 2, 3, 4, 6))
    planes(lambda i: pack_inner(i, [q0[f, i + 1] for f in (0, 1, 2, 3, 4, 6, 5)]))
    first_rows, first_next = packed()
    first_rows = jnp.where(sub == 7, pairs.astype(F32), first_rows)
    tile[0, :8] = first_rows
    tile[0, 8:] = first_next
    pl.semaphore_wait(
        barrier,
        MEMBERS - 1 + GROUPS - 1 + 4 + jnp.where(slab > 0, 2, 0) + jnp.where(slab < SLABS - 1, 2, 0),
    )
    exchange_tiles(0, start)
    sent.append(lambda: exchange_tiles(0, leave))
    exchange(q0, 0, 0, 0, 5, start)
    sent.append(lambda: exchange(q0, 0, 0, 0, 5, leave))

    def mate_copy(source, target, which, r, to):
        return pltpu.make_async_remote_copy(
            src_ref=source.at[r],
            dst_ref=target.at[r],
            send_sem=many_send.at[which],
            recv_sem=many_recv.at[which],
            device_id=(to, slab),
            device_id_type=MESH,
        )

    def to_mate(source, target, which):
        return lambda r: mate_copy(source, target, which, r, mate(r))

    def back_mate(source, target, which):
        return lambda r: mate_copy(source, target, which, r, mate(MEMBERS - r))

    def start_all(copy_of):
        def step(r, carry):
            copy_of(r).start()
            return carry

        lax.fori_loop(4, MEMBERS, step, 0)
        lax.fori_loop(1, 4, step, 0)

    def all_of(source, target, which):
        rest = pl.ds(1, MEMBERS - 1)
        return pltpu.make_async_remote_copy(
            src_ref=source.at[rest],
            dst_ref=target.at[rest],
            send_sem=many_send.at[which],
            recv_sem=many_recv.at[which],
            device_id=(right, slab),
            device_id_type=MESH,
        )

    wave_in[0] = wave_out[0]
    exchange(q0, 0, 0, 0, 5, arrive)
    planes(functools.partial(forward_plane, q0, 0, q1))
    pack_columns(q1, 1, range(5))
    exchange(q1, 1, 1, 0, 5, start)
    sent.append(lambda: exchange(q1, 1, 1, 0, 5, leave))
    start_all(to_mate(wave_out, wave_in, 0))
    sent.append(lambda: all_of(wave_out, wave_in, 0).wait_send())
    exchange(q1, 1, 1, 0, 5, arrive)
    planes(functools.partial(forward_plane, q1, 1, p0))
    exchange_tiles(0, arrive)
    theirs, theirs_next = far[0][:8], far[0][8:]
    by_us = [near[0, k] for k in range(4)]
    by_them = [far_near[0, k] for k in range(4)]
    cross_right = crossing(by_us[0][7:8].astype(I32))
    cross_left = crossing(by_us[1][7:8].astype(I32))
    cross_back = crossing(theirs[7:8].astype(I32))

    def opposite_values(which):
        three = across_axis(stack(which), cross)
        return [
            three[:8],
            across_axis(far_near[which, 0], cross_right),
            across_axis(far_near[which, 1], cross_left),
            three[8:16],
            three[16:],
        ]

    met_values = opposite_values(0)
    met_speeds = [values[5:6] for values in met_values]
    speed, speed_next, flow = first_rows[5:6], first_next[5:6], first_rows[6:7]
    speeds = [speed] + [values[5:6] for values in by_us]
    added = [met(radial, values * parity, at) for values, at in zip(met_values, speeds)]
    there = across_axis(first_rows, cross_back)
    met_speed_there = there[5:6]
    theirs_after = forward_inner(theirs, theirs_next, by_them, theirs[5:6], theirs[6:7])
    theirs_after = theirs_after + met(radial, there * parity, theirs[5:6])
    mirrored = across_axis(theirs_after, cross) * parity
    inner = forward_inner(added[0], None, added[1:], speed, flow) + met(radial, mirrored, speed)
    following = met(radial, added[0], speed_next)
    patch(p0, 1, inner, following, (4,))

    pressure = p0[4, 1 : PLANES + 1].reshape(PLANES * COLS, RADII)
    high, low = split(pressure)
    lines = (dot(pick[...], high) + dot(pick[...], low)) * factor[...]
    lines_out[...] = lines.reshape(2, MEMBERS, PART, RADII)
    for h in range(2):
        start_all(to_mate(lines_out.at[h], lines_in.at[h], 1 + h))
        sent.append(lambda h=h: all_of(lines_out.at[h], lines_in.at[h], 1 + h).wait_send())
        lines_in[h, 0] = lines_out[h, 0]
    patch(p0, 1, inner, following, range(4))
    planes(lambda i: pack_inner(i, [p0[f, i + 1] for f in range(4)]))
    forward_rows, forward_next = packed()
    pack_columns(p0, 2, range(4))
    all_of(wave_out, wave_in, 0).wait_recv()
    given = wave_in[...]
    sub3, ray3 = iota((MEMBERS, 8, 128), 1), iota((MEMBERS, 8, 128), 2)
    for h in range(2):
        some = given[:, :, h * 128 : (h + 1) * 128]
        first = jnp.where(sub3 // CAP == ray3 // WAVES, some, 0.0)
        second = jnp.where(sub3 // CAP + 2 == ray3 // WAVES, some, 0.0)
        encoder = jnp.concatenate([first, second], axis=1).reshape(MEMBERS * PART, 128)
        enc[h, 0], enc[h, 1] = split(encoder)
        enc_t[h, 0], enc_t[h, 1] = split(encoder.T)

    def rows_of(k):
        return pl.ds(ORDER.index(k % GROUPS) * WAVES, WAVES)

    def to_twin(k):
        return pltpu.make_async_remote_copy(
            src_ref=part.at[rows_of(k)],
            dst_ref=part_in.at[k - 1],
            send_sem=few_send.at[0, k - 1],
            recv_sem=few_recv.at[0, k - 1],
            device_id=(twin(k), slab),
            device_id_type=MESH,
        )

    def from_owner(k):
        return pltpu.make_async_remote_copy(
            src_ref=whole.at[rows_of(0)],
            dst_ref=whole.at[rows_of(GROUPS - k)],
            send_sem=few_send.at[1, k - 1],
            recv_sem=few_recv.at[1, k - 1],
            device_id=(twin(k), slab),
            device_id_type=MESH,
        )

    for h in range(2):
        all_of(lines_out.at[h], lines_in.at[h], 1 + h).wait_recv()
        high, low = split(lines_in[h].reshape(MEMBERS * PART, RADII))
        part[h * 128 : (h + 1) * 128] = dot(enc_t[h, 0], high) + (
            dot(enc_t[h, 0], low) + dot(enc_t[h, 1], high)
        )
        for k in HALVES[h]:
            if k > 0:
                to_twin(k).start()
                sent.append(lambda k=k: to_twin(k).wait_send())
    exchange(p0, 2, 2, 0, 4, start)
    sent.append(lambda: exchange(p0, 2, 2, 0, 4, leave))
    exchange(q0, 0, 5, 6, 1, start, 5)
    sent.append(lambda: exchange(q0, 0, 5, 6, 1, leave, 5))
    mine = part[rows_of(0), :]
    for k in ORDER[::-1][1:]:
        to_twin(k).wait_recv()
        mine = mine + part_in[k - 1]
    whole[rows_of(0), :] = mine
    for k in ORDER[:-1]:
        from_owner(k).start()
        sent.append(lambda k=k: from_owner(k).wait_send())
    harm[:, 0] = mine[:MODES]

    for h in (1, 0):
        for k in HALVES[h]:
            if k > 0:
                from_owner(GROUPS - k).wait_recv()
        high, low = split(whole[h * 128 : (h + 1) * 128])
        grad = dot(enc[h, 0], high) + (dot(enc[h, 0], low) + dot(enc[h, 1], high))
        grad_out[h] = grad.reshape(MEMBERS, PART, RADII)
        start_all(back_mate(grad_out.at[h], grad_in.at[h], 3 + h))
        sent.append(lambda h=h: all_of(grad_out.at[h], grad_in.at[h], 3 + h).wait_send())
        grad_in[h, 0] = grad_out[h, 0]
    exchange(p0, 2, 2, 0, 4, arrive)
    for h in (1, 0):
        all_of(grad_out.at[h], grad_in.at[h], 3 + h).wait_recv()
    high, low = split(grad_in[...].reshape(ROWS, RADII) * factor[...])
    impulse = dot(pick_t[...], high) + dot(pick_t[...], low)
    impulse = impulse.reshape(PLANES, COLS, RADII)
    p0[4, 1 : PLANES + 1] = p0[4, 1 : PLANES + 1] + impulse

    pressure = p0[4, 1 : PLANES + 1].reshape(PLANES * COLS, RADII)
    pressure = pressure.T
    start_rows = jnp.where(sub == 4, pressure[:1], forward_rows)
    start_next = jnp.where(sub == 4, pressure[1:2], forward_next)
    tile[1, :8] = start_rows
    tile[1, 8:] = start_next
    exchange_tiles(1, start)
    sent.append(lambda: exchange_tiles(1, leave))
    pack_columns(p0, 2, (4,))
    exchange(p0, 2, 3, 4, 1, start)
    sent.append(lambda: exchange(p0, 2, 3, 4, 1, leave))
    exchange(q0, 0, 5, 6, 1, arrive, 5)
    exchange(p0, 2, 3, 4, 1, arrive)

    def store_p1(f, i, value):
        p1[f, i + 1] = value

    def store_out(f, i, value):
        out[f, i] = value

    planes(functools.partial(adjoint_plane, p0, 2, store_p1))
    pack_columns(p1, 3, range(5))
    exchange(p1, 3, 4, 0, 5, start)
    sent.append(lambda: exchange(p1, 3, 4, 0, 5, leave))
    exchange(p1, 3, 4, 0, 5, arrive)
    planes(functools.partial(adjoint_plane, p1, 3, store_out))
    exchange_tiles(1, arrive)
    coefs = shifted(first_rows, by_us)
    added = [
        met(radial_back, values * parity, at) for values, at in zip(opposite_values(1), met_speeds)
    ]
    theirs, theirs_follow = far[1][:8], far[1][8:]
    theirs_after = adjoint_inner(
        theirs,
        theirs_follow,
        [far_near[1, k] for k in range(4)],
        shifted(far[0][:8], by_them),
        theirs_next[5:6],
    )
    there = across_axis(start_rows, cross_back) * parity
    theirs_after = theirs_after + met(radial_back, there, met_speed_there)
    mirrored = across_axis(theirs_after, cross) * parity
    inner = adjoint_inner(added[0], None, added[1:], coefs, None)
    inner = inner + met(radial_back, mirrored, met_speeds[0])
    following = met(radial_back, added[0], speed)
    patch(out, 0, inner, following, range(5))

    for wait in sent:
        wait()


def local(
    state,
    mean_velocity,
    sound_speed,
    flux_axial,
    flux_radial,
    flux_azimuthal,
    axis_pair,
    panel_weight,
    panel_cell,
    panel_owner,
    panel_count,
):
    outside = pl.BlockSpec(memory_space=pltpu.HBM)
    vector = pl.BlockSpec(memory_space=pltpu.VMEM)

    def grid_of(fields):
        return pltpu.VMEM((fields, PLANES + 2, COLS, RADII), F32)

    fields, rows = pl.pallas_call(
        kernel,
        out_shape=(
            jax.ShapeDtypeStruct((5, PLANES, COLS, RADII), F32),
            jax.ShapeDtypeStruct((MODES, 1, RADII), F32),
        ),
        in_specs=[outside] * 11,
        out_specs=(vector, vector),
        scratch_shapes=[
            grid_of(7),
            grid_of(5),
            grid_of(5),
            grid_of(5),
            pltpu.VMEM((1, PANELS), F32),
            pltpu.VMEM((1, PANELS), I32),
            pltpu.VMEM((1, PANELS), I32),
            pltpu.SMEM((5, 5), F32),
            pltpu.SMEM((5, 5), F32),
            pltpu.SMEM((5, 5), F32),
            pltpu.SMEM((1, COLS), I32),
            pltpu.SMEM((1, 1), I32),
            pltpu.VMEM((4, 2, 7 * PLANES, RADII), F32),
            pltpu.VMEM((4, 2, 7 * PLANES, RADII), F32),
            pltpu.VMEM((2, 16, 128), F32),
            pltpu.VMEM((2, 4, 8, 128), F32),
            pltpu.VMEM((2, 16, 128), F32),
            pltpu.VMEM((2, 4, 8, 128), F32),
            pltpu.VMEM((PLANES, COLS, 128), F32),
            pltpu.VMEM((PLANES, COLS, 128), F32),
            pltpu.VMEM((ROWS, 128), BF16),
            pltpu.VMEM((128, ROWS), BF16),
            pltpu.VMEM((ROWS, 128), F32),
            pltpu.VMEM((MEMBERS, 8, LANES), F32),
            pltpu.VMEM((MEMBERS, 8, LANES), F32),
            pltpu.VMEM((2, 2, MEMBERS * PART, 128), BF16),
            pltpu.VMEM((2, 2, 128, MEMBERS * PART), BF16),
            pltpu.VMEM((2, MEMBERS, PART, RADII), F32),
            pltpu.VMEM((2, MEMBERS, PART, RADII), F32),
            pltpu.VMEM((GROUPS * WAVES, RADII), F32),
            pltpu.VMEM((GROUPS - 1, WAVES, RADII), F32),
            pltpu.VMEM((GROUPS * WAVES, RADII), F32),
            pltpu.VMEM((2, MEMBERS, PART, RADII), F32),
            pltpu.VMEM((2, MEMBERS, PART, RADII), F32),
            pltpu.SemaphoreType.DMA((11,)),
            pltpu.SemaphoreType.DMA((6, 4)),
            pltpu.SemaphoreType.DMA((6, 4)),
            pltpu.SemaphoreType.DMA((2, 9)),
            pltpu.SemaphoreType.DMA((2, 9)),
            pltpu.SemaphoreType.DMA((5,)),
            pltpu.SemaphoreType.DMA((5,)),
            pltpu.SemaphoreType.DMA((2, GROUPS - 1)),
            pltpu.SemaphoreType.DMA((2, GROUPS - 1)),
        ],
        compiler_params=pltpu.CompilerParams(
            collective_id=0, has_side_effects=True, vmem_limit_bytes=VMEM_GRANT
        ),
    )(
        *(
            pltpu.with_memory_space_constraint(argument, pltpu.HBM)
            for argument in (
                state,
                mean_velocity,
                sound_speed,
                flux_axial,
                flux_radial,
                flux_azimuthal,
                axis_pair,
                panel_weight,
                panel_cell,
                panel_owner.reshape(1, PANELS),
            )
        ),
        panel_count,
    )
    return fields, rows.reshape(1, 1, MODES, RADII)


def solution(mesh):
    return jax.shard_map(
        local,
        mesh=mesh,
        in_specs=(
            P(None, "slab", "sector", None),
            P("slab", "sector", None),
            P("slab", "sector", None),
            P(),
            P(),
            P(),
            P("sector", None),
            P("slab", "sector"),
            P("slab", "sector"),
            P("slab", "sector", None),
            P("slab", "sector"),
        ),
        out_specs=(P(None, "slab", "sector", None), P("slab", "sector", None, None)),
        check_vma=False,
    )
```

```python
import functools
import math

import jax
import jax.numpy as jnp
from jax import lax
from jax.experimental import pallas as pl
from jax.experimental.pallas import tpu as pltpu
from jax.sharding import PartitionSpec as P

PLANES = 16
COLS = 8
RADII = 128
PANELS = 384
ORDERS = 16
MODES = 31
SECTORS = 128
SLABS = 4
GROUPS = 8
MEMBERS = SECTORS // GROUPS
CAP = 4
SLOTS = GROUPS * CAP
ROWS = MEMBERS * SLOTS
WAVES = 32
LANES = GROUPS * WAVES
SCALE = PANELS**-0.5
TIME_STEP = 0.25
VISCOSITY = 0.05
KEEP = 1.0 - 6.0 * VISCOSITY * TIME_STEP
SPREAD = VISCOSITY * TIME_STEP
HALF = 0.5 * TIME_STEP
ORDER = (4, 3, 5, 2, 6, 1, 7, 0)
HALVES = (ORDER[: GROUPS // 2], ORDER[GROUPS // 2 :])
PART = SLOTS // 2
UNROLL = 8
VMEM_GRANT = 32 << 20
MESH = pl.DeviceIdType.MESH
F32, BF16, I32 = jnp.float32, jnp.bfloat16, jnp.int32


def split(x):
    high = x.astype(BF16)
    return high, (x - high.astype(F32)).astype(BF16)


def dot(a, b):
    return lax.dot_general(a, b, (((1,), (0,)), ((), ())), preferred_element_type=F32)


def dot_nt(a, b):
    return lax.dot_general(a, b, (((1,), (1,)), ((), ())), preferred_element_type=F32)


def iota(shape, dim):
    return lax.broadcasted_iota(I32, shape, dim)


def kernel(
    state,
    mean,
    sound,
    flux_a_in,
    flux_r_in,
    flux_t_in,
    pair_in,
    weight_in,
    cell_in,
    owner_in,
    count_in,
    out,
    harm,
    q0,
    q1,
    p0,
    p1,
    weight,
    cell,
    owner,
    flux_a,
    flux_r,
    flux_t,
    pair,
    count,
    col_send,
    col_recv,
    tile,
    near,
    far,
    far_near,
    rows0,
    turned,
    pick,
    pick_t,
    factor,
    wave_out,
    wave_in,
    enc,
    enc_t,
    lines_out,
    lines_in,
    part,
    part_in,
    whole,
    grad_out,
    grad_in,
    load_sem,
    halo_send,
    halo_recv,
    tile_send,
    tile_recv,
    many_send,
    many_recv,
    few_send,
    few_recv,
):
    sector = lax.axis_index("sector")
    slab = lax.axis_index("slab")
    group = lax.div(sector, MEMBERS)
    member = lax.rem(sector, MEMBERS)
    right = lax.rem(sector + 1, SECTORS)
    left = lax.rem(sector + SECTORS - 1, SECTORS)
    behind = lax.rem(sector + SECTORS // 2, SECTORS)

    def mate(r):
        return group * MEMBERS + lax.rem(member + r, MEMBERS)

    def twin(k):
        return lax.rem(group + k, GROUPS) * MEMBERS + member

    sent = []

    barrier = pltpu.get_barrier_semaphore()

    def greet(to_sector, to_slab):
        pl.semaphore_signal(barrier, inc=1, device_id=(to_sector, to_slab), device_id_type=MESH)

    behind_right = lax.rem(behind + 1, SECTORS)
    behind_left = lax.rem(behind + SECTORS - 1, SECTORS)
    greet(right, slab)
    greet(left, slab)
    greet(behind_right, slab)
    greet(behind_left, slab)

    @pl.when(slab > 0)
    def _():
        greet(sector, slab - 1)
        greet(behind, slab - 1)

    @pl.when(slab < SLABS - 1)
    def _():
        greet(sector, slab + 1)
        greet(behind, slab + 1)

    for k in range(1, GROUPS):
        greet(twin(k), slab)

    def greet_mate(r, carry):
        greet(mate(r), slab)
        return carry

    lax.fori_loop(1, MEMBERS, greet_mate, 0)

    loads = [
        pltpu.make_async_copy(state, q0.at[pl.ds(0, 5), pl.ds(1, PLANES)], load_sem.at[0]),
        pltpu.make_async_copy(mean, q0.at[5, pl.ds(1, PLANES)], load_sem.at[1]),
        pltpu.make_async_copy(sound, q0.at[6, pl.ds(1, PLANES)], load_sem.at[2]),
    ]
    lists = [
        pltpu.make_async_copy(weight_in, weight, load_sem.at[3]),
        pltpu.make_async_copy(cell_in, cell, load_sem.at[4]),
        pltpu.make_async_copy(owner_in, owner, load_sem.at[5]),
        pltpu.make_async_copy(flux_a_in, flux_a, load_sem.at[6]),
        pltpu.make_async_copy(flux_r_in, flux_r, load_sem.at[7]),
        pltpu.make_async_copy(flux_t_in, flux_t, load_sem.at[8]),
        pltpu.make_async_copy(pair_in, pair, load_sem.at[9]),
        pltpu.make_async_copy(count_in, count, load_sem.at[10]),
    ]
    for load in lists + loads:
        load.start()


    row = iota((128, 128), 0)
    lane = iota((128, 128), 1)
    for load in lists:
        load.wait()
    owners = owner[...]
    cells = cell[...]
    weights = weight[...]
    live = count[0, 0]
    across, down = [], []
    for q in range(3):
        wide = jnp.broadcast_to(owners[:, q * 128 : (q + 1) * 128], (128, 128)).astype(F32)
        across.append(wide)
        down.append(wide.T)
    slot_pieces, cell_pieces, weight_pieces = [], [], []
    tall = iota((ROWS, 128), 0)
    for q in range(3):
        earlier = jnp.where((down[q] == across[q]) & (row < lane), 1.0, 0.0)
        for s in range(q):
            earlier = earlier + jnp.where(down[s] == across[q], 1.0, 0.0)
        rank = jnp.sum(earlier, axis=0, keepdims=True).astype(I32)
        at = slice(q * 128, (q + 1) * 128)
        name = owners[:, at]
        relative = (name + MEMBERS - member) % MEMBERS
        ahead = (name // MEMBERS + GROUPS - group) % GROUPS
        position = jnp.zeros((1, 128), I32)
        for at_position, k in enumerate(ORDER):
            position = jnp.where(ahead == k, at_position, position)
        half = position // (GROUPS // 2)
        slot = (half * MEMBERS + relative) * PART + (position % (GROUPS // 2)) * CAP + rank
        place = iota((1, 128), 1) + q * 128
        slot = jnp.where(place < live, slot, -1)
        slot_pieces.append(jnp.where(tall == slot, 1.0, 0.0).astype(BF16))
        cell_pieces.append(jnp.where(row == cells[:, at], 1.0, 0.0).astype(BF16))
        weight_pieces.append(jnp.broadcast_to(weights[:, at], (128, 128)))
    slots = jnp.concatenate(slot_pieces, axis=1)
    spots = jnp.concatenate(cell_pieces, axis=1)
    heavy, light = split(jnp.concatenate(weight_pieces, axis=1))
    picked = dot_nt(slots, spots).astype(BF16)
    pick[...] = picked
    pick_t[...] = dot_nt(spots, slots).astype(BF16)
    factor[...] = dot_nt(slots, heavy) + dot_nt(slots, light)
    spread_row, spread_lane = iota((128, LANES), 0), iota((128, LANES), 1)
    order = spread_lane % WAVES
    turn = jnp.where(order < ORDERS, order, order - (ORDERS - 1))
    turn = turn * (sector * COLS + spread_row % COLS) + jnp.where(order < ORDERS, 0, 768)
    turn = turn % 1024
    table = jnp.cos(turn.astype(F32) * (2.0 * math.pi / 1024.0)) * SCALE
    table = jnp.where(order < MODES, table, 0.0)
    table_high, table_low = split(table)
    waves = dot(picked, table_high) + dot(picked, table_low)
    tall, tall_lane = iota((ROWS, LANES), 0), iota((ROWS, LANES), 1)
    position = (tall % PART) // CAP + (tall // (MEMBERS * PART)) * (GROUPS // 2)
    waves = jnp.where(position == tall_lane // WAVES, waves, 0.0)
    waves = waves.reshape(2, MEMBERS, PART, LANES)
    halves = (waves[0, :, :8] + waves[0, :, 8:]) + (waves[1, :, :8] + waves[1, :, 8:])
    wave_out[...] = halves + jnp.concatenate([halves[:, 4:], halves[:, :4]], axis=1)

    sub = iota((8, 128), 0)
    ray = iota((8, 128), 1)
    pairs = jnp.zeros((1, 128), I32)
    for c in range(COLS):
        pairs = jnp.where(lane[:1] % COLS == c, pair[0, c], pairs)
    parity = jnp.where((sub == 2) | (sub == 3), -1.0, 1.0)

    def crossing(columns):
        meets = (row % COLS == columns) & (row // COLS == lane // COLS)
        return jnp.where(meets, 1.0, 0.0).astype(BF16)

    cross = crossing(pairs)

    def across_axis(fields, matrix):
        high, low = split(fields)
        return dot(high, matrix) + dot(low, matrix)

    def matrix_columns(entry):
        columns = []
        for g in range(5):
            column = jnp.zeros((8, 128), F32)
            for f in range(5):
                column = jnp.where(sub == f, entry(f, g), column)
            columns.append(column)
        return columns

    axial = matrix_columns(lambda f, g: flux_a[f, g] * HALF)
    radial = matrix_columns(lambda f, g: flux_r[f, g] * HALF)
    angular = matrix_columns(lambda f, g: flux_t[f, g] * (2.0 * HALF))
    axial_t = matrix_columns(lambda f, g: flux_a[g, f] * HALF)
    radial_t = matrix_columns(lambda f, g: flux_r[g, f] * HALF)
    angular_t = matrix_columns(lambda f, g: flux_t[g, f] * (2.0 * HALF))
    radial_back = [-column for column in radial_t]

    def met(columns, mirrored, speed):
        return jnp.where(sub < 5, mirrored * SPREAD + mix(columns, mirrored) * speed, 0.0)

    @pl.when(slab == 0)
    def _():
        for ref in (near, far_near):
            ref[:, 3] = jnp.zeros((2, 8, 128), F32)
        for ref in (q0, q1, p0, p1):
            ref[:, 0] = jnp.zeros_like(ref[:, 0])

    @pl.when(slab == SLABS - 1)
    def _():
        for ref in (near, far_near):
            ref[:, 2] = jnp.zeros((2, 8, 128), F32)
        for ref in (q0, q1, p0, p1):
            ref[:, PLANES + 1] = jnp.zeros_like(ref[:, PLANES + 1])

    def pack_columns(ref, level, fields):
        flat = ref.reshape(ref.shape[0] * (PLANES + 2) * COLS, RADII)
        for f in fields:
            for side, c in ((0, 0), (1, COLS - 1)):
                begin = (f * (PLANES + 2) + 1) * COLS + c
                col_send[level, side, f * PLANES : (f + 1) * PLANES] = flat[
                    pl.ds(begin, PLANES, stride=COLS), :
                ]

    def columns_of(ref, level, phase, first, number):
        rows = pl.ds(first * PLANES, number * PLANES)
        copies = []
        for side, to in ((0, left), (1, right)):
            copies.append(
                pltpu.make_async_remote_copy(
                    src_ref=col_send.at[level, side, rows],
                    dst_ref=col_recv.at[level, side, rows],
                    send_sem=halo_send.at[phase, side],
                    recv_sem=halo_recv.at[phase, side],
                    device_id=(to, slab),
                    device_id_type=MESH,
                )
            )
        return copies

    def planes_of(ref, phase, first, number):
        fields = pl.ds(first, number)
        up = pltpu.make_async_remote_copy(
            src_ref=ref.at[fields, PLANES],
            dst_ref=ref.at[fields, 0],
            send_sem=halo_send.at[phase, 2],
            recv_sem=halo_recv.at[phase, 2],
            device_id=(sector, lax.rem(slab + 1, SLABS)),
            device_id_type=MESH,
        )
        downward = pltpu.make_async_remote_copy(
            src_ref=ref.at[fields, 1],
            dst_ref=ref.at[fields, PLANES + 1],
            send_sem=halo_send.at[phase, 3],
            recv_sem=halo_recv.at[phase, 3],
            device_id=(sector, lax.rem(slab + SLABS - 1, SLABS)),
            device_id_type=MESH,
        )
        return up, downward

    def tile_copy(which, place, source, target, to):
        return pltpu.make_async_remote_copy(
            src_ref=source,
            dst_ref=target,
            send_sem=tile_send.at[which, place],
            recv_sem=tile_recv.at[which, place],
            device_id=to,
            device_id_type=MESH,
        )

    slab_down, slab_up = lax.rem(slab + SLABS - 1, SLABS), lax.rem(slab + 1, SLABS)

    def exchange_tiles(which, act):
        inner = tile.at[which, pl.ds(0, 8)]
        act(tile_copy(which, 8, tile.at[which], far.at[which], (behind, slab)), "both")
        act(tile_copy(which, 4, inner, far_near.at[which, 0], (behind_left, slab)), "both")
        act(tile_copy(which, 5, inner, far_near.at[which, 1], (behind_right, slab)), "both")
        act(tile_copy(which, 0, inner, near.at[which, 0], (left, slab)), "both")
        act(tile_copy(which, 1, inner, near.at[which, 1], (right, slab)), "both")
        downward = (
            tile_copy(which, 6, inner, far_near.at[which, 2], (behind, slab_down)),
            tile_copy(which, 2, inner, near.at[which, 2], (sector, slab_down)),
        )
        upward = (
            tile_copy(which, 7, inner, far_near.at[which, 3], (behind, slab_up)),
            tile_copy(which, 3, inner, near.at[which, 3], (sector, slab_up)),
        )

        @pl.when(slab > 0)
        def _():
            for copy in downward:
                act(copy, "send")
            for copy in upward:
                act(copy, "recv")

        @pl.when(slab < SLABS - 1)
        def _():
            for copy in upward:
                act(copy, "send")
            for copy in downward:
                act(copy, "recv")

    def shifted(rows, beside):
        from_right, from_left, from_up, from_down = beside
        t_minus = jnp.where(ray % COLS == 0, pltpu.roll(from_left, 121, 1), pltpu.roll(rows, 1, 1))
        t_plus = jnp.where(ray % COLS == 7, pltpu.roll(from_right, 7, 1), pltpu.roll(rows, 127, 1))
        x_minus = jnp.where(ray < COLS, pltpu.roll(from_down, 8, 1), pltpu.roll(rows, 8, 1))
        x_plus = jnp.where(ray >= 120, pltpu.roll(from_up, 120, 1), pltpu.roll(rows, 120, 1))
        return x_minus, x_plus, t_minus, t_plus

    def mix(columns, fields):
        total = columns[0] * fields[:1]
        for g in range(1, 5):
            total = total + columns[g] * fields[g : g + 1]
        return total

    def forward_inner(rows, following, beside, speed, flow):
        x_minus, x_plus, t_minus, t_plus = shifted(rows, beside)
        dx = x_plus - x_minus
        mixed = mix(axial, dx) + mix(angular, t_plus - t_minus)
        around = x_plus + x_minus + t_plus + t_minus
        if following is not None:
            mixed, around = mixed + mix(radial, following), around + following
        result = rows * KEEP + around * SPREAD - (flow * HALF) * dx - speed * mixed
        return jnp.where(sub < 5, result, 0.0)

    def adjoint_inner(rows, following, beside, coefs, speed_next):
        x_minus, x_plus, t_minus, t_plus = shifted(rows, beside)
        k_x_minus, k_x_plus, k_t_minus, k_t_plus = coefs
        result = mix(axial_t, x_plus * k_x_plus[5:6] - x_minus * k_x_minus[5:6])
        result = result + mix(angular_t, t_plus * k_t_plus[5:6] - t_minus * k_t_minus[5:6])
        result = result + (x_plus * k_x_plus[6:7] - x_minus * k_x_minus[6:7]) * HALF
        around = x_plus + x_minus + t_plus + t_minus
        if following is not None:
            result, around = result + mix(radial_t, following * speed_next), around + following
        result = result + rows * KEEP + around * SPREAD
        return jnp.where(sub < 5, result, 0.0)

    def stack(which):
        return jnp.concatenate([far[which][:8], far_near[which, 2], far_near[which, 3]], axis=0)

    def exchange(ref, level, phase, first, number, act, planes_first=None):
        for copy in columns_of(ref, level, phase, first, number):
            act(copy, "both")
        if planes_first is None:
            up, downward = planes_of(ref, phase, first, number)
        else:
            up, downward = planes_of(ref, phase, planes_first, first + number - planes_first)

        @pl.when(slab < SLABS - 1)
        def _():
            act(up, "send")
            act(downward, "recv")

        @pl.when(slab > 0)
        def _():
            act(downward, "send")
            act(up, "recv")

    def start(copy, part_of):
        if part_of != "recv":
            copy.start()

    def arrive(copy, part_of):
        if part_of != "send":
            copy.wait_recv()

    def leave(copy, part_of):
        if part_of != "recv":
            copy.wait_send()

    wanted = jnp.where(row[:16] < 8, 2 * row[:16], 2 * (row[:16] - 8) + 1)
    chosen = jnp.where(lane[:16] == wanted, 1.0, 0.0).astype(BF16)

    def pack_inner(i, fields):
        here = jnp.zeros((8, 128), F32)
        for f, value in enumerate(fields):
            here = jnp.where(ray // 2 == f, value if f == 0 else pltpu.roll(value, 2 * f, 1), here)
        rows0[i] = here

    def packed():
        high, low = split(rows0[...].reshape(128, 128))
        both = dot_nt(chosen, high) + dot_nt(chosen, low)
        return both[:8], both[8:]

    def patch(ref, skip, inner, following, fields):
        wide = jnp.concatenate([inner, following, jnp.zeros((112, 128), F32)], axis=0)
        turned[...] = wide.T.reshape(PLANES, COLS, 128)

        def step(i, carry):
            here = turned[i]
            for f in fields:
                zero = here if f == 0 else pltpu.roll(here, 128 - f, 1)
                one = pltpu.roll(here, 121 - f, 1)
                ref[f, i + skip] += jnp.where(ray == 0, zero, jnp.where(ray == 1, one, 0.0))
            return carry

        lax.fori_loop(0, PLANES, step, 0, unroll=PLANES)

    def beside(value, level, f, i):
        before = jnp.broadcast_to(col_recv[level, 1, pl.ds(f * PLANES + i, 1), :], (8, 128))
        after = jnp.broadcast_to(col_recv[level, 0, pl.ds(f * PLANES + i, 1), :], (8, 128))
        t_minus = jnp.where(sub == 0, before, pltpu.roll(value, 1, 0))
        t_plus = jnp.where(sub == COLS - 1, after, pltpu.roll(value, COLS - 1, 0))
        r_minus = jnp.where(ray == 0, 0.0, pltpu.roll(value, 1, 1))
        r_plus = jnp.where(ray == RADII - 1, 0.0, pltpu.roll(value, RADII - 1, 1))
        return t_minus, t_plus, r_minus, r_plus

    inverse = 1.0 / (ray.astype(F32) + 0.5)

    def forward_plane(src, level, dst, i):
        u, c = q0[5, i + 1] * HALF, q0[6, i + 1] * HALF
        values, dx, dr, dt, around = [], [], [], [], []
        for f in range(5):
            value, x_minus, x_plus = src[f, i + 1], src[f, i], src[f, i + 2]
            t_minus, t_plus, r_minus, r_plus = beside(value, level, f, i)
            values.append(value)
            dx.append(x_plus - x_minus)
            dr.append(r_plus - r_minus)
            dt.append((t_plus - t_minus) * inverse)
            around.append((x_plus + x_minus) + (t_plus + t_minus) + (r_plus + r_minus))
        for f in range(5):
            mixed = flux_a[f, 0] * dx[0] + flux_r[f, 0] * dr[0] + flux_t[f, 0] * dt[0]
            for g in range(1, 5):
                mixed = mixed + flux_a[f, g] * dx[g] + flux_r[f, g] * dr[g] + flux_t[f, g] * dt[g]
            dst[f, i + 1] = values[f] * KEEP + around[f] * SPREAD - u * dx[f] - c * mixed

    def adjoint_plane(src, level, store, i):
        u_minus, u_plus = q0[5, i] * HALF, q0[5, i + 2] * HALF
        c = q0[6, i + 1] * HALF
        c_minus, c_plus = q0[6, i] * HALF, q0[6, i + 2] * HALF
        before = jnp.broadcast_to(col_recv[0, 1, pl.ds(6 * PLANES + i, 1), :], (8, 128)) * HALF
        after = jnp.broadcast_to(col_recv[0, 0, pl.ds(6 * PLANES + i, 1), :], (8, 128)) * HALF
        c_t_minus = jnp.where(sub == 0, before, pltpu.roll(c, 1, 0)) * inverse
        c_t_plus = jnp.where(sub == COLS - 1, after, pltpu.roll(c, COLS - 1, 0)) * inverse
        c_r_minus = pltpu.roll(c, 1, 1)
        c_r_plus = pltpu.roll(c, RADII - 1, 1)
        carried, dx, dr, dt = [], [], [], []
        for f in range(5):
            value, x_minus, x_plus = src[f, i + 1], src[f, i], src[f, i + 2]
            t_minus, t_plus, r_minus, r_plus = beside(value, level, f, i)
            dx.append(c_plus * x_plus - c_minus * x_minus)
            dr.append(c_r_plus * r_plus - c_r_minus * r_minus)
            dt.append(c_t_plus * t_plus - c_t_minus * t_minus)
            around = (x_plus + x_minus) + (t_plus + t_minus) + (r_plus + r_minus)
            carried.append(
                value * KEEP + around * SPREAD + (u_plus * x_plus - u_minus * x_minus)
            )
        for f in range(5):
            result = carried[f]
            for g in range(5):
                result = result + flux_a[g, f] * dx[g] + flux_r[g, f] * dr[g] + flux_t[g, f] * dt[g]
            store(f, i, result)

    def planes(body):
        def step(i, carry):
            body(i)
            return carry

        lax.fori_loop(0, PLANES, step, 0, unroll=UNROLL)

    for load in loads:
        load.wait()
    pack_columns(q0, 0, (0, 1, 2, 3, 4, 6))
    planes(lambda i: pack_inner(i, [q0[f, i + 1] for f in (0, 1, 2, 3, 4, 6, 5)]))
    first_rows, first_next = packed()
    first_rows = jnp.where(sub == 7, pairs.astype(F32), first_rows)
    tile[0, :8] = first_rows
    tile[0, 8:] = first_next
    pl.semaphore_wait(
        barrier,
        MEMBERS - 1 + GROUPS - 1 + 4 + jnp.where(slab > 0, 2, 0) + jnp.where(slab < SLABS - 1, 2, 0),
    )
    exchange_tiles(0, start)
    sent.append(lambda: exchange_tiles(0, leave))
    exchange(q0, 0, 0, 0, 5, start)
    sent.append(lambda: exchange(q0, 0, 0, 0, 5, leave))

    def mate_copy(source, target, which, r, to):
        return pltpu.make_async_remote_copy(
            src_ref=source.at[r],
            dst_ref=target.at[r],
            send_sem=many_send.at[which],
            recv_sem=many_recv.at[which],
            device_id=(to, slab),
            device_id_type=MESH,
        )

    def to_mate(source, target, which):
        return lambda r: mate_copy(source, target, which, r, mate(r))

    def back_mate(source, target, which):
        return lambda r: mate_copy(source, target, which, r, mate(MEMBERS - r))

    def start_all(copy_of):
        def step(r, carry):
            copy_of(r).start()
            return carry

        lax.fori_loop(4, MEMBERS, step, 0)
        lax.fori_loop(1, 4, step, 0)

    def all_of(source, target, which):
        rest = pl.ds(1, MEMBERS - 1)
        return pltpu.make_async_remote_copy(
            src_ref=source.at[rest],
            dst_ref=target.at[rest],
            send_sem=many_send.at[which],
            recv_sem=many_recv.at[which],
            device_id=(right, slab),
            device_id_type=MESH,
        )

    wave_in[0] = wave_out[0]
    exchange(q0, 0, 0, 0, 5, arrive)
    planes(functools.partial(forward_plane, q0, 0, q1))
    pack_columns(q1, 1, range(5))
    exchange(q1, 1, 1, 0, 5, start)
    sent.append(lambda: exchange(q1, 1, 1, 0, 5, leave))
    start_all(to_mate(wave_out, wave_in, 0))
    sent.append(lambda: all_of(wave_out, wave_in, 0).wait_send())
    exchange(q1, 1, 1, 0, 5, arrive)
    planes(functools.partial(forward_plane, q1, 1, p0))
    exchange_tiles(0, arrive)
    theirs, theirs_next = far[0][:8], far[0][8:]
    by_us = [near[0, k] for k in range(4)]
    by_them = [far_near[0, k] for k in range(4)]
    cross_right = crossing(by_us[0][7:8].astype(I32))
    cross_left = crossing(by_us[1][7:8].astype(I32))
    cross_back = crossing(theirs[7:8].astype(I32))

    def opposite_values(which):
        three = across_axis(stack(which), cross)
        return [
            three[:8],
            across_axis(far_near[which, 0], cross_right),
            across_axis(far_near[which, 1], cross_left),
            three[8:16],
            three[16:],
        ]

    met_values = opposite_values(0)
    met_speeds = [values[5:6] for values in met_values]
    speed, speed_next, flow = first_rows[5:6], first_next[5:6], first_rows[6:7]
    speeds = [speed] + [values[5:6] for values in by_us]
    added = [met(radial, values * parity, at) for values, at in zip(met_values, speeds)]
    there = across_axis(first_rows, cross_back)
    met_speed_there = there[5:6]
    theirs_after = forward_inner(theirs, theirs_next, by_them, theirs[5:6], theirs[6:7])
    theirs_after = theirs_after + met(radial, there * parity, theirs[5:6])
    mirrored = across_axis(theirs_after, cross) * parity
    inner = forward_inner(added[0], None, added[1:], speed, flow) + met(radial, mirrored, speed)
    following = met(radial, added[0], speed_next)
    patch(p0, 1, inner, following, (4,))

    pressure = p0[4, 1 : PLANES + 1].reshape(PLANES * COLS, RADII)
    high, low = split(pressure)
    lines = (dot(pick[...], high) + dot(pick[...], low)) * factor[...]
    lines_out[...] = lines.reshape(2, MEMBERS, PART, RADII)
    for h in range(2):
        start_all(to_mate(lines_out.at[h], lines_in.at[h], 1 + h))
        sent.append(lambda h=h: all_of(lines_out.at[h], lines_in.at[h], 1 + h).wait_send())
        lines_in[h, 0] = lines_out[h, 0]
    patch(p0, 1, inner, following, range(4))
    planes(lambda i: pack_inner(i, [p0[f, i + 1] for f in range(4)]))
    forward_rows, forward_next = packed()
    pack_columns(p0, 2, range(4))
    all_of(wave_out, wave_in, 0).wait_recv()
    given = wave_in[...]
    sub3, ray3 = iota((MEMBERS, 8, 128), 1), iota((MEMBERS, 8, 128), 2)
    for h in range(2):
        some = given[:, :, h * 128 : (h + 1) * 128]
        first = jnp.where(sub3 // CAP == ray3 // WAVES, some, 0.0)
        second = jnp.where(sub3 // CAP + 2 == ray3 // WAVES, some, 0.0)
        encoder = jnp.concatenate([first, second], axis=1).reshape(MEMBERS * PART, 128)
        enc[h, 0], enc[h, 1] = split(encoder)
        enc_t[h, 0], enc_t[h, 1] = split(encoder.T)

    def rows_of(k):
        return pl.ds(ORDER.index(k % GROUPS) * WAVES, WAVES)

    def to_twin(k):
        return pltpu.make_async_remote_copy(
            src_ref=part.at[rows_of(k)],
            dst_ref=part_in.at[k - 1],
            send_sem=few_send.at[0, k - 1],
            recv_sem=few_recv.at[0, k - 1],
            device_id=(twin(k), slab),
            device_id_type=MESH,
        )

    def from_owner(k):
        return pltpu.make_async_remote_copy(
            src_ref=whole.at[rows_of(0)],
            dst_ref=whole.at[rows_of(GROUPS - k)],
            send_sem=few_send.at[1, k - 1],
            recv_sem=few_recv.at[1, k - 1],
            device_id=(twin(k), slab),
            device_id_type=MESH,
        )

    for h in range(2):
        all_of(lines_out.at[h], lines_in.at[h], 1 + h).wait_recv()
        high, low = split(lines_in[h].reshape(MEMBERS * PART, RADII))
        part[h * 128 : (h + 1) * 128] = dot(enc_t[h, 0], high) + (
            dot(enc_t[h, 0], low) + dot(enc_t[h, 1], high)
        )
        for k in HALVES[h]:
            if k > 0:
                to_twin(k).start()
                sent.append(lambda k=k: to_twin(k).wait_send())
    exchange(p0, 2, 2, 0, 4, start)
    sent.append(lambda: exchange(p0, 2, 2, 0, 4, leave))
    exchange(q0, 0, 5, 6, 1, start, 5)
    sent.append(lambda: exchange(q0, 0, 5, 6, 1, leave, 5))
    mine = part[rows_of(0), :]
    for k in ORDER[::-1][1:]:
        to_twin(k).wait_recv()
        mine = mine + part_in[k - 1]
    whole[rows_of(0), :] = mine
    for k in ORDER[:-1]:
        from_owner(k).start()
        sent.append(lambda k=k: from_owner(k).wait_send())
    harm[:, 0] = mine[:MODES]

    for h in (1, 0):
        for k in HALVES[h]:
            if k > 0:
                from_owner(GROUPS - k).wait_recv()
        high, low = split(whole[h * 128 : (h + 1) * 128])
        grad = dot(enc[h, 0], high) + (dot(enc[h, 0], low) + dot(enc[h, 1], high))
        grad_out[h] = grad.reshape(MEMBERS, PART, RADII)
        start_all(back_mate(grad_out.at[h], grad_in.at[h], 3 + h))
        sent.append(lambda h=h: all_of(grad_out.at[h], grad_in.at[h], 3 + h).wait_send())
        grad_in[h, 0] = grad_out[h, 0]
    exchange(p0, 2, 2, 0, 4, arrive)
    for h in (1, 0):
        all_of(grad_out.at[h], grad_in.at[h], 3 + h).wait_recv()
    high, low = split(grad_in[...].reshape(ROWS, RADII) * factor[...])
    impulse = dot(pick_t[...], high) + dot(pick_t[...], low)
    impulse = impulse.reshape(PLANES, COLS, RADII)
    p0[4, 1 : PLANES + 1] = p0[4, 1 : PLANES + 1] + impulse

    pressure = p0[4, 1 : PLANES + 1].reshape(PLANES * COLS, RADII)
    pressure = pressure.T
    start_rows = jnp.where(sub == 4, pressure[:1], forward_rows)
    start_next = jnp.where(sub == 4, pressure[1:2], forward_next)
    tile[1, :8] = start_rows
    tile[1, 8:] = start_next
    exchange_tiles(1, start)
    sent.append(lambda: exchange_tiles(1, leave))
    pack_columns(p0, 2, (4,))
    exchange(p0, 2, 3, 4, 1, start)
    sent.append(lambda: exchange(p0, 2, 3, 4, 1, leave))
    exchange(q0, 0, 5, 6, 1, arrive, 5)
    exchange(p0, 2, 3, 4, 1, arrive)

    def store_p1(f, i, value):
        p1[f, i + 1] = value

    def store_out(f, i, value):
        out[f, i] = value

    planes(functools.partial(adjoint_plane, p0, 2, store_p1))
    pack_columns(p1, 3, range(5))
    exchange(p1, 3, 4, 0, 5, start)
    sent.append(lambda: exchange(p1, 3, 4, 0, 5, leave))
    exchange(p1, 3, 4, 0, 5, arrive)
    planes(functools.partial(adjoint_plane, p1, 3, store_out))
    exchange_tiles(1, arrive)
    coefs = shifted(first_rows, by_us)
    added = [
        met(radial_back, values * parity, at) for values, at in zip(opposite_values(1), met_speeds)
    ]
    theirs, theirs_follow = far[1][:8], far[1][8:]
    theirs_after = adjoint_inner(
        theirs,
        theirs_follow,
        [far_near[1, k] for k in range(4)],
        shifted(far[0][:8], by_them),
        theirs_next[5:6],
    )
    there = across_axis(start_rows, cross_back) * parity
    theirs_after = theirs_after + met(radial_back, there, met_speed_there)
    mirrored = across_axis(theirs_after, cross) * parity
    inner = adjoint_inner(added[0], None, added[1:], coefs, None)
    inner = inner + met(radial_back, mirrored, met_speeds[0])
    following = met(radial_back, added[0], speed)
    patch(out, 0, inner, following, range(5))

    for wait in sent:
        wait()


def local(
    state,
    mean_velocity,
    sound_speed,
    flux_axial,
    flux_radial,
    flux_azimuthal,
    axis_pair,
    panel_weight,
    panel_cell,
    panel_owner,
    panel_count,
):
    outside = pl.BlockSpec(memory_space=pltpu.HBM)
    vector = pl.BlockSpec(memory_space=pltpu.VMEM)

    def grid_of(fields):
        return pltpu.VMEM((fields, PLANES + 2, COLS, RADII), F32)

    fields, rows = pl.pallas_call(
        kernel,
        out_shape=(
            jax.ShapeDtypeStruct((5, PLANES, COLS, RADII), F32),
            jax.ShapeDtypeStruct((MODES, 1, RADII), F32),
        ),
        in_specs=[outside] * 11,
        out_specs=(vector, vector),
        scratch_shapes=[
            grid_of(7),
            grid_of(5),
            grid_of(5),
            grid_of(5),
            pltpu.VMEM((1, PANELS), F32),
            pltpu.VMEM((1, PANELS), I32),
            pltpu.VMEM((1, PANELS), I32),
            pltpu.SMEM((5, 5), F32),
            pltpu.SMEM((5, 5), F32),
            pltpu.SMEM((5, 5), F32),
            pltpu.SMEM((1, COLS), I32),
            pltpu.SMEM((1, 1), I32),
            pltpu.VMEM((4, 2, 7 * PLANES, RADII), F32),
            pltpu.VMEM((4, 2, 7 * PLANES, RADII), F32),
            pltpu.VMEM((2, 16, 128), F32),
            pltpu.VMEM((2, 4, 8, 128), F32),
            pltpu.VMEM((2, 16, 128), F32),
            pltpu.VMEM((2, 4, 8, 128), F32),
            pltpu.VMEM((PLANES, COLS, 128), F32),
            pltpu.VMEM((PLANES, COLS, 128), F32),
            pltpu.VMEM((ROWS, 128), BF16),
            pltpu.VMEM((128, ROWS), BF16),
            pltpu.VMEM((ROWS, 128), F32),
            pltpu.VMEM((MEMBERS, 8, LANES), F32),
            pltpu.VMEM((MEMBERS, 8, LANES), F32),
            pltpu.VMEM((2, 2, MEMBERS * PART, 128), BF16),
            pltpu.VMEM((2, 2, 128, MEMBERS * PART), BF16),
            pltpu.VMEM((2, MEMBERS, PART, RADII), F32),
            pltpu.VMEM((2, MEMBERS, PART, RADII), F32),
            pltpu.VMEM((GROUPS * WAVES, RADII), F32),
            pltpu.VMEM((GROUPS - 1, WAVES, RADII), F32),
            pltpu.VMEM((GROUPS * WAVES, RADII), F32),
            pltpu.VMEM((2, MEMBERS, PART, RADII), F32),
            pltpu.VMEM((2, MEMBERS, PART, RADII), F32),
            pltpu.SemaphoreType.DMA((11,)),
            pltpu.SemaphoreType.DMA((6, 4)),
            pltpu.SemaphoreType.DMA((6, 4)),
            pltpu.SemaphoreType.DMA((2, 9)),
            pltpu.SemaphoreType.DMA((2, 9)),
            pltpu.SemaphoreType.DMA((5,)),
            pltpu.SemaphoreType.DMA((5,)),
            pltpu.SemaphoreType.DMA((2, GROUPS - 1)),
            pltpu.SemaphoreType.DMA((2, GROUPS - 1)),
        ],
        compiler_params=pltpu.CompilerParams(
            collective_id=0, has_side_effects=True, vmem_limit_bytes=VMEM_GRANT
        ),
    )(
        *(
            pltpu.with_memory_space_constraint(argument, pltpu.HBM)
            for argument in (
                state,
                mean_velocity,
                sound_speed,
                flux_axial,
                flux_radial,
                flux_azimuthal,
                axis_pair,
                panel_weight,
                panel_cell,
                panel_owner.reshape(1, PANELS),
            )
        ),
        panel_count,
    )
    return fields, rows.reshape(1, 1, MODES, RADII)


def solution(mesh):
    return jax.shard_map(
        local,
        mesh=mesh,
        in_specs=(
            P(None, "slab", "sector", None),
            P("slab", "sector", None),
            P("slab", "sector", None),
            P(),
            P(),
            P(),
            P("sector", None),
            P("slab", "sector"),
            P("slab", "sector"),
            P("slab", "sector", None),
            P("slab", "sector"),
        ),
        out_specs=(P(None, "slab", "sector", None), P("slab", "sector", None, None)),
        check_vma=False,
    )
```
